256 devices in a mesh: section: 32 (over x_hi, z, core), tensor: 2 (over x_lo), dp: 4 (over y).
Axes of the slice: x: 4 (x_hi: 2, x_lo: 2; x = x_hi * 2 + x_lo), y: 4, z: 8, core: 2. Of those that a mesh axis runs over, the one named last changes fastest.
Arguments:
- queries: bfloat16 [32, 12, 128, 4096], P('section', 'dp', None, 'tensor'), may hold values from -6 to 6
- context_gradient: bfloat16 [32, 12, 128, 4096], P('section', 'dp', None, 'tensor'), may hold values from -0.59765625 to 0.59765625
- vision_feature_states: bfloat16 [12, 64, 8192], P('dp', 'section', 'tensor'), may hold values from -6 to 6
- key_value_weight: bfloat16 [32, 2, 8192, 512], P('section', None, None, 'tensor'), may hold values from -0.0625 to 0.0625
- adapter_down_maps: bfloat16 [32, 2, 16, 8192], P('section'), may hold values from -0.0625 to 0.0625
- adapter_up_maps: bfloat16 [32, 2, 16, 512], P('section'), may hold values from -0.375 to 0.375
- norm_gain_pair: bfloat16 [32, 2, 128], P('section'), may hold values from 0.5 to 1.5
- image_tile_count: int32 [12], P('dp'), may hold values from 1 to 4
- text_start_position: int32 [12], P('dp'), may hold values from 0 to 63
Outputs:
- vision_grad: float32 [12, 64, 8192], P('dp', 'section', 'tensor')
- down_grad: float32 [32, 2, 16, 8192], P('section')
- up_grad: float32 [32, 2, 16, 512], P('section')
The draws below stay inside these ranges and needn't reach their ends.
All inputs are finite; a program needn't handle non-finite values.
Results may differ from the reference program's by a relative error of at most 0.03.
Values may be sent and summed in bfloat16 or wider, within the bound.
No kernel may reach another device: no remote copies, remote signals or barrier semaphores. Data moves between devices by JAX's collectives and lax.ppermute only.
A program may use at most 128 MiB of HBM per device.

```python
import jax
import jax.numpy as jnp
from jax import lax

MODEL_WIDTH = 8192
KEY_VALUE_HEADS = 4
QH = 32
HEAD_SIZE = 128
ADAPTER_RANK = 16
TILES = 4
TQ = 128
VT = 64
BATCHES = 12
N_SECTION = 32


def with_ends(array, rng, low, high):
    extent = array.shape
    spot = [jax.random.randint(jax.random.fold_in(rng, axis), (), 0, extent[axis]) for axis in range(len(extent))]
    array = array.at[tuple(spot)].set(low)
    longest = extent.index(max(extent))
    spot[longest] = (spot[longest] + 1) % extent[longest]
    return array.at[tuple(spot)].set(high)


def level_of(key, extent, pieces, least, top_value):
    def one(position, blocks):
        heights = jax.random.uniform(jax.random.fold_in(jax.random.fold_in(key, 6), position), (blocks,), jnp.float32, least / len(pieces), top_value / len(pieces))
        return jnp.repeat(jnp.exp(heights), extent[position] // blocks).reshape((-1,) + (1,) * (len(extent) - position - 1))

    factor_of = one(*pieces[0])
    for cut in pieces[1:]:
        factor_of = factor_of * one(*cut)
    return factor_of


def centred(rng, dims, deviation, reach, split=(), dtype=jnp.bfloat16):
    drawn = jax.random.normal(rng, dims, jnp.float32) * deviation
    if len(split) > 0:
        drawn = level_of(rng, dims, split, -0.22, 0.18) * drawn
    return jnp.clip(drawn, min=-reach, max=reach).astype(dtype)


def setup_inputs(seed: int = 0) -> dict:
    splits = jax.random.split(jax.random.key(seed), 10)
    queries = centred(splits[0], (N_SECTION, BATCHES, TQ, QH * HEAD_SIZE), 1.0, 6.0, ((0, 32), (1, 4), (3, 2)))
    context_gradient = centred(splits[1], (N_SECTION, BATCHES, TQ, QH * HEAD_SIZE), 0.1, 0.59765625, ((0, 32), (1, 4), (3, 2)))
    vision_feature_states = centred(splits[2], (BATCHES, VT, MODEL_WIDTH), 1.0, 6.0, ((0, 4), (1, 32), (2, 2)))
    key_value_weight = centred(splits[3], (N_SECTION, 2, MODEL_WIDTH, KEY_VALUE_HEADS * HEAD_SIZE), MODEL_WIDTH ** -0.5, 0.0625, ((0, 32), (3, 2)))
    adapter_down_maps = centred(splits[4], (N_SECTION, 2, ADAPTER_RANK, MODEL_WIDTH), MODEL_WIDTH ** -0.5, 0.0625, ((0, 32),))
    adapter_up_maps = centred(splits[5], (N_SECTION, 2, ADAPTER_RANK, KEY_VALUE_HEADS * HEAD_SIZE), (16 * ADAPTER_RANK) ** -0.5, 0.375, ((0, 32),))
    norm_gain_pair = jnp.clip(1.0 + 0.1 * jax.random.normal(splits[6], (N_SECTION, 2, HEAD_SIZE), jnp.float32), 0.5, 1.5).astype(jnp.bfloat16)
    image_tile_count = with_ends(jax.random.randint(splits[7], (BATCHES,), 1, TILES + 1), jax.random.fold_in(splits[7], 1), 1, TILES).astype(jnp.int32)
    text_start_position = with_ends(jax.random.randint(splits[8], (BATCHES,), 0, TQ // 2), jax.random.fold_in(splits[8], 1), 0, (TQ // 2) - 1).astype(jnp.int32)
    return dict(queries=queries, context_gradient=context_gradient, vision_feature_states=vision_feature_states, key_value_weight=key_value_weight, adapter_down_maps=adapter_down_maps, adapter_up_maps=adapter_up_maps, norm_gain_pair=norm_gain_pair, image_tile_count=image_tile_count, text_start_position=text_start_position)


ADAPTER_SCALE = 2.0
EPS = 1e-05

def mult_wide(pattern, first_op, second_op):
    return jnp.einsum(pattern, first_op.astype(jnp.float32), second_op.astype(jnp.float32))

def section_terms(vision_rows, layer_weights, down_projection, up_map_shard, norm_gains, queries, context_gradient, count, start, matrix_product):
    head_dim = norm_gains.shape[1]
    kv_width = layer_weights.shape[2]
    kv_heads = kv_width // head_dim
    q_heads = queries.shape[1] // head_dim
    group_size = q_heads // kv_heads
    text_len = queries.shape[0]
    vision_len = vision_rows.shape[0]
    tile_len = vision_len // TILES
    reduced_gradient = matrix_product('vd,crd->cvr', vision_rows, down_projection).astype(jnp.bfloat16)
    projected_states = matrix_product('xo,noj->nxj', vision_rows, layer_weights) + ADAPTER_SCALE * matrix_product('uqy,uyi->uqi', reduced_gradient, up_map_shard)
    key_raw = projected_states[0].reshape(vision_len, kv_heads, head_dim)
    key_scale = lax.rsqrt(lax.optimization_barrier(jnp.mean(key_raw * key_raw, axis=-1, keepdims=True)) + EPS)
    key_gain = norm_gains[1].astype(jnp.float32)
    unit_keys = key_raw * key_scale
    key_heads = (unit_keys * key_gain).astype(jnp.bfloat16)
    value_heads = projected_states[1].astype(jnp.bfloat16).reshape(vision_len, kv_heads, head_dim)
    query_raw = queries.astype(jnp.float32).reshape(text_len, kv_heads, group_size, head_dim)
    query_scale = lax.rsqrt(lax.optimization_barrier(jnp.mean(query_raw * query_raw, axis=-1, keepdims=True)) + EPS)
    normed = (query_raw * query_scale * norm_gains[0].astype(jnp.float32)).astype(jnp.bfloat16)
    scores = matrix_product('tkgh,vkh->kgtv', normed, key_heads) * head_dim ** (-0.5)
    key_allowed = jnp.arange(vision_len) < count * tile_len
    row_allowed = (jnp.arange(text_len) >= start).astype(jnp.float32)
    weighted = jnp.where(key_allowed, jnp.exp(scores), 0.0)
    denominator = lax.optimization_barrier(jnp.sum(weighted, axis=-1, keepdims=True))
    attention = weighted / denominator * row_allowed[:, None]
    attention_low = attention.astype(jnp.bfloat16)
    grad_context = context_gradient.reshape(text_len, kv_heads, group_size, head_dim)
    grad_probs = matrix_product('tkgh,vkh->kgtv', grad_context, value_heads)
    grad_scores = attention * (grad_probs - lax.optimization_barrier(jnp.sum(attention * grad_probs, axis=-1, keepdims=True))) * head_dim ** (-0.5)
    grad_scores_low = grad_scores.astype(jnp.bfloat16)
    grad_keys = matrix_product('kgtv,tkgh->vkh', grad_scores_low, normed)
    grad_values = matrix_product('kgtv,tkgh->vkh', attention_low, grad_context)
    gain_grad = grad_keys * key_gain
    grad_key_raw = key_scale * (gain_grad - unit_keys * lax.optimization_barrier(jnp.mean(gain_grad * unit_keys, axis=-1, keepdims=True)))
    unnormed_gradient = jnp.stack([grad_key_raw.reshape(vision_len, kv_width), grad_values.reshape(vision_len, kv_width)]).astype(jnp.bfloat16)
    up_map_gradient = ADAPTER_SCALE * matrix_product('lha,lhq->laq', reduced_gradient, unnormed_gradient)
    middle_product = matrix_product('cvw,crw->cvr', unnormed_gradient, up_map_shard).astype(jnp.bfloat16)
    down_map_gradient = ADAPTER_SCALE * matrix_product('npz,py->nzy', middle_product, vision_rows)
    vision_gradient = matrix_product('osx,okx->sk', unnormed_gradient, layer_weights) + ADAPTER_SCALE * matrix_product('ugq,uqe->ge', middle_product, down_projection)
    return (vision_gradient, down_map_gradient, up_map_gradient)

def reference(queries, context_gradient, vision_feature_states, key_value_weight, adapter_down_maps, adapter_up_maps, norm_gain_pair, image_tile_count, text_start_position):

    def per_section(running, current_layer_index):
        layer_weights = key_value_weight[current_layer_index]
        down_projection = adapter_down_maps[current_layer_index]
        up_map_shard = adapter_up_maps[current_layer_index]
        norm_gains = norm_gain_pair[current_layer_index]

        def per_batch(partial_sums, micro_index):
            vision_gradient, down_map_gradient, up_map_gradient = section_terms(vision_feature_states[micro_index], layer_weights, down_projection, up_map_shard, norm_gains, queries[current_layer_index, micro_index], context_gradient[current_layer_index, micro_index], image_tile_count[micro_index], text_start_position[micro_index], mult_wide)
            return ((partial_sums[0] + down_map_gradient, partial_sums[1] + up_map_gradient), vision_gradient)
        start_sums = (jnp.zeros(down_projection.shape, jnp.float32), jnp.zeros(up_map_shard.shape, jnp.float32))
        (down_sum, up_sum), grads = lax.scan(per_batch, start_sums, jnp.arange(BATCHES))
        return (running + grads, (down_sum, up_sum))
    start_total = jnp.zeros((BATCHES, VT, MODEL_WIDTH), jnp.float32)
    total, (down_grad, up_grad) = lax.scan(per_section, start_total, jnp.arange(N_SECTION))
    return (total, down_grad, up_grad)
```

```python
import jax
import jax.numpy as jnp
from jax import lax
from jax.sharding import PartitionSpec as P

TILES = 4
ADAPTER_SCALE = 2.0
EPS = 1e-05
PLANE = ("section", "tensor")
NZ = 8


def plane_pairs(route):
    def index(x, z, core):
        return (((x // 2) * NZ + z) * 2 + core) * 2 + x % 2

    return [
        (index(x, z, core), index(*route(x, z, core)))
        for x in range(4)
        for z in range(NZ)
        for core in range(2)
    ]


SIBLING = plane_pairs(lambda x, z, core: (x, z, 1 - core))
RISE = {
    k: plane_pairs(lambda x, z, core, k=k: (x, (z + (k if core == 0 else -k)) % NZ, core))
    for k in (1, 2, 3, 4)
}
FALL = {
    k: plane_pairs(lambda x, z, core, k=k: (x, (z - (k if core == 0 else -k)) % NZ, core))
    for k in (1, 2, 3, 4)
}
NEAR = plane_pairs(lambda x, z, core: (x ^ 1 if core == 0 else 3 - x, z, core))
FAR = plane_pairs(lambda x, z, core: (3 - x if core == 0 else x ^ 1, z, core))
TENSOR_SWAP = [(0, 1), (1, 0)]
DP_NEAR = [(i, i ^ 1) for i in range(4)]
DP_FAR = [(i, 3 - i) for i in range(4)]


def move(block, pairs):
    return lax.ppermute(block, PLANE, pairs)


def mm(pattern, first, second, precision=None):
    return jnp.einsum(
        pattern, first, second, preferred_element_type=jnp.float32, precision=precision
    )


def gather_rows(own):
    chip = jnp.concatenate([own, move(own, SIBLING)])
    parts = [move(chip, RISE[k]) for k in (1, 2, 3)] + [move(own, RISE[4]), own]
    base = jnp.concatenate(parts)
    first = move(base, NEAR)
    second = move(base, FAR)
    third = move(first, FAR)
    here = [base, third, first, second]
    there = [move(block, SIBLING) for block in here]
    return here, there


def row_tokens(x_hi, z, core, x_lo):
    def base_rows(chain, x_high):
        step = jnp.where(chain == 0, 1, -1)
        places = []
        for k in (1, 2, 3):
            for other in (0, 1):
                places.append(((z - step * k) % NZ, jnp.where(other == 0, chain, 1 - chain)))
        places += [((z - step * 4) % NZ, chain), (z, chain)]
        rows = []
        for level, which in places:
            token = ((x_high * NZ + level) * 2 + which) * 2
            for batch in range(3):
                rows += [batch * 64 + token, batch * 64 + token + 1]
        return jnp.stack(rows)

    own_half, other_half = [], []
    for chain in (core, 1 - core):
        own_half += [base_rows(chain, x_hi), base_rows(chain, 1 - x_hi)]
        near = jnp.where(chain == 0, x_hi, 1 - x_hi)
        other_half += [base_rows(chain, near), base_rows(chain, 1 - near)]
    return jnp.concatenate(own_half), jnp.concatenate(other_half)


def scatter_rows(here, there):
    f32, low = jnp.float32, jnp.bfloat16
    base, third, first, second = (
        mine.astype(f32) + move(theirs, SIBLING).astype(f32) for mine, theirs in zip(here, there)
    )
    first = first + move(third.astype(low), FAR).astype(f32)
    base = base + move(second.astype(low), FAR).astype(f32)
    base = base + move(first.astype(low), NEAR).astype(f32)
    sent = base[:42].astype(low)
    own = base[42:] + move(sent[36:42], FALL[4]).astype(f32)
    chip = sum(
        move(sent[12 * i : 12 * i + 12], FALL[k]).astype(f32) for i, k in enumerate((1, 2, 3))
    )
    return own + chip[:6] + move(chip[6:].astype(low), SIBLING).astype(f32)


def per_device(
    queries,
    context_gradient,
    vision_feature_states,
    key_value_weight,
    adapter_down_maps,
    adapter_up_maps,
    norm_gain_pair,
    image_tile_count,
    text_start_position,
):
    low, f32 = jnp.bfloat16, jnp.float32
    weights = key_value_weight[0]
    down_maps = adapter_down_maps[0]
    gains = norm_gain_pair[0].astype(f32)
    section, side = lax.axis_index("section"), lax.axis_index("tensor")
    width = weights.shape[2]
    up_maps = lax.dynamic_slice_in_dim(adapter_up_maps[0], side * width, width, 2)
    batches, _, half = vision_feature_states.shape
    head = gains.shape[1]
    kv_heads = width // head
    text = queries.shape[2]
    group = queries.shape[3] // width
    tokens = 64

    here, there = gather_rows(vision_feature_states.reshape(-1, half))
    own_rows = jnp.concatenate(here[:2] + there[:2])
    other_rows = jnp.concatenate(here[2:] + there[2:])
    own_token, other_token = row_tokens(section // 16, (section // 2) % NZ, section % 2, side)
    line = jnp.arange(batches * tokens)[:, None]
    own_map = (line == own_token[None]).astype(low)
    other_map = (line == other_token[None]).astype(low)

    own_w = lax.dynamic_slice_in_dim(weights, side * half, half, 1)
    other_w = lax.dynamic_slice_in_dim(weights, (1 - side) * half, half, 1)
    own_a = lax.dynamic_slice_in_dim(down_maps, side * half, half, 2)
    other_a = lax.dynamic_slice_in_dim(down_maps, (1 - side) * half, half, 2)

    def ordered(own, other):
        own = mm("vr,cro->cvo", own_map.astype(f32), own, lax.Precision.HIGHEST)
        return own + mm("vr,cro->cvo", other_map.astype(f32), other, lax.Precision.HIGHEST)

    reduced = ordered(
        mm("rf,caf->cra", own_rows, own_a), mm("rf,caf->cra", other_rows, other_a)
    ).astype(low)
    projected = ordered(
        mm("rf,cfo->cro", own_rows, own_w), mm("rf,cfo->cro", other_rows, other_w)
    ) + ADAPTER_SCALE * mm("cva,cao->cvo", reduced, up_maps)

    key_raw = projected[0].reshape(batches, tokens, kv_heads, head)
    key_scale = lax.rsqrt(jnp.mean(key_raw * key_raw, axis=-1, keepdims=True) + EPS)
    unit = key_raw * key_scale
    keys = (unit * gains[1]).astype(low)
    values = projected[1].astype(low).reshape(batches, tokens, kv_heads, head)
    query_raw = queries[0].astype(f32).reshape(batches, text, kv_heads, group, head)
    query_scale = lax.rsqrt(jnp.mean(query_raw * query_raw, axis=-1, keepdims=True) + EPS)
    normed = (query_raw * query_scale * gains[0]).astype(low)
    context = context_gradient[0].reshape(batches, text, kv_heads, group, head)
    scores = mm("bvkh,btkgh->bkvgt", keys, normed) * head ** (-0.5)
    allowed = jnp.arange(tokens)[None] < image_tile_count[:, None] * (tokens // TILES)
    live = (jnp.arange(text)[None] >= text_start_position[:, None]).astype(f32)
    weighted = jnp.where(allowed[:, None, :, None, None], jnp.exp(scores), 0.0)
    attention = weighted / jnp.sum(weighted, axis=2, keepdims=True) * live[:, None, None, None]
    grad_probs = mm("bvkh,btkgh->bkvgt", values, context)
    grad_scores = (
        attention
        * (grad_probs - jnp.sum(attention * grad_probs, axis=2, keepdims=True))
        * head ** (-0.5)
    ).astype(low)
    grad_keys = mm("bkvgt,btkgh->bvkh", grad_scores, normed)
    grad_values = mm("bkvgt,btkgh->bvkh", attention.astype(low), context)
    gain_grad = grad_keys * gains[1]
    grad_key_raw = key_scale * (
        gain_grad - unit * jnp.mean(gain_grad * unit, axis=-1, keepdims=True)
    )
    rows = batches * tokens
    grad_raw = jnp.stack(
        [grad_key_raw.reshape(rows, width), grad_values.reshape(rows, width)]
    ).astype(low)

    up_part = ADAPTER_SCALE * mm("cva,cvo->cao", reduced, grad_raw)
    middle = mm("cvo,cao->cva", grad_raw, up_maps).astype(low)

    def arrival(mapping, values):
        return mm("vr,cvo->cro", mapping, values).astype(low)

    pieces = []
    downs = []
    for mapping, w, a, x in (
        (own_map, own_w, own_a, own_rows),
        (other_map, other_w, other_a, other_rows),
    ):
        part, mid = arrival(mapping, grad_raw), arrival(mapping, middle)
        pieces.append(
            (
                mm("cro,cfo->rf", part, w) + ADAPTER_SCALE * mm("cra,caf->rf", mid, a)
            ).astype(low)
        )
        downs.append(ADAPTER_SCALE * mm("cra,rf->caf", mid, x))
    v_own, v_other = pieces
    cut = v_own.shape[0] // 4
    own_grad = scatter_rows(
        [v_own[:cut], v_own[cut : 2 * cut], v_other[:cut], v_other[cut : 2 * cut]],
        [v_own[2 * cut : 3 * cut], v_own[3 * cut :], v_other[2 * cut : 3 * cut], v_other[3 * cut :]],
    )

    ranks = 2 * down_maps.shape[1]
    down = downs[0] + lax.ppermute(downs[1].astype(low), "tensor", TENSOR_SWAP).astype(f32)
    sums = jnp.concatenate([down.reshape(ranks, half), up_part.reshape(ranks, width)], 1)
    for pairs in (DP_NEAR, DP_FAR):
        sums = sums.astype(low)
        sums = sums.astype(f32) + lax.ppermute(sums, "dp", pairs).astype(f32)
    sums = sums.astype(low)
    facing = lax.ppermute(sums, "tensor", TENSOR_SWAP)
    left = jnp.where(side == 0, sums, facing).astype(f32)
    right = jnp.where(side == 0, facing, sums).astype(f32)
    down_total = jnp.concatenate([left[:, :half], right[:, :half]], 1)
    up_total = jnp.concatenate([left[:, half:], right[:, half:]], 1)
    return (
        own_grad.reshape(vision_feature_states.shape),
        down_total.reshape(1, 2, ranks // 2, 2 * half),
        up_total.reshape(1, 2, ranks // 2, 2 * width),
    )


def solution(mesh):
    in_specs = (
        P("section", "dp", None, "tensor"),
        P("section", "dp", None, "tensor"),
        P("dp", "section", "tensor"),
        P("section", None, None, "tensor"),
        P("section", None, None, None),
        P("section", None, None, None),
        P("section", None, None),
        P("dp"),
        P("dp"),
    )
    out_specs = (
        P("dp", "section", "tensor"),
        P("section", None, None, None),
        P("section", None, None, None),
    )
    return jax.shard_map(
        per_device, mesh=mesh, in_specs=in_specs, out_specs=out_specs, check_vma=False
    )
```

```python
import jax
import jax.numpy as jnp
from jax import lax
from jax.experimental import pallas as pl
from jax.experimental.pallas import tpu as pltpu
from jax.sharding import PartitionSpec as P

TILES = 4
ADAPTER_SCALE = 2.0
EPS = 1e-05
PLANE = ("section", "tensor")
NZ = 8


def plane_pairs(route):
    def index(x, z, core):
        return (((x // 2) * NZ + z) * 2 + core) * 2 + x % 2

    return [
        (index(x, z, core), index(*route(x, z, core)))
        for x in range(4)
        for z in range(NZ)
        for core in range(2)
    ]


SIBLING = plane_pairs(lambda x, z, core: (x, z, 1 - core))
RISE = {
    k: plane_pairs(lambda x, z, core, k=k: (x, (z + (k if core == 0 else -k)) % NZ, core))
    for k in (1, 2, 3, 4)
}
FALL = {
    k: plane_pairs(lambda x, z, core, k=k: (x, (z - (k if core == 0 else -k)) % NZ, core))
    for k in (1, 2, 3, 4)
}
NEAR = plane_pairs(lambda x, z, core: (x ^ 1 if core == 0 else 3 - x, z, core))
FAR = plane_pairs(lambda x, z, core: (3 - x if core == 0 else x ^ 1, z, core))
TENSOR_SWAP = [(0, 1), (1, 0)]
DP_NEAR = [(i, i ^ 1) for i in range(4)]
DP_FAR = [(i, 3 - i) for i in range(4)]


def move(block, pairs):
    return lax.ppermute(block, PLANE, pairs)


def after(value, *others):
    return lax.optimization_barrier((value, *others))[0]


NT = (((1,), (1,)), ((), ()))
TN = (((0,), (0,)), ((), ()))
F32, LOW = jnp.float32, jnp.bfloat16
ROOM = pltpu.CompilerParams(vmem_limit_bytes=48 * 1024 * 1024)


def dot(first, second, dims=(((1,), (0,)), ((), ()))):
    return lax.dot_general(first, second, dims, preferred_element_type=F32)


def cost(flops, moved):
    return pl.CostEstimate(flops=int(flops), bytes_accessed=int(moved), transcendentals=0)


def pair_kernel(gain_ref, query_ref, context_ref, pair_ref):
    gain = gain_ref[0:1, :].astype(F32)
    head = gain.shape[1]
    text = query_ref.shape[1]
    kv_heads = pair_ref.shape[0]
    group = query_ref.shape[2] // (head * kv_heads)
    for kv in range(kv_heads):
        for member in range(group):
            columns = slice((kv * group + member) * head, (kv * group + member + 1) * head)
            rows = slice(member * text, (member + 1) * text)
            query = query_ref[0, :, columns].astype(F32)
            scale = lax.rsqrt(jnp.mean(query * query, axis=-1, keepdims=True) + EPS)
            pair_ref[kv, rows, 0:head] = (query * scale * gain).astype(LOW)
            pair_ref[kv, rows, head : 2 * head] = context_ref[0, :, columns]


def pair_queries(queries, context, gains, kv_heads):
    batches, text, wide = queries.shape
    head = gains.shape[1]
    rows = wide // (kv_heads * head) * text
    block = pl.BlockSpec((1, text, wide), lambda b: (b, 0, 0))
    return pl.pallas_call(
        pair_kernel,
        out_shape=jax.ShapeDtypeStruct((batches * kv_heads, rows, 2 * head), LOW),
        grid=(batches,),
        in_specs=[pl.BlockSpec(gains.shape, lambda b: (0, 0)), block, block],
        out_specs=pl.BlockSpec((kv_heads, rows, 2 * head), lambda b: (b, 0, 0)),
        compiler_params=ROOM,
        cost_estimate=cost(2e8, 4 * queries.size * 2),
        name="pair_queries",
    )(gains, queries, context)


def project_kernel(which_ref, *refs):
    *row_refs, w_ref, a_ref, y_ref, r_ref = refs
    rows = jnp.concatenate([ref[...] for ref in row_refs])
    maps = a_ref[...].reshape(-1, a_ref.shape[2])

    @pl.when(pl.program_id(0) == 0)
    def _():
        y_ref[...] = jnp.zeros_like(y_ref)
        r_ref[...] = jnp.zeros_like(r_ref)

    for part in range(2):
        y_ref[part] += dot(rows, w_ref[part])
    r_ref[...] += dot(rows, maps, NT)


def project(blocks, weights, down_maps, which):
    count, half = len(blocks) * blocks[0].shape[0], blocks[0].shape[1]
    chunk = 1024
    steps = half // chunk
    width, ranks = weights.shape[2], 2 * down_maps.shape[1]
    grid_spec = pltpu.PrefetchScalarGridSpec(
        num_scalar_prefetch=1,
        grid=(steps,),
        in_specs=[pl.BlockSpec((block.shape[0], chunk), lambda i, s: (0, i)) for block in blocks]
        + [
            pl.BlockSpec((2, chunk, width), lambda i, s: (0, s[0] * steps + i, 0)),
            pl.BlockSpec((2, ranks // 2, chunk), lambda i, s: (0, 0, s[0] * steps + i)),
        ],
        out_specs=[
            pl.BlockSpec((2, count, width), lambda i, s: (0, 0, 0)),
            pl.BlockSpec((count, ranks), lambda i, s: (0, 0)),
        ],
    )
    return pl.pallas_call(
        project_kernel,
        out_shape=[
            jax.ShapeDtypeStruct((2, count, width), F32),
            jax.ShapeDtypeStruct((count, ranks), F32),
        ],
        grid_spec=grid_spec,
        compiler_params=ROOM,
        cost_estimate=cost(4 * 192 * half * width, 4 * half * width + 2 * count * half),
        name="project",
    )(which, *blocks, weights, down_maps)


def attention_kernel(
    count_ref, start_ref, y0, y1, y2, r0, r1, r2, own_map, other_map, own_back, other_back,
    up_diagonal, gains_ref, pair_ref, g_own, m_own, g_other, m_other, up_ref, grad_ref,
):
    width = y0.shape[2]
    head = gains_ref.shape[1]
    kv_heads = width // head
    batches = pair_ref.shape[0] // kv_heads
    tokens = own_map.shape[0] // batches
    ranks = r0.shape[1]
    text = 128
    scale = head ** (-0.5)

    def ordered(own, other):
        total = None
        for mapping, values in ((own_map, own), (other_map, other)):
            high = values.astype(LOW)
            rest = values - high.astype(F32)
            middle = rest.astype(LOW)
            lowest = (rest - middle.astype(F32)).astype(LOW)
            for term in (lowest, middle, high):
                moved = dot(mapping[...], term)
                total = moved if total is None else total + moved
        return total

    reduced = ordered(jnp.concatenate([r0[...], r1[...]]), r2[...]).astype(LOW)
    adapted = ADAPTER_SCALE * dot(reduced, up_diagonal[...])
    raw = [
        ordered(jnp.concatenate([y0[part], y1[part]]), y2[part])
        + adapted[:, part * width : (part + 1) * width]
        for part in range(2)
    ]
    gain = gains_ref[1:2, :].astype(F32)
    lane = lax.broadcasted_iota(jnp.int32, (1, pair_ref.shape[1]), 1) % text
    token = lax.broadcasted_iota(jnp.int32, (tokens, 1), 0)
    for kv in range(kv_heads):
        columns = slice(kv * head, (kv + 1) * head)
        key_raw = raw[0][:, columns]
        key_scale = lax.rsqrt(jnp.mean(key_raw * key_raw, axis=-1, keepdims=True) + EPS)
        unit = key_raw * key_scale
        keys = (unit * gain).astype(LOW)
        values = raw[1][:, columns].astype(LOW)
        for batch in range(batches):
            rows = slice(batch * tokens, (batch + 1) * tokens)
            none = jnp.zeros((tokens, head), LOW)
            both = jnp.concatenate(
                [
                    jnp.concatenate([keys[rows], none], 1),
                    jnp.concatenate([none, values[rows]], 1),
                ]
            )
            pair = pair_ref[batch * kv_heads + kv]
            scores = dot(both, pair, NT)
            allowed = token < count_ref[batch] * (tokens // TILES)
            live = (lane >= start_ref[batch]).astype(F32)
            weighted = jnp.where(allowed, jnp.exp(scores[:tokens] * scale), 0.0)
            attention = weighted * (live / jnp.sum(weighted, axis=0, keepdims=True))
            probs = scores[tokens:]
            mean = jnp.sum(attention * probs, axis=0, keepdims=True)
            grads = attention * (probs - mean) * scale
            out = dot(jnp.concatenate([grads.astype(LOW), attention.astype(LOW)]), pair)
            gained = out[:tokens, :head] * gain
            inner = jnp.mean(gained * unit[rows], axis=-1, keepdims=True)
            grad_ref[rows, columns] = (key_scale[rows] * (gained - unit[rows] * inner)).astype(LOW)
            grad_ref[rows, width + kv * head : width + (kv + 1) * head] = out[
                tokens:, head:
            ].astype(LOW)
    grad = grad_ref[...]
    middle = dot(grad, up_diagonal[...], NT).astype(LOW)
    up = ADAPTER_SCALE * dot(reduced, grad, TN)
    for part in range(2):
        half = slice(part * ranks // 2, (part + 1) * ranks // 2)
        up_ref[half, :] = up[half, part * width : (part + 1) * width]
    for back, g_ref, m_ref in ((own_back, g_own, m_own), (other_back, g_other, m_other)):
        g_ref[...] = dot(back[...], grad).astype(LOW)
        m_ref[...] = (ADAPTER_SCALE * dot(back[...], middle)).astype(LOW)


def attend(counts, starts, projected, maps, up_diagonal, gains, pair):
    (y0, r0), (y1, r1), (y2, r2) = projected
    rows, ranks, width = y2.shape[1], r0.shape[1], y0.shape[2]
    scalar = pl.BlockSpec(memory_space=pltpu.SMEM)
    vector = pl.BlockSpec(memory_space=pltpu.VMEM)
    return pl.pallas_call(
        attention_kernel,
        out_shape=[
            jax.ShapeDtypeStruct((rows, 2 * width), LOW),
            jax.ShapeDtypeStruct((rows, ranks), LOW),
            jax.ShapeDtypeStruct((rows, 2 * width), LOW),
            jax.ShapeDtypeStruct((rows, ranks), LOW),
            jax.ShapeDtypeStruct((ranks, width), F32),
        ],
        in_specs=[scalar, scalar] + [vector] * 13,
        out_specs=[vector] * 5,
        scratch_shapes=[pltpu.VMEM((rows, 2 * width), LOW)],
        compiler_params=ROOM,
        cost_estimate=cost(1e9, 2 * pair.size),
        name="attend",
    )(counts, starts, y0, y1, y2, r0, r1, r2, *maps, up_diagonal, gains, pair)


def feature_kernel(which_ref, g_ref, m_ref, w_ref, a_ref, *out_refs):
    width = w_ref.shape[2]
    total = dot(m_ref[...], a_ref[...].reshape(-1, a_ref.shape[2]))
    for part in range(2):
        total += dot(g_ref[:, part * width : (part + 1) * width], w_ref[part], NT)
    cut = out_refs[0].shape[0]
    for i, ref in enumerate(out_refs):
        ref[...] = total[i * cut : (i + 1) * cut].astype(LOW)


def feature_grad(grad, middle, weights, down_maps, which):
    rows, wide = grad.shape
    ranks = middle.shape[1]
    half = weights.shape[1] // 2
    chunk = 1024
    steps = half // chunk
    cut = rows // 4
    grid_spec = pltpu.PrefetchScalarGridSpec(
        num_scalar_prefetch=1,
        grid=(steps,),
        in_specs=[
            pl.BlockSpec((rows, wide), lambda i, s: (0, 0)),
            pl.BlockSpec((rows, ranks), lambda i, s: (0, 0)),
            pl.BlockSpec((2, chunk, wide // 2), lambda i, s: (0, s[0] * steps + i, 0)),
            pl.BlockSpec((2, ranks // 2, chunk), lambda i, s: (0, 0, s[0] * steps + i)),
        ],
        out_specs=[pl.BlockSpec((cut, chunk), lambda i, s: (0, i))] * 4,
    )
    return pl.pallas_call(
        feature_kernel,
        out_shape=[jax.ShapeDtypeStruct((cut, half), LOW)] * 4,
        grid_spec=grid_spec,
        compiler_params=ROOM,
        cost_estimate=cost(2 * rows * half * wide, 2 * half * (wide + rows)),
        name="feature_grad",
    )(which, grad, middle, weights, down_maps)


def down_kernel(m_ref, *refs):
    *row_refs, out_ref = refs
    rows = jnp.concatenate([ref[...] for ref in row_refs])
    out_ref[...] = dot(m_ref[...], rows, TN).astype(out_ref.dtype)


def down_grad(middle, blocks, dtype):
    half = blocks[0].shape[1]
    chunk = 1024
    return pl.pallas_call(
        down_kernel,
        out_shape=jax.ShapeDtypeStruct((middle.shape[1], half), dtype),
        grid=(half // chunk,),
        in_specs=[pl.BlockSpec(middle.shape, lambda i: (0, 0))]
        + [pl.BlockSpec((block.shape[0], chunk), lambda i: (0, i)) for block in blocks],
        out_specs=pl.BlockSpec((middle.shape[1], chunk), lambda i: (0, i)),
        compiler_params=ROOM,
        cost_estimate=cost(5e8, 2 * 200 * half),
        name="down_grad",
    )(middle, *blocks)


def row_tokens(x_hi, z, core, x_lo):
    def base_rows(chain, x_high):
        step = jnp.where(chain == 0, 1, -1)
        places = []
        for k in (1, 2, 3):
            for other in (0, 1):
                places.append(((z - step * k) % NZ, jnp.where(other == 0, chain, 1 - chain)))
        places += [((z - step * 4) % NZ, chain), (z, chain)]
        rows = []
        for level, which in places:
            token = ((x_high * NZ + level) * 2 + which) * 2
            for batch in range(3):
                rows += [batch * 64 + token, batch * 64 + token + 1]
        return jnp.stack(rows)

    own_half, other_half = [], []
    for chain in (core, 1 - core):
        own_half += [base_rows(chain, x_hi)]
        near = jnp.where(chain == 0, x_hi, 1 - x_hi)
        other_half += [base_rows(chain, near), base_rows(chain, 1 - near)]
    for chain in (core, 1 - core):
        own_half += [base_rows(chain, 1 - x_hi)]
    return jnp.concatenate(own_half), jnp.concatenate(other_half)


def per_device(
    queries,
    context_gradient,
    vision_feature_states,
    key_value_weight,
    adapter_down_maps,
    adapter_up_maps,
    norm_gain_pair,
    image_tile_count,
    text_start_position,
):
    weights, down_maps, gains = key_value_weight[0], adapter_down_maps[0], norm_gain_pair[0]
    section, side = lax.axis_index("section"), lax.axis_index("tensor")
    width, half = weights.shape[2], vision_feature_states.shape[2]
    ranks = 2 * down_maps.shape[1]
    here = side.reshape(1).astype(jnp.int32)
    opposite = 1 - here
    up_maps = lax.dynamic_slice_in_dim(adapter_up_maps[0], side * width, width, 2)
    up_diagonal = jnp.concatenate(
        [jnp.pad(up_maps[0], ((0, 0), (0, width))), jnp.pad(up_maps[1], ((0, 0), (width, 0)))]
    )

    own = vision_feature_states.reshape(-1, half)
    chip = jnp.concatenate([own, move(own, SIBLING)])
    parts = [move(chip, RISE[k]) for k in (1, 2, 3)] + [move(own, RISE[4]), own]
    pair = pair_queries(
        after(queries[0], chip), context_gradient[0], gains, width // gains.shape[1]
    )
    base = jnp.concatenate(parts)
    first = move(base, NEAR)
    second = move(base, FAR)
    base_there = move(base, SIBLING)
    step_a = project([base, base_there], weights, down_maps, here)
    third = move(first, FAR)
    first_there = move(first, SIBLING)
    second_there = move(second, SIBLING)
    others = [first, second, first_there, second_there]
    step_b = project(others, weights, down_maps, opposite)
    third_there = move(third, SIBLING)
    step_c = project([third, third_there], weights, down_maps, here)
    owns = [base, base_there, third, third_there]

    own_token, other_token = row_tokens(section // 16, (section // 2) % NZ, section % 2, side)
    line = jnp.arange(own_token.shape[0])
    maps = [
        (line[:, None] == own_token[None]).astype(LOW),
        (line[:, None] == other_token[None]).astype(LOW),
        (own_token[:, None] == line[None]).astype(LOW),
        (other_token[:, None] == line[None]).astype(LOW),
    ]
    g_own, m_own, g_other, m_other, up_part = attend(
        image_tile_count,
        text_start_position,
        (step_a, step_c, step_b),
        maps,
        up_diagonal,
        gains,
        pair,
    )

    down_other = down_grad(m_other, others, LOW)
    down_facing = lax.ppermute(down_other, "tensor", TENSOR_SWAP)
    base, base_out, third, third_out = feature_grad(
        after(g_own, down_other), m_own, weights, down_maps, here
    )
    down_own = down_grad(m_own, owns, F32)
    first, second, first_out, second_out = feature_grad(
        after(g_other, base), m_other, weights, down_maps, opposite
    )

    def add(mine, theirs):
        return mine.astype(F32) + theirs.astype(F32)

    third = add(third, move(third_out, SIBLING)).astype(LOW)
    second = add(second, move(second_out, SIBLING)).astype(LOW)
    first = add(first, move(first_out, SIBLING))
    base = add(base, move(base_out, SIBLING))

    sums = jnp.concatenate(
        [down_own + after(down_facing, first_out).astype(F32), up_part], 1
    ).astype(LOW)
    near_sums = lax.ppermute(sums, "dp", DP_NEAR)
    third_in = move(third, FAR)
    second_in = move(second, FAR)
    first = (first + third_in.astype(F32)).astype(LOW)
    first_in = move(first, NEAR)
    sums = add(sums, after(near_sums, first)).astype(LOW)
    far_sums = lax.ppermute(sums, "dp", DP_FAR)
    base = base + second_in.astype(F32) + first_in.astype(F32)
    sent = base[:42].astype(LOW)
    sums = add(sums, after(far_sums, sent)).astype(LOW)
    facing = lax.ppermute(sums, "tensor", TENSOR_SWAP)
    low_rows = [move(sent[12 * i : 12 * i + 12], FALL[k]) for i, k in enumerate((1, 2, 3))]
    own = base[42:] + move(sent[36:42], FALL[4]).astype(F32)
    chip = sum(block.astype(F32) for block in low_rows)
    passed = move(chip[6:].astype(LOW), SIBLING)
    own_grad = own + chip[:6] + passed.astype(F32)

    left = jnp.where(side == 0, sums, facing).astype(F32)
    right = jnp.where(side == 0, facing, sums).astype(F32)
    down_total = jnp.concatenate([left[:, :half], right[:, :half]], 1)
    up_total = jnp.concatenate([left[:, half:], right[:, half:]], 1)
    return (
        own_grad.reshape(vision_feature_states.shape),
        down_total.reshape(1, 2, ranks // 2, 2 * half),
        up_total.reshape(1, 2, ranks // 2, 2 * width),
    )


def solution(mesh):
    in_specs = (
        P("section", "dp", None, "tensor"),
        P("section", "dp", None, "tensor"),
        P("dp", "section", "tensor"),
        P("section", None, None, "tensor"),
        P("section", None, None, None),
        P("section", None, None, None),
        P("section", None, None),
        P("dp"),
        P("dp"),
    )
    out_specs = (
        P("dp", "section", "tensor"),
        P("section", None, None, None),
        P("section", None, None, None),
    )
    return jax.shard_map(
        per_device, mesh=mesh, in_specs=in_specs, out_specs=out_specs, check_vma=False
    )
```

```python
import jax
import jax.numpy as jnp
from jax import lax
from jax.experimental import pallas as pl
from jax.experimental.pallas import tpu as pltpu
from jax.sharding import PartitionSpec as P

TILES = 4
ADAPTER_SCALE = 2.0
EPS = 1e-05
PLANE = ("section", "tensor")
NZ = 8


def plane_pairs(route):
    def index(x, z, core):
        return (((x // 2) * NZ + z) * 2 + core) * 2 + x % 2

    return [
        (index(x, z, core), index(*route(x, z, core)))
        for x in range(4)
        for z in range(NZ)
        for core in range(2)
    ]


SIBLING = plane_pairs(lambda x, z, core: (x, z, 1 - core))
SHIFTS = (4, 3, 5, 2, 6, 1, 7)
ALONG = {
    k: plane_pairs(lambda x, z, core, k=k: (x, (z + k) % NZ, core)) for k in SHIFTS
}
NEAR = plane_pairs(lambda x, z, core: (x ^ 1 if core == 0 else 3 - x, z, core))
FAR = plane_pairs(lambda x, z, core: (3 - x if core == 0 else x ^ 1, z, core))
TENSOR_SWAP = [(0, 1), (1, 0)]
DP_NEAR = [(i, i ^ 1) for i in range(4)]
DP_FAR = [(i, 3 - i) for i in range(4)]


def move(block, pairs):
    return lax.ppermute(block, PLANE, pairs)


def after(value, *others):
    return lax.optimization_barrier((value, *others))[0]


NT = (((1,), (1,)), ((), ()))
TN = (((0,), (0,)), ((), ()))
F32, LOW = jnp.float32, jnp.bfloat16
ROOM = pltpu.CompilerParams(vmem_limit_bytes=48 * 1024 * 1024)


def dot(first, second, dims=(((1,), (0,)), ((), ()))):
    return lax.dot_general(first, second, dims, preferred_element_type=F32)


def cost(flops, moved):
    return pl.CostEstimate(flops=int(flops), bytes_accessed=int(moved), transcendentals=0)


def pair_kernel(gain_ref, query_ref, context_ref, pair_ref):
    gain = gain_ref[0:1, :].astype(F32)
    head = gain.shape[1]
    text = query_ref.shape[1]
    kv_heads = pair_ref.shape[0]
    group = query_ref.shape[2] // (head * kv_heads)
    for kv in range(kv_heads):
        for member in range(group):
            columns = slice((kv * group + member) * head, (kv * group + member + 1) * head)
            rows = slice(member * text, (member + 1) * text)
            query = query_ref[0, :, columns].astype(F32)
            scale = lax.rsqrt(jnp.mean(query * query, axis=-1, keepdims=True) + EPS)
            pair_ref[kv, rows, 0:head] = (query * scale * gain).astype(LOW)
            pair_ref[kv, rows, head : 2 * head] = context_ref[0, :, columns]


def pair_queries(queries, context, gains, kv_heads):
    batches, text, wide = queries.shape
    head = gains.shape[1]
    rows = wide // (kv_heads * head) * text
    block = pl.BlockSpec((1, text, wide), lambda b: (b, 0, 0))
    return pl.pallas_call(
        pair_kernel,
        out_shape=jax.ShapeDtypeStruct((batches * kv_heads, rows, 2 * head), LOW),
        grid=(batches,),
        in_specs=[pl.BlockSpec(gains.shape, lambda b: (0, 0)), block, block],
        out_specs=pl.BlockSpec((kv_heads, rows, 2 * head), lambda b: (b, 0, 0)),
        compiler_params=ROOM,
        cost_estimate=cost(2e8, 4 * queries.size * 2),
        name="pair_queries",
    )(gains, queries, context)


def project_kernel(which_ref, *refs):
    *row_refs, w_ref, a_ref, y_ref, r_ref = refs
    rows = jnp.concatenate([ref[...] for ref in row_refs])
    maps = a_ref[...].reshape(-1, a_ref.shape[2])

    @pl.when(pl.program_id(0) == 0)
    def _():
        y_ref[...] = jnp.zeros_like(y_ref)
        r_ref[...] = jnp.zeros_like(r_ref)

    for part in range(2):
        y_ref[part] += dot(rows, w_ref[part])
    r_ref[...] += dot(rows, maps, NT)


def project(blocks, weights, down_maps, which):
    count, half = len(blocks) * blocks[0].shape[0], blocks[0].shape[1]
    chunk = 1024
    steps = half // chunk
    width, ranks = weights.shape[2], 2 * down_maps.shape[1]
    grid_spec = pltpu.PrefetchScalarGridSpec(
        num_scalar_prefetch=1,
        grid=(steps,),
        in_specs=[pl.BlockSpec((block.shape[0], chunk), lambda i, s: (0, i)) for block in blocks]
        + [
            pl.BlockSpec((2, chunk, width), lambda i, s: (0, s[0] * steps + i, 0)),
            pl.BlockSpec((2, ranks // 2, chunk), lambda i, s: (0, 0, s[0] * steps + i)),
        ],
        out_specs=[
            pl.BlockSpec((2, count, width), lambda i, s: (0, 0, 0)),
            pl.BlockSpec((count, ranks), lambda i, s: (0, 0)),
        ],
    )
    return pl.pallas_call(
        project_kernel,
        out_shape=[
            jax.ShapeDtypeStruct((2, count, width), F32),
            jax.ShapeDtypeStruct((count, ranks), F32),
        ],
        grid_spec=grid_spec,
        compiler_params=ROOM,
        cost_estimate=cost(4 * 192 * half * width, 4 * half * width + 2 * count * half),
        name="project",
    )(which, *blocks, weights, down_maps)


def attention_kernel(
    count_ref, start_ref, y0, y1, y2, r0, r1, r2, own_map, other_map, own_back, other_back,
    up_diagonal, gains_ref, pair_ref, g_own, m_own, g_other, m_other, up_ref, grad_ref,
):
    width = y0.shape[2]
    head = gains_ref.shape[1]
    kv_heads = width // head
    batches = pair_ref.shape[0] // kv_heads
    tokens = own_map.shape[0] // batches
    ranks = r0.shape[1]
    text = 128
    scale = head ** (-0.5)

    def ordered(own, other):
        total = None
        for mapping, values in ((own_map, own), (other_map, other)):
            high = values.astype(LOW)
            rest = values - high.astype(F32)
            middle = rest.astype(LOW)
            lowest = (rest - middle.astype(F32)).astype(LOW)
            for term in (lowest, middle, high):
                moved = dot(mapping[...], term)
                total = moved if total is None else total + moved
        return total

    reduced = ordered(jnp.concatenate([r0[...], r1[...]]), r2[...]).astype(LOW)
    adapted = ADAPTER_SCALE * dot(reduced, up_diagonal[...])
    raw = [
        ordered(jnp.concatenate([y0[part], y1[part]]), y2[part])
        + adapted[:, part * width : (part + 1) * width]
        for part in range(2)
    ]
    gain = gains_ref[1:2, :].astype(F32)
    lane = lax.broadcasted_iota(jnp.int32, (1, pair_ref.shape[1]), 1) % text
    token = lax.broadcasted_iota(jnp.int32, (tokens, 1), 0)
    for kv in range(kv_heads):
        columns = slice(kv * head, (kv + 1) * head)
        key_raw = raw[0][:, columns]
        key_scale = lax.rsqrt(jnp.mean(key_raw * key_raw, axis=-1, keepdims=True) + EPS)
        unit = key_raw * key_scale
        keys = (unit * gain).astype(LOW)
        values = raw[1][:, columns].astype(LOW)
        for batch in range(batches):
            rows = slice(batch * tokens, (batch + 1) * tokens)
            none = jnp.zeros((tokens, head), LOW)
            both = jnp.concatenate(
                [
                    jnp.concatenate([keys[rows], none], 1),
                    jnp.concatenate([none, values[rows]], 1),
                ]
            )
            pair = pair_ref[batch * kv_heads + kv]
            scores = dot(both, pair, NT)
            allowed = token < count_ref[batch] * (tokens // TILES)
            live = (lane >= start_ref[batch]).astype(F32)
            weighted = jnp.where(allowed, jnp.exp(scores[:tokens] * scale), 0.0)
            attention = weighted * (live / jnp.sum(weighted, axis=0, keepdims=True))
            probs = scores[tokens:]
            mean = jnp.sum(attention * probs, axis=0, keepdims=True)
            grads = attention * (probs - mean) * scale
            out = dot(jnp.concatenate([grads.astype(LOW), attention.astype(LOW)]), pair)
            gained = out[:tokens, :head] * gain
            inner = jnp.mean(gained * unit[rows], axis=-1, keepdims=True)
            grad_ref[rows, columns] = (key_scale[rows] * (gained - unit[rows] * inner)).astype(LOW)
            grad_ref[rows, width + kv * head : width + (kv + 1) * head] = out[
                tokens:, head:
            ].astype(LOW)
    grad = grad_ref[...]
    middle = dot(grad, up_diagonal[...], NT).astype(LOW)
    up = ADAPTER_SCALE * dot(reduced, grad, TN)
    for part in range(2):
        half = slice(part * ranks // 2, (part + 1) * ranks // 2)
        up_ref[half, :] = up[half, part * width : (part + 1) * width]
    for back, g_ref, m_ref in ((own_back, g_own, m_own), (other_back, g_other, m_other)):
        g_ref[...] = dot(back[...], grad).astype(LOW)
        m_ref[...] = (ADAPTER_SCALE * dot(back[...], middle)).astype(LOW)


def attend(counts, starts, projected, maps, up_diagonal, gains, pair):
    (y0, r0), (y1, r1), (y2, r2) = projected
    rows, ranks, width = y2.shape[1], r0.shape[1], y0.shape[2]
    scalar = pl.BlockSpec(memory_space=pltpu.SMEM)
    vector = pl.BlockSpec(memory_space=pltpu.VMEM)
    return pl.pallas_call(
        attention_kernel,
        out_shape=[
            jax.ShapeDtypeStruct((rows, 2 * width), LOW),
            jax.ShapeDtypeStruct((rows, ranks), LOW),
            jax.ShapeDtypeStruct((rows, 2 * width), LOW),
            jax.ShapeDtypeStruct((rows, ranks), LOW),
            jax.ShapeDtypeStruct((ranks, width), F32),
        ],
        in_specs=[scalar, scalar] + [vector] * 13,
        out_specs=[vector] * 5,
        scratch_shapes=[pltpu.VMEM((rows, 2 * width), LOW)],
        compiler_params=ROOM,
        cost_estimate=cost(1e9, 2 * pair.size),
        name="attend",
    )(counts, starts, y0, y1, y2, r0, r1, r2, *maps, up_diagonal, gains, pair)


def feature_kernel(which_ref, g_ref, m_ref, w_ref, a_ref, *out_refs):
    width = w_ref.shape[2]
    total = dot(m_ref[...], a_ref[...].reshape(-1, a_ref.shape[2]))
    for part in range(2):
        total += dot(g_ref[:, part * width : (part + 1) * width], w_ref[part], NT)
    cut = out_refs[0].shape[0]
    for i, ref in enumerate(out_refs):
        ref[...] = total[i * cut : (i + 1) * cut].astype(LOW)


def feature_grad(grad, middle, weights, down_maps, which):
    rows, wide = grad.shape
    ranks = middle.shape[1]
    half = weights.shape[1] // 2
    chunk = 1024
    steps = half // chunk
    cut = rows // 4
    grid_spec = pltpu.PrefetchScalarGridSpec(
        num_scalar_prefetch=1,
        grid=(steps,),
        in_specs=[
            pl.BlockSpec((rows, wide), lambda i, s: (0, 0)),
            pl.BlockSpec((rows, ranks), lambda i, s: (0, 0)),
            pl.BlockSpec((2, chunk, wide // 2), lambda i, s: (0, s[0] * steps + i, 0)),
            pl.BlockSpec((2, ranks // 2, chunk), lambda i, s: (0, 0, s[0] * steps + i)),
        ],
        out_specs=[pl.BlockSpec((cut, chunk), lambda i, s: (0, i))] * 4,
    )
    return pl.pallas_call(
        feature_kernel,
        out_shape=[jax.ShapeDtypeStruct((cut, half), LOW)] * 4,
        grid_spec=grid_spec,
        compiler_params=ROOM,
        cost_estimate=cost(2 * rows * half * wide, 2 * half * (wide + rows)),
        name="feature_grad",
    )(which, grad, middle, weights, down_maps)


def down_kernel(m_ref, *refs):
    *row_refs, out_ref = refs
    rows = jnp.concatenate([ref[...] for ref in row_refs])
    out_ref[...] = dot(m_ref[...], rows, TN).astype(out_ref.dtype)


def down_grad(middle, blocks, dtype):
    half = blocks[0].shape[1]
    chunk = 1024
    return pl.pallas_call(
        down_kernel,
        out_shape=jax.ShapeDtypeStruct((middle.shape[1], half), dtype),
        grid=(half // chunk,),
        in_specs=[pl.BlockSpec(middle.shape, lambda i: (0, 0))]
        + [pl.BlockSpec((block.shape[0], chunk), lambda i: (0, i)) for block in blocks],
        out_specs=pl.BlockSpec((middle.shape[1], chunk), lambda i: (0, i)),
        compiler_params=ROOM,
        cost_estimate=cost(5e8, 2 * 200 * half),
        name="down_grad",
    )(middle, *blocks)


def row_tokens(x_hi, z, core, x_lo):
    def base_rows(chain, x_high):
        rows = []
        for k in (*SHIFTS, 0):
            token = ((x_high * NZ + (z - k) % NZ) * 2 + chain) * 2
            for batch in range(3):
                rows += [batch * 64 + token, batch * 64 + token + 1]
        return jnp.stack(rows)

    own_half, other_half = [], []
    for chain in (core, 1 - core):
        own_half += [base_rows(chain, x_hi)]
        near = jnp.where(chain == 0, x_hi, 1 - x_hi)
        other_half += [base_rows(chain, near), base_rows(chain, 1 - near)]
    for chain in (core, 1 - core):
        own_half += [base_rows(chain, 1 - x_hi)]
    return jnp.concatenate(own_half), jnp.concatenate(other_half)


def per_device(
    queries,
    context_gradient,
    vision_feature_states,
    key_value_weight,
    adapter_down_maps,
    adapter_up_maps,
    norm_gain_pair,
    image_tile_count,
    text_start_position,
):
    weights, down_maps, gains = key_value_weight[0], adapter_down_maps[0], norm_gain_pair[0]
    section, side = lax.axis_index("section"), lax.axis_index("tensor")
    width, half = weights.shape[2], vision_feature_states.shape[2]
    ranks = 2 * down_maps.shape[1]
    here = side.reshape(1).astype(jnp.int32)
    opposite = 1 - here

    own = vision_feature_states.reshape(-1, half)
    base = jnp.concatenate([move(own, ALONG[k]) for k in SHIFTS] + [own])
    first = move(base, NEAR)
    second = move(base, FAR)
    base_there = move(base, SIBLING)
    late_side = after(side, base)
    late_section = after(section, base)
    up_maps = lax.dynamic_slice_in_dim(adapter_up_maps[0], late_side * width, width, 2)
    up_diagonal = jnp.concatenate(
        [jnp.pad(up_maps[0], ((0, 0), (0, width))), jnp.pad(up_maps[1], ((0, 0), (width, 0)))]
    )
    own_token, other_token = row_tokens(
        late_section // 16, (late_section // 2) % NZ, late_section % 2, late_side
    )
    line = jnp.arange(own_token.shape[0])
    maps = [
        (line[:, None] == own_token[None]).astype(LOW),
        (line[:, None] == other_token[None]).astype(LOW),
        (own_token[:, None] == line[None]).astype(LOW),
        (other_token[:, None] == line[None]).astype(LOW),
    ]
    pair = pair_queries(
        after(queries[0], base), context_gradient[0], gains, width // gains.shape[1]
    )
    step_a = project([base, base_there], weights, down_maps, here)
    first = after(first, pair, *step_a, up_diagonal, *maps)
    third = move(first, FAR)
    first_there = move(first, SIBLING)
    second_there = move(second, SIBLING)
    others = [first, second, first_there, second_there]
    step_b = project(others, weights, down_maps, opposite)
    third = after(third, *step_b)
    third_there = move(third, SIBLING)
    step_c = project([third, third_there], weights, down_maps, here)
    owns = [base, base_there, third, third_there]

    g_own, m_own, g_other, m_other, up_part = attend(
        image_tile_count,
        text_start_position,
        (step_a, step_c, step_b),
        maps,
        up_diagonal,
        gains,
        pair,
    )

    down_other = down_grad(m_other, others, LOW)
    down_facing = lax.ppermute(down_other, "tensor", TENSOR_SWAP)
    base, base_out, third, third_out = feature_grad(
        after(g_own, down_other), m_own, weights, down_maps, here
    )
    down_own = down_grad(m_own, owns, F32)
    sums = jnp.concatenate(
        [down_own + after(down_facing, base).astype(F32), up_part], 1
    ).astype(LOW)
    near_sums = lax.ppermute(sums, "dp", DP_NEAR)

    def add(mine, theirs):
        return mine.astype(F32) + theirs.astype(F32)

    third = add(third, move(third_out, SIBLING)).astype(LOW)
    third_in = move(third, FAR)
    first, second, first_out, second_out = feature_grad(
        after(g_other, sums, third), m_other, weights, down_maps, opposite
    )
    second = add(second, move(second_out, SIBLING)).astype(LOW)
    first = add(first, move(first_out, SIBLING))
    base = add(base, move(base_out, SIBLING))

    second_in = move(second, FAR)
    sums = add(sums, after(near_sums, second)).astype(LOW)
    far_sums = lax.ppermute(sums, "dp", DP_FAR)
    first = (first + third_in.astype(F32)).astype(LOW)
    first_in = move(first, NEAR)
    sums = add(sums, after(far_sums, first)).astype(LOW)
    facing = lax.ppermute(sums, "tensor", TENSOR_SWAP)
    base = base + second_in.astype(F32) + first_in.astype(F32)
    low_base = base.astype(LOW)
    count = own.shape[0]
    own_grad = base[len(SHIFTS) * count :]
    for i, k in enumerate(SHIFTS):
        own_grad += move(low_base[i * count : (i + 1) * count], ALONG[NZ - k]).astype(F32)

    left = jnp.where(side == 0, sums, facing).astype(F32)
    right = jnp.where(side == 0, facing, sums).astype(F32)
    down_total = jnp.concatenate([left[:, :half], right[:, :half]], 1)
    up_total = jnp.concatenate([left[:, half:], right[:, half:]], 1)
    return (
        own_grad.reshape(vision_feature_states.shape),
        down_total.reshape(1, 2, ranks // 2, 2 * half),
        up_total.reshape(1, 2, ranks // 2, 2 * width),
    )


def solution(mesh):
    in_specs = (
        P("section", "dp", None, "tensor"),
        P("section", "dp", None, "tensor"),
        P("dp", "section", "tensor"),
        P("section", None, None, "tensor"),
        P("section", None, None, None),
        P("section", None, None, None),
        P("section", None, None),
        P("dp"),
        P("dp"),
    )
    out_specs = (
        P("dp", "section", "tensor"),
        P("section", None, None, None),
        P("section", None, None, None),
    )
    return jax.shard_map(
        per_device, mesh=mesh, in_specs=in_specs, out_specs=out_specs, check_vma=False
    )
```

```python
import jax
import jax.numpy as jnp
from jax import lax
from jax.experimental import pallas as pl
from jax.experimental.pallas import tpu as pltpu
from jax.sharding import PartitionSpec as P

TILES = 4
ADAPTER_SCALE = 2.0
EPS = 1e-05
PLANE = ("section", "tensor")
NZ = 8


def plane_pairs(route):
    def index(x, z, core):
        return (((x // 2) * NZ + z) * 2 + core) * 2 + x % 2

    return [
        (index(x, z, core), index(*route(x, z, core)))
        for x in range(4)
        for z in range(NZ)
        for core in range(2)
    ]


SIBLING = plane_pairs(lambda x, z, core: (x, z, 1 - core))
SHIFTS = (4, 3, 5, 2, 6, 1, 7)
ALONG = {
    k: plane_pairs(lambda x, z, core, k=k: (x, (z + k) % NZ, core)) for k in SHIFTS
}
NEAR = plane_pairs(lambda x, z, core: (x ^ 1 if core == 0 else 3 - x, z, core))
FAR = plane_pairs(lambda x, z, core: (3 - x if core == 0 else x ^ 1, z, core))
TENSOR_SWAP = [(0, 1), (1, 0)]
DP_NEAR = [(i, i ^ 1) for i in range(4)]
DP_FAR = [(i, 3 - i) for i in range(4)]


def move(block, pairs):
    return lax.ppermute(block, PLANE, pairs)


def after(value, *others):
    return lax.optimization_barrier((value, *others))[0]


NT = (((1,), (1,)), ((), ()))
TN = (((0,), (0,)), ((), ()))
F32, LOW = jnp.float32, jnp.bfloat16
ROOM = pltpu.CompilerParams(vmem_limit_bytes=20 * 1024 * 1024)
SCALAR = pl.BlockSpec(memory_space=pltpu.SMEM)
VECTOR = pl.BlockSpec(memory_space=pltpu.VMEM)
CHUNK = 1024


def dot(first, second, dims=(((1,), (0,)), ((), ()))):
    return lax.dot_general(first, second, dims, preferred_element_type=F32)


def cost(flops, moved):
    return pl.CostEstimate(flops=int(flops), bytes_accessed=int(moved), transcendentals=0)


def pair_kernel(gain_ref, query_ref, context_ref, pair_ref):
    gain = gain_ref[0:1, :].astype(F32)
    head = gain.shape[1]
    text = query_ref.shape[1]
    kv_heads = pair_ref.shape[0]
    group = query_ref.shape[2] // (head * kv_heads)
    for kv in range(kv_heads):
        for member in range(group):
            columns = slice((kv * group + member) * head, (kv * group + member + 1) * head)
            rows = slice(member * text, (member + 1) * text)
            query = query_ref[0, :, columns].astype(F32)
            scale = lax.rsqrt(jnp.mean(query * query, axis=-1, keepdims=True) + EPS)
            pair_ref[kv, rows, 0:head] = (query * scale * gain).astype(LOW)
            pair_ref[kv, rows, head : 2 * head] = context_ref[0, :, columns]


def pair_queries(queries, context, gains, kv_heads):
    batches, text, wide = queries.shape
    head = gains.shape[1]
    rows = wide // (kv_heads * head) * text
    block = pl.BlockSpec((1, text, wide), lambda b: (b, 0, 0))
    return pl.pallas_call(
        pair_kernel,
        out_shape=jax.ShapeDtypeStruct((batches * kv_heads, rows, 2 * head), LOW),
        grid=(batches,),
        in_specs=[pl.BlockSpec(gains.shape, lambda b: (0, 0)), block, block],
        out_specs=pl.BlockSpec((kv_heads, rows, 2 * head), lambda b: (b, 0, 0)),
        compiler_params=ROOM,
        cost_estimate=cost(2e8, 4 * queries.size * 2),
        name="pair_queries",
    )(gains, queries, context)


def hold_kernel(ready_ref, from_ref, to_ref, semaphore):
    copy = pltpu.make_async_copy(from_ref, to_ref, semaphore)
    copy.start()
    copy.wait()


def hold(array, ready):
    return pl.pallas_call(
        hold_kernel,
        out_shape=pltpu.VMEM(array.shape, array.dtype),
        in_specs=[pl.BlockSpec(memory_space=pl.ANY), pl.BlockSpec(memory_space=pltpu.HBM)],
        scratch_shapes=[pltpu.SemaphoreType.DMA],
        out_specs=VECTOR,
        compiler_params=ROOM,
        cost_estimate=cost(0, 2 * array.size),
        name="hold",
    )(ready, array)


def project_kernel(which_ref, *refs):
    *row_refs, w_ref, a_ref, y_ref, r_ref = refs
    half = row_refs[0].shape[1]
    totals = [None, None, None]
    for i in range(half // CHUNK):
        rows = jnp.concatenate([ref[:, i * CHUNK : (i + 1) * CHUNK] for ref in row_refs])
        place = pl.ds(pl.multiple_of(which_ref[0] * half + i * CHUNK, CHUNK), CHUNK)
        maps = a_ref[:, :, place].reshape(-1, CHUNK)
        terms = [dot(rows, w_ref[part, place, :]) for part in range(2)] + [dot(rows, maps, NT)]
        totals = [new if old is None else old + new for old, new in zip(totals, terms)]
    y_ref[0] = totals[0]
    y_ref[1] = totals[1]
    r_ref[...] = totals[2]


def project(blocks, weights, down_maps, which):
    count, half = len(blocks) * blocks[0].shape[0], blocks[0].shape[1]
    width, ranks = weights.shape[2], 2 * down_maps.shape[1]
    return pl.pallas_call(
        project_kernel,
        out_shape=[
            jax.ShapeDtypeStruct((2, count, width), F32),
            jax.ShapeDtypeStruct((count, ranks), F32),
        ],
        in_specs=[SCALAR] + [VECTOR] * (len(blocks) + 2),
        out_specs=[VECTOR] * 2,
        compiler_params=ROOM,
        cost_estimate=cost(4 * 192 * half * width, 4 * half * width + 2 * count * half),
        name="project",
    )(which, *blocks, weights, down_maps)


def attention_kernel(
    count_ref, start_ref, y0, y1, y2, r0, r1, r2, own_map, other_map, own_back, other_back,
    up_diagonal, gains_ref, pair_ref, g_own, m_own, g_other, m_other, up_ref, grad_ref,
):
    width = y0.shape[2]
    head = gains_ref.shape[1]
    kv_heads = width // head
    batches = pair_ref.shape[0] // kv_heads
    tokens = own_map.shape[0] // batches
    ranks = r0.shape[1]
    text = 128
    scale = head ** (-0.5)

    def ordered(own, other):
        total = None
        for mapping, values in ((own_map, own), (other_map, other)):
            high = values.astype(LOW)
            rest = values - high.astype(F32)
            middle = rest.astype(LOW)
            lowest = (rest - middle.astype(F32)).astype(LOW)
            for term in (lowest, middle, high):
                moved = dot(mapping[...], term)
                total = moved if total is None else total + moved
        return total

    reduced = ordered(jnp.concatenate([r0[...], r1[...]]), r2[...]).astype(LOW)
    adapted = ADAPTER_SCALE * dot(reduced, up_diagonal[...])
    raw = [
        ordered(jnp.concatenate([y0[part], y1[part]]), y2[part])
        + adapted[:, part * width : (part + 1) * width]
        for part in range(2)
    ]
    gain = gains_ref[1:2, :].astype(F32)
    lane = lax.broadcasted_iota(jnp.int32, (1, pair_ref.shape[1]), 1) % text
    token = lax.broadcasted_iota(jnp.int32, (tokens, 1), 0)
    for kv in range(kv_heads):
        columns = slice(kv * head, (kv + 1) * head)
        key_raw = raw[0][:, columns]
        key_scale = lax.rsqrt(jnp.mean(key_raw * key_raw, axis=-1, keepdims=True) + EPS)
        unit = key_raw * key_scale
        keys = (unit * gain).astype(LOW)
        values = raw[1][:, columns].astype(LOW)
        for batch in range(batches):
            rows = slice(batch * tokens, (batch + 1) * tokens)
            none = jnp.zeros((tokens, head), LOW)
            both = jnp.concatenate(
                [
                    jnp.concatenate([keys[rows], none], 1),
                    jnp.concatenate([none, values[rows]], 1),
                ]
            )
            pair = pair_ref[batch * kv_heads + kv]
            scores = dot(both, pair, NT)
            allowed = token < count_ref[batch] * (tokens // TILES)
            live = (lane >= start_ref[batch]).astype(F32)
            weighted = jnp.where(allowed, jnp.exp(scores[:tokens] * scale), 0.0)
            attention = weighted * (live / jnp.sum(weighted, axis=0, keepdims=True))
            probs = scores[tokens:]
            mean = jnp.sum(attention * probs, axis=0, keepdims=True)
            grads = attention * (probs - mean) * scale
            out = dot(jnp.concatenate([grads.astype(LOW), attention.astype(LOW)]), pair)
            gained = out[:tokens, :head] * gain
            inner = jnp.mean(gained * unit[rows], axis=-1, keepdims=True)
            grad_ref[rows, columns] = (key_scale[rows] * (gained - unit[rows] * inner)).astype(LOW)
            grad_ref[rows, width + kv * head : width + (kv + 1) * head] = out[
                tokens:, head:
            ].astype(LOW)
    grad = grad_ref[...]
    middle = dot(grad, up_diagonal[...], NT).astype(LOW)
    up = ADAPTER_SCALE * dot(reduced, grad, TN)
    for part in range(2):
        half = slice(part * ranks // 2, (part + 1) * ranks // 2)
        up_ref[half, :] = up[half, part * width : (part + 1) * width]
    for back, g_ref, m_ref in ((own_back, g_own, m_own), (other_back, g_other, m_other)):
        g_ref[...] = dot(back[...], grad).astype(LOW)
        m_ref[...] = (ADAPTER_SCALE * dot(back[...], middle)).astype(LOW)


def attend(counts, starts, projected, maps, up_diagonal, gains, pair):
    (y0, r0), (y1, r1), (y2, r2) = projected
    rows, ranks, width = y2.shape[1], r0.shape[1], y0.shape[2]
    scalar = pl.BlockSpec(memory_space=pltpu.SMEM)
    vector = pl.BlockSpec(memory_space=pltpu.VMEM)
    return pl.pallas_call(
        attention_kernel,
        out_shape=[
            jax.ShapeDtypeStruct((rows, 2 * width), LOW),
            jax.ShapeDtypeStruct((rows, ranks), LOW),
            jax.ShapeDtypeStruct((rows, 2 * width), LOW),
            jax.ShapeDtypeStruct((rows, ranks), LOW),
            jax.ShapeDtypeStruct((ranks, width), F32),
        ],
        in_specs=[scalar, scalar] + [vector] * 13,
        out_specs=[vector] * 5,
        scratch_shapes=[pltpu.VMEM((rows, 2 * width), LOW)],
        compiler_params=ROOM,
        cost_estimate=cost(1e9, 2 * pair.size),
        name="attend",
    )(counts, starts, y0, y1, y2, r0, r1, r2, *maps, up_diagonal, gains, pair)


def feature_kernel(which_ref, g_ref, m_ref, w_ref, a_ref, *out_refs):
    width = w_ref.shape[2]
    cut, half = out_refs[0].shape
    for i in range(half // CHUNK):
        place = pl.ds(pl.multiple_of(which_ref[0] * half + i * CHUNK, CHUNK), CHUNK)
        total = dot(m_ref[...], a_ref[:, :, place].reshape(-1, CHUNK))
        for part in range(2):
            total += dot(g_ref[:, part * width : (part + 1) * width], w_ref[part, place, :], NT)
        for j, ref in enumerate(out_refs):
            ref[:, i * CHUNK : (i + 1) * CHUNK] = total[j * cut : (j + 1) * cut].astype(LOW)


def feature_grad(grad, middle, weights, down_maps, which):
    rows, wide = grad.shape
    half = weights.shape[1] // 2
    return pl.pallas_call(
        feature_kernel,
        out_shape=[jax.ShapeDtypeStruct((rows // 4, half), LOW)] * 4,
        in_specs=[SCALAR] + [VECTOR] * 4,
        out_specs=[VECTOR] * 4,
        compiler_params=ROOM,
        cost_estimate=cost(2 * rows * half * wide, 2 * half * (wide + rows)),
        name="feature_grad",
    )(which, grad, middle, weights, down_maps)


def down_kernel(m_ref, *refs):
    *row_refs, out_ref = refs
    rows = jnp.concatenate([ref[...] for ref in row_refs])
    out_ref[...] = dot(m_ref[...], rows, TN).astype(out_ref.dtype)


def down_grad(middle, blocks, dtype):
    half = blocks[0].shape[1]
    return pl.pallas_call(
        down_kernel,
        out_shape=jax.ShapeDtypeStruct((middle.shape[1], half), dtype),
        in_specs=[VECTOR] * (1 + len(blocks)),
        out_specs=VECTOR,
        compiler_params=ROOM,
        cost_estimate=cost(5e7, 2 * 200 * half),
        name="down_grad",
    )(middle, *blocks)


def row_tokens(x_hi, z, core, x_lo):
    def base_rows(chain, x_high):
        rows = []
        for k in (*SHIFTS, 0):
            token = ((x_high * NZ + (z - k) % NZ) * 2 + chain) * 2
            for batch in range(3):
                rows += [batch * 64 + token, batch * 64 + token + 1]
        return jnp.stack(rows)

    own_half, other_half = [], []
    for chain in (core, 1 - core):
        own_half += [base_rows(chain, x_hi)]
        near = jnp.where(chain == 0, x_hi, 1 - x_hi)
        other_half += [base_rows(chain, near), base_rows(chain, 1 - near)]
    for chain in (core, 1 - core):
        own_half += [base_rows(chain, 1 - x_hi)]
    return jnp.concatenate(own_half), jnp.concatenate(other_half)


def per_device(
    queries,
    context_gradient,
    vision_feature_states,
    key_value_weight,
    adapter_down_maps,
    adapter_up_maps,
    norm_gain_pair,
    image_tile_count,
    text_start_position,
):
    weights, down_maps, gains = key_value_weight[0], adapter_down_maps[0], norm_gain_pair[0]
    section, side = lax.axis_index("section"), lax.axis_index("tensor")
    width, half = weights.shape[2], vision_feature_states.shape[2]
    ranks = 2 * down_maps.shape[1]
    here = side.reshape(1).astype(jnp.int32)
    opposite = 1 - here

    own = vision_feature_states.reshape(-1, half)
    base = jnp.concatenate([move(own, ALONG[k]) for k in SHIFTS] + [own])
    first = move(base, NEAR)
    second = move(base, FAR)
    base_there = move(base, SIBLING)
    late_side = after(side, base)
    late_section = after(section, base)
    up_maps = lax.dynamic_slice_in_dim(adapter_up_maps[0], late_side * width, width, 2)
    up_diagonal = jnp.concatenate(
        [jnp.pad(up_maps[0], ((0, 0), (0, width))), jnp.pad(up_maps[1], ((0, 0), (width, 0)))]
    )
    own_token, other_token = row_tokens(
        late_section // 16, (late_section // 2) % NZ, late_section % 2, late_side
    )
    line = jnp.arange(own_token.shape[0])
    maps = [
        (line[:, None] == own_token[None]).astype(LOW),
        (line[:, None] == other_token[None]).astype(LOW),
        (own_token[:, None] == line[None]).astype(LOW),
        (other_token[:, None] == line[None]).astype(LOW),
    ]
    pair = pair_queries(
        after(queries[0], base), context_gradient[0], gains, width // gains.shape[1]
    )
    step_a = project([base, base_there], weights, down_maps, here)
    first = after(first, pair, *step_a, up_diagonal, *maps)
    weights = hold(weights, first)
    third = move(first, FAR)
    first_there = move(first, SIBLING)
    second_there = move(second, SIBLING)
    others = [first, second, first_there, second_there]
    step_b = project(others, weights, down_maps, opposite)
    third = after(third, *step_b)
    third_there = move(third, SIBLING)
    step_c = project([third, third_there], weights, down_maps, here)
    owns = [base, base_there, third, third_there]

    g_own, m_own, g_other, m_other, up_part = attend(
        image_tile_count,
        text_start_position,
        (step_a, step_c, step_b),
        maps,
        up_diagonal,
        gains,
        pair,
    )

    down_other = down_grad(m_other, others, LOW)
    down_facing = lax.ppermute(down_other, "tensor", TENSOR_SWAP)
    base, base_out, third, third_out = feature_grad(
        after(g_own, down_other), m_own, weights, down_maps, here
    )
    down_own = down_grad(m_own, owns, F32)

    def add(mine, theirs):
        return mine.astype(F32) + theirs.astype(F32)

    third = add(third, move(third_out, SIBLING)).astype(LOW)
    third_in = move(third, FAR)
    first, second, first_out, second_out = feature_grad(
        after(g_other, third, down_own), m_other, weights, down_maps, opposite
    )
    second = add(second, move(second_out, SIBLING)).astype(LOW)
    first = add(first, move(first_out, SIBLING))
    base = add(base, move(base_out, SIBLING))
    sums = jnp.concatenate(
        [down_own + after(down_facing, first_out).astype(F32), up_part], 1
    ).astype(LOW)
    near_sums = lax.ppermute(sums, "dp", DP_NEAR)
    second_in = move(second, FAR)
    first = (first + third_in.astype(F32)).astype(LOW)
    first_in = move(first, NEAR)
    sums = add(sums, after(near_sums, first)).astype(LOW)
    far_sums = lax.ppermute(sums, "dp", DP_FAR)
    base = base + second_in.astype(F32) + first_in.astype(F32)
    low_base = base.astype(LOW)
    sums = add(sums, after(far_sums, low_base)).astype(LOW)
    low_base = after(low_base, sums)
    facing = lax.ppermute(sums, "tensor", TENSOR_SWAP)
    count = own.shape[0]
    own_grad = base[len(SHIFTS) * count :]
    for i, k in enumerate(SHIFTS):
        own_grad += move(low_base[i * count : (i + 1) * count], ALONG[NZ - k]).astype(F32)

    left = jnp.where(side == 0, sums, facing).astype(F32)
    right = jnp.where(side == 0, facing, sums).astype(F32)
    down_total = jnp.concatenate([left[:, :half], right[:, :half]], 1)
    up_total = jnp.concatenate([left[:, half:], right[:, half:]], 1)
    return (
        own_grad.reshape(vision_feature_states.shape),
        down_total.reshape(1, 2, ranks // 2, 2 * half),
        up_total.reshape(1, 2, ranks // 2, 2 * width),
    )


def solution(mesh):
    in_specs = (
        P("section", "dp", None, "tensor"),
        P("section", "dp", None, "tensor"),
        P("dp", "section", "tensor"),
        P("section", None, None, "tensor"),
        P("section", None, None, None),
        P("section", None, None, None),
        P("section", None, None),
        P("dp"),
        P("dp"),
    )
    out_specs = (
        P("dp", "section", "tensor"),
        P("section", None, None, None),
        P("section", None, None, None),
    )
    return jax.shard_map(
        per_device, mesh=mesh, in_specs=in_specs, out_specs=out_specs, check_vma=False
    )
```

```python
import jax
import jax.numpy as jnp
from jax import lax
from jax.experimental import pallas as pl
from jax.experimental.pallas import tpu as pltpu
from jax.sharding import PartitionSpec as P

TILES = 4
ADAPTER_SCALE = 2.0
EPS = 1e-05
PLANE = ("section", "tensor")
NZ = 8


def plane_pairs(route):
    def index(x, z, core):
        return (((x // 2) * NZ + z) * 2 + core) * 2 + x % 2

    return [
        (index(x, z, core), index(*route(x, z, core)))
        for x in range(4)
        for z in range(NZ)
        for core in range(2)
    ]


SIBLING = plane_pairs(lambda x, z, core: (x, z, 1 - core))
SHIFTS = (4, 3, 5, 2, 6, 1, 7)
ALONG = {
    k: plane_pairs(lambda x, z, core, k=k: (x, (z + k) % NZ, core)) for k in SHIFTS
}
NEAR = plane_pairs(lambda x, z, core: (x ^ 1 if core == 0 else 3 - x, z, core))
FAR = plane_pairs(lambda x, z, core: (3 - x if core == 0 else x ^ 1, z, core))
TENSOR_SWAP = [(0, 1), (1, 0)]
DP_NEAR = [(i, i ^ 1) for i in range(4)]
DP_FAR = [(i, 3 - i) for i in range(4)]


def move(block, pairs):
    return lax.ppermute(block, PLANE, pairs)


def after(value, *others):
    return lax.optimization_barrier((value, *others))[0]


NT = (((1,), (1,)), ((), ()))
TN = (((0,), (0,)), ((), ()))
F32, LOW = jnp.float32, jnp.bfloat16
ROOM = pltpu.CompilerParams(vmem_limit_bytes=20 * 1024 * 1024)
SCALAR = pl.BlockSpec(memory_space=pltpu.SMEM)
VECTOR = pl.BlockSpec(memory_space=pltpu.VMEM)
CHUNK = 1024


def dot(first, second, dims=(((1,), (0,)), ((), ()))):
    return lax.dot_general(first, second, dims, preferred_element_type=F32)


def cost(flops, moved):
    return pl.CostEstimate(flops=int(flops) // 1000, bytes_accessed=int(moved) // 1000, transcendentals=0)


def pair_kernel(gain_ref, query_ref, context_ref, pair_ref):
    gain = gain_ref[0:1, :].astype(F32)
    head = gain.shape[1]
    text = query_ref.shape[1]
    kv_heads = pair_ref.shape[0]
    group = query_ref.shape[2] // (head * kv_heads)
    for kv in range(kv_heads):
        for member in range(group):
            columns = slice((kv * group + member) * head, (kv * group + member + 1) * head)
            rows = slice(member * text, (member + 1) * text)
            query = query_ref[0, :, columns].astype(F32)
            scale = lax.rsqrt(jnp.mean(query * query, axis=-1, keepdims=True) + EPS)
            pair_ref[kv, rows, 0:head] = (query * scale * gain).astype(LOW)
            pair_ref[kv, rows, head : 2 * head] = context_ref[0, :, columns]


def pair_queries(queries, context, gains, kv_heads):
    batches, text, wide = queries.shape
    head = gains.shape[1]
    rows = wide // (kv_heads * head) * text
    block = pl.BlockSpec((1, text, wide), lambda b: (b, 0, 0))
    return pl.pallas_call(
        pair_kernel,
        out_shape=jax.ShapeDtypeStruct((batches * kv_heads, rows, 2 * head), LOW),
        grid=(batches,),
        in_specs=[pl.BlockSpec(gains.shape, lambda b: (0, 0)), block, block],
        out_specs=pl.BlockSpec((kv_heads, rows, 2 * head), lambda b: (b, 0, 0)),
        compiler_params=ROOM,
        cost_estimate=cost(2e8, 4 * queries.size * 2),
        name="pair_queries",
    )(gains, queries, context)


def flatten_kernel(from_ref, to_ref):
    outer, inner, _ = from_ref.shape
    for i in range(outer):
        to_ref[i * inner : (i + 1) * inner, :] = from_ref[i]


def flatten(array):
    outer, inner, wide = array.shape
    return pl.pallas_call(
        flatten_kernel,
        out_shape=jax.ShapeDtypeStruct((outer * inner, wide), array.dtype),
        in_specs=[VECTOR],
        out_specs=VECTOR,
        compiler_params=ROOM,
        cost_estimate=cost(0, 4 * array.size),
        name="flatten",
    )(array)


def total_kernel(own_ref, *refs):
    *arrived, to_ref = refs
    rows = own_ref[...]
    for ref in arrived:
        rows += ref[...].astype(F32)
    outer, inner, _ = to_ref.shape
    for i in range(outer):
        to_ref[i] = rows[i * inner : (i + 1) * inner]


def total(own, arrived, shape):
    return pl.pallas_call(
        total_kernel,
        out_shape=jax.ShapeDtypeStruct(shape, F32),
        in_specs=[VECTOR] * (1 + len(arrived)),
        out_specs=VECTOR,
        compiler_params=ROOM,
        cost_estimate=cost(own.size * len(arrived), 2 * own.size * len(arrived)),
        name="total",
    )(own, *arrived)


def hold_kernel(ready_ref, from_ref, to_ref, semaphore):
    copy = pltpu.make_async_copy(from_ref, to_ref, semaphore)
    copy.start()
    copy.wait()


def hold(array, ready):
    return pl.pallas_call(
        hold_kernel,
        out_shape=pltpu.VMEM(array.shape, array.dtype),
        in_specs=[pl.BlockSpec(memory_space=pl.ANY), pl.BlockSpec(memory_space=pltpu.HBM)],
        scratch_shapes=[pltpu.SemaphoreType.DMA],
        out_specs=VECTOR,
        compiler_params=ROOM,
        cost_estimate=cost(0, 2 * array.size),
        name="hold",
    )(ready, array)


def project_kernel(which_ref, *refs):
    *row_refs, w_ref, a_ref, y_ref, r_ref = refs
    half = row_refs[0].shape[1]
    totals = [None, None, None]
    for i in range(half // CHUNK):
        rows = jnp.concatenate([ref[:, i * CHUNK : (i + 1) * CHUNK] for ref in row_refs])
        place = pl.ds(pl.multiple_of(which_ref[0] * half + i * CHUNK, CHUNK), CHUNK)
        maps = a_ref[:, :, place].reshape(-1, CHUNK)
        terms = [dot(rows, w_ref[part, place, :]) for part in range(2)] + [dot(rows, maps, NT)]
        totals = [new if old is None else old + new for old, new in zip(totals, terms)]
    y_ref[0] = totals[0]
    y_ref[1] = totals[1]
    r_ref[...] = totals[2]


def project(blocks, weights, down_maps, which):
    count, half = len(blocks) * blocks[0].shape[0], blocks[0].shape[1]
    width, ranks = weights.shape[2], 2 * down_maps.shape[1]
    return pl.pallas_call(
        project_kernel,
        out_shape=[
            jax.ShapeDtypeStruct((2, count, width), F32),
            jax.ShapeDtypeStruct((count, ranks), F32),
        ],
        in_specs=[SCALAR] + [VECTOR] * (len(blocks) + 2),
        out_specs=[VECTOR] * 2,
        compiler_params=ROOM,
        cost_estimate=cost(4 * 192 * half * width, 4 * half * width + 2 * count * half),
        name="project",
    )(which, *blocks, weights, down_maps)


def attention_kernel(
    count_ref, start_ref, y0, y1, y2, r0, r1, r2, own_map, other_map, own_back, other_back,
    up_diagonal, gains_ref, pair_ref, g_own, m_own, g_other, m_other, middle_ref, up_ref, grad_ref,
):
    width = y0.shape[2]
    head = gains_ref.shape[1]
    kv_heads = width // head
    batches = pair_ref.shape[0] // kv_heads
    tokens = own_map.shape[0] // batches
    ranks = r0.shape[1]
    text = 128
    scale = head ** (-0.5)

    def ordered(own, other):
        total = None
        for mapping, values in ((own_map, own), (other_map, other)):
            high = values.astype(LOW)
            rest = values - high.astype(F32)
            middle = rest.astype(LOW)
            lowest = (rest - middle.astype(F32)).astype(LOW)
            for term in (lowest, middle, high):
                moved = dot(mapping[...], term)
                total = moved if total is None else total + moved
        return total

    reduced = ordered(jnp.concatenate([r0[...], r1[...]]), r2[...]).astype(LOW)
    adapted = ADAPTER_SCALE * dot(reduced, up_diagonal[...])
    raw = [
        ordered(jnp.concatenate([y0[part], y1[part]]), y2[part])
        + adapted[:, part * width : (part + 1) * width]
        for part in range(2)
    ]
    gain = gains_ref[1:2, :].astype(F32)
    lane = lax.broadcasted_iota(jnp.int32, (1, pair_ref.shape[1]), 1) % text
    token = lax.broadcasted_iota(jnp.int32, (tokens, 1), 0)
    for kv in range(kv_heads):
        columns = slice(kv * head, (kv + 1) * head)
        key_raw = raw[0][:, columns]
        key_scale = lax.rsqrt(jnp.mean(key_raw * key_raw, axis=-1, keepdims=True) + EPS)
        unit = key_raw * key_scale
        keys = (unit * gain).astype(LOW)
        values = raw[1][:, columns].astype(LOW)
        for batch in range(batches):
            rows = slice(batch * tokens, (batch + 1) * tokens)
            none = jnp.zeros((tokens, head), LOW)
            both = jnp.concatenate(
                [
                    jnp.concatenate([keys[rows], none], 1),
                    jnp.concatenate([none, values[rows]], 1),
                ]
            )
            pair = pair_ref[batch * kv_heads + kv]
            scores = dot(both, pair, NT)
            allowed = token < count_ref[batch] * (tokens // TILES)
            live = (lane >= start_ref[batch]).astype(F32)
            weighted = jnp.where(allowed, jnp.exp(scores[:tokens] * scale), 0.0)
            attention = weighted * (live / jnp.sum(weighted, axis=0, keepdims=True))
            probs = scores[tokens:]
            mean = jnp.sum(attention * probs, axis=0, keepdims=True)
            grads = attention * (probs - mean) * scale
            out = dot(jnp.concatenate([grads.astype(LOW), attention.astype(LOW)]), pair)
            gained = out[:tokens, :head] * gain
            inner = jnp.mean(gained * unit[rows], axis=-1, keepdims=True)
            grad_ref[rows, columns] = (key_scale[rows] * (gained - unit[rows] * inner)).astype(LOW)
            grad_ref[rows, width + kv * head : width + (kv + 1) * head] = out[
                tokens:, head:
            ].astype(LOW)
    grad = grad_ref[...]
    middle = dot(grad, up_diagonal[...], NT).astype(LOW)
    middle_ref[...] = (ADAPTER_SCALE * middle.astype(F32)).astype(LOW)
    up = ADAPTER_SCALE * dot(reduced, grad, TN)
    for part in range(2):
        half = slice(part * ranks // 2, (part + 1) * ranks // 2)
        up_ref[half, :] = up[half, part * width : (part + 1) * width]
    for back, g_ref, m_ref in ((own_back, g_own, m_own), (other_back, g_other, m_other)):
        g_ref[...] = dot(back[...], grad).astype(LOW)
        m_ref[...] = (ADAPTER_SCALE * dot(back[...], middle)).astype(LOW)


def attend(counts, starts, projected, maps, up_diagonal, gains, pair):
    (y0, r0), (y1, r1), (y2, r2) = projected
    rows, ranks, width = y2.shape[1], r0.shape[1], y0.shape[2]
    scalar = pl.BlockSpec(memory_space=pltpu.SMEM)
    vector = pl.BlockSpec(memory_space=pltpu.VMEM)
    return pl.pallas_call(
        attention_kernel,
        out_shape=[
            jax.ShapeDtypeStruct((rows, 2 * width), LOW),
            jax.ShapeDtypeStruct((rows, ranks), LOW),
            jax.ShapeDtypeStruct((rows, 2 * width), LOW),
            jax.ShapeDtypeStruct((rows, ranks), LOW),
            jax.ShapeDtypeStruct((rows, ranks), LOW),
            jax.ShapeDtypeStruct((ranks, width), F32),
        ],
        in_specs=[scalar, scalar] + [vector] * 13,
        out_specs=[vector] * 6,
        scratch_shapes=[pltpu.VMEM((rows, 2 * width), LOW)],
        compiler_params=ROOM,
        cost_estimate=cost(1e9, 2 * pair.size),
        name="attend",
    )(counts, starts, y0, y1, y2, r0, r1, r2, *maps, up_diagonal, gains, pair)


def feature_kernel(which_ref, g_ref, m_ref, w_ref, a_ref, *out_refs):
    width = w_ref.shape[2]
    cut, half = out_refs[0].shape
    for i in range(half // CHUNK):
        place = pl.ds(pl.multiple_of(which_ref[0] * half + i * CHUNK, CHUNK), CHUNK)
        total = dot(m_ref[...], a_ref[:, :, place].reshape(-1, CHUNK))
        for part in range(2):
            total += dot(g_ref[:, part * width : (part + 1) * width], w_ref[part, place, :], NT)
        for j, ref in enumerate(out_refs):
            ref[:, i * CHUNK : (i + 1) * CHUNK] = total[j * cut : (j + 1) * cut].astype(LOW)


def feature_grad(grad, middle, weights, down_maps, which):
    rows, wide = grad.shape
    half = weights.shape[1] // 2
    return pl.pallas_call(
        feature_kernel,
        out_shape=[jax.ShapeDtypeStruct((rows // 4, half), LOW)] * 4,
        in_specs=[SCALAR] + [VECTOR] * 4,
        out_specs=[VECTOR] * 4,
        compiler_params=ROOM,
        cost_estimate=cost(2 * rows * half * wide, 2 * half * (wide + rows)),
        name="feature_grad",
    )(which, grad, middle, weights, down_maps)


def down_kernel(back_ref, mine_ref, facing_ref, *refs):
    *row_refs, out_ref = refs
    rows = jnp.concatenate([ref[...] for ref in row_refs])
    ranks = mine_ref.shape[1]
    both = jnp.concatenate([mine_ref[...], facing_ref[...]], 1)
    parts = dot(dot(back_ref[...], both).astype(LOW), rows, TN)
    out_ref[...] = parts[:ranks] + parts[ranks:]


def down_grad(back, mine, facing, blocks):
    ranks, half = mine.shape[1], blocks[0].shape[1]
    return pl.pallas_call(
        down_kernel,
        out_shape=jax.ShapeDtypeStruct((ranks, half), F32),
        in_specs=[VECTOR] * (3 + len(blocks)),
        out_specs=VECTOR,
        compiler_params=ROOM,
        cost_estimate=cost(5e7, 2 * 200 * half),
        name="down_grad",
    )(back, mine, facing, *blocks)


def row_tokens(x_hi, z, core, x_lo):
    def base_rows(chain, x_high):
        rows = []
        for k in (*SHIFTS, 0):
            token = ((x_high * NZ + (z - k) % NZ) * 2 + chain) * 2
            for batch in range(3):
                rows += [batch * 64 + token, batch * 64 + token + 1]
        return jnp.stack(rows)

    own_half, other_half = [], []
    for chain in (core, 1 - core):
        own_half += [base_rows(chain, x_hi)]
        near = jnp.where(chain == 0, x_hi, 1 - x_hi)
        other_half += [base_rows(chain, near), base_rows(chain, 1 - near)]
    for chain in (core, 1 - core):
        own_half += [base_rows(chain, 1 - x_hi)]
    return jnp.concatenate(own_half), jnp.concatenate(other_half)


def per_device(
    queries,
    context_gradient,
    vision_feature_states,
    key_value_weight,
    adapter_down_maps,
    adapter_up_maps,
    norm_gain_pair,
    image_tile_count,
    text_start_position,
):
    weights, down_maps, gains = key_value_weight[0], adapter_down_maps[0], norm_gain_pair[0]
    section, side = lax.axis_index("section"), lax.axis_index("tensor")
    width, half = weights.shape[2], vision_feature_states.shape[2]
    ranks = 2 * down_maps.shape[1]
    here = side.reshape(1).astype(jnp.int32)
    opposite = 1 - here

    own = flatten(vision_feature_states)
    base = jnp.concatenate([move(own, ALONG[k]) for k in SHIFTS] + [own])
    first = move(base, NEAR)
    second = move(base, FAR)
    base_there = move(base, SIBLING)
    late_side = after(side, base)
    late_section = after(section, base)
    up_maps = lax.dynamic_slice_in_dim(adapter_up_maps[0], late_side * width, width, 2)
    up_diagonal = jnp.concatenate(
        [jnp.pad(up_maps[0], ((0, 0), (0, width))), jnp.pad(up_maps[1], ((0, 0), (width, 0)))]
    )
    own_token, other_token = row_tokens(
        late_section // 16, (late_section // 2) % NZ, late_section % 2, late_side
    )
    line = jnp.arange(own_token.shape[0])
    maps = [
        (line[:, None] == own_token[None]).astype(LOW),
        (line[:, None] == other_token[None]).astype(LOW),
        (own_token[:, None] == line[None]).astype(LOW),
        (other_token[:, None] == line[None]).astype(LOW),
    ]
    pair = pair_queries(
        after(queries[0], base), context_gradient[0], gains, width // gains.shape[1]
    )
    weights = hold(weights, after(pair, up_diagonal, *maps))
    step_a = project([base, base_there], weights, down_maps, here)
    first = after(first, pair, *step_a, up_diagonal, *maps)
    third = move(first, FAR)
    first_there = move(first, SIBLING)
    second_there = move(second, SIBLING)
    others = [first, second, first_there, second_there]
    step_b = project(others, weights, down_maps, opposite)
    third = after(third, *step_b)
    third_there = move(third, SIBLING)
    step_c = project([third, third_there], weights, down_maps, here)
    owns = [base, base_there, third, third_there]

    g_own, m_own, g_other, m_other, middle, up_part = attend(
        image_tile_count,
        text_start_position,
        (step_a, step_c, step_b),
        maps,
        up_diagonal,
        gains,
        pair,
    )

    middle_facing = lax.ppermute(middle, "tensor", TENSOR_SWAP)
    base, base_out, third, third_out = feature_grad(g_own, m_own, weights, down_maps, here)

    def add(mine, theirs):
        return mine.astype(F32) + theirs.astype(F32)

    third = add(third, move(third_out, SIBLING)).astype(LOW)
    third_in = move(third, FAR)
    first, second, first_out, second_out = feature_grad(
        after(g_other, third), m_other, weights, down_maps, opposite
    )
    second = add(second, move(second_out, SIBLING)).astype(LOW)
    first = add(first, move(first_out, SIBLING))
    base = add(base, move(base_out, SIBLING))
    second_in = move(second, FAR)
    down_own = down_grad(maps[2], middle, after(middle_facing, second), owns)
    sums = jnp.concatenate([down_own, up_part], 1).astype(LOW)
    near_sums = lax.ppermute(sums, "dp", DP_NEAR)
    first = (first + third_in.astype(F32)).astype(LOW)
    first_in = move(first, NEAR)
    sums = add(sums, after(near_sums, second_in, first)).astype(LOW)
    far_sums = lax.ppermute(sums, "dp", DP_FAR)
    base = base + second_in.astype(F32) + first_in.astype(F32)
    low_base = base.astype(LOW)
    sums = add(sums, after(far_sums, low_base)).astype(LOW)
    low_base = after(low_base, sums)
    facing = lax.ppermute(sums, "tensor", TENSOR_SWAP)
    count = own.shape[0]
    arrived = [
        move(low_base[i * count : (i + 1) * count], ALONG[NZ - k]) for i, k in enumerate(SHIFTS)
    ]
    own_grad = total(base[len(SHIFTS) * count :], arrived, vision_feature_states.shape)

    left = jnp.where(side == 0, sums, facing).astype(F32)
    right = jnp.where(side == 0, facing, sums).astype(F32)
    down_total = jnp.concatenate([left[:, :half], right[:, :half]], 1)
    up_total = jnp.concatenate([left[:, half:], right[:, half:]], 1)
    return (
        own_grad,
        down_total.reshape(1, 2, ranks // 2, 2 * half),
        up_total.reshape(1, 2, ranks // 2, 2 * width),
    )


def solution(mesh):
    in_specs = (
        P("section", "dp", None, "tensor"),
        P("section", "dp", None, "tensor"),
        P("dp", "section", "tensor"),
        P("section", None, None, "tensor"),
        P("section", None, None, None),
        P("section", None, None, None),
        P("section", None, None),
        P("dp"),
        P("dp"),
    )
    out_specs = (
        P("dp", "section", "tensor"),
        P("section", None, None, None),
        P("section", None, None, None),
    )
    return jax.shard_map(
        per_device, mesh=mesh, in_specs=in_specs, out_specs=out_specs, check_vma=False
    )
```

```python
import jax
import jax.numpy as jnp
from jax import lax
from jax.experimental import pallas as pl
from jax.experimental.pallas import tpu as pltpu
from jax.sharding import PartitionSpec as P

TILES = 4
ADAPTER_SCALE = 2.0
EPS = 1e-05
PLANE = ("section", "tensor")
NZ = 8


def plane_pairs(route):
    def index(x, z, core):
        return (((x // 2) * NZ + z) * 2 + core) * 2 + x % 2

    return [
        (index(x, z, core), index(*route(x, z, core)))
        for x in range(4)
        for z in range(NZ)
        for core in range(2)
    ]


SIBLING = plane_pairs(lambda x, z, core: (x, z, 1 - core))
SHIFTS = (4, 3, 5, 2, 6, 1, 7)
ALONG = {
    k: plane_pairs(lambda x, z, core, k=k: (x, (z + k) % NZ, core)) for k in SHIFTS
}
NEAR = plane_pairs(lambda x, z, core: (x ^ 1 if core == 0 else 3 - x, z, core))
FAR = plane_pairs(lambda x, z, core: (3 - x if core == 0 else x ^ 1, z, core))
TENSOR_SWAP = [(0, 1), (1, 0)]
DP_NEAR = [(i, i ^ 1) for i in range(4)]
DP_FAR = [(i, 3 - i) for i in range(4)]
DP_ACROSS = [(i, i ^ 2) for i in range(4)]


def move(block, pairs):
    return lax.ppermute(block, PLANE, pairs)


def after(value, *others):
    return lax.optimization_barrier((value, *others))[0]


NT = (((1,), (1,)), ((), ()))
TN = (((0,), (0,)), ((), ()))
F32, LOW = jnp.float32, jnp.bfloat16
ROOM = pltpu.CompilerParams(vmem_limit_bytes=20 * 1024 * 1024)
SCALAR = pl.BlockSpec(memory_space=pltpu.SMEM)
VECTOR = pl.BlockSpec(memory_space=pltpu.VMEM)
CHUNK = 1024


def dot(first, second, dims=(((1,), (0,)), ((), ()))):
    return lax.dot_general(first, second, dims, preferred_element_type=F32)


def cost(flops, moved):
    return pl.CostEstimate(flops=int(flops) // 1000, bytes_accessed=int(moved) // 1000, transcendentals=0)


def pair_kernel(gain_ref, query_ref, context_ref, pair_ref):
    gain = gain_ref[0:1, :].astype(F32)
    head = gain.shape[1]
    text = query_ref.shape[1]
    kv_heads = pair_ref.shape[0]
    group = query_ref.shape[2] // (head * kv_heads)
    for kv in range(kv_heads):
        for member in range(group):
            columns = slice((kv * group + member) * head, (kv * group + member + 1) * head)
            rows = slice(member * text, (member + 1) * text)
            query = query_ref[0, :, columns].astype(F32)
            scale = lax.rsqrt(jnp.mean(query * query, axis=-1, keepdims=True) + EPS)
            pair_ref[kv, rows, 0:head] = (query * scale * gain).astype(LOW)
            pair_ref[kv, rows, head : 2 * head] = context_ref[0, :, columns]


def pair_queries(queries, context, gains, kv_heads):
    batches, text, wide = queries.shape
    head = gains.shape[1]
    rows = wide // (kv_heads * head) * text
    block = pl.BlockSpec((1, text, wide), lambda b: (b, 0, 0))
    return pl.pallas_call(
        pair_kernel,
        out_shape=jax.ShapeDtypeStruct((batches * kv_heads, rows, 2 * head), LOW),
        grid=(batches,),
        in_specs=[pl.BlockSpec(gains.shape, lambda b: (0, 0)), block, block],
        out_specs=pl.BlockSpec((kv_heads, rows, 2 * head), lambda b: (b, 0, 0)),
        compiler_params=ROOM,
        cost_estimate=cost(2e8, 4 * queries.size * 2),
        name="pair_queries",
    )(gains, queries, context)


def flatten_kernel(from_ref, to_ref):
    outer, inner, _ = from_ref.shape
    for i in range(outer):
        to_ref[i * inner : (i + 1) * inner, :] = from_ref[i]


def flatten(array):
    outer, inner, wide = array.shape
    return pl.pallas_call(
        flatten_kernel,
        out_shape=jax.ShapeDtypeStruct((outer * inner, wide), array.dtype),
        in_specs=[VECTOR],
        out_specs=VECTOR,
        compiler_params=ROOM,
        cost_estimate=cost(0, 4 * array.size),
        name="flatten",
    )(array)


def total_kernel(own_ref, *refs):
    *arrived, to_ref = refs
    rows = own_ref[...]
    for ref in arrived:
        rows += ref[...].astype(F32)
    outer, inner, _ = to_ref.shape
    for i in range(outer):
        to_ref[i] = rows[i * inner : (i + 1) * inner]


def total(own, arrived, shape):
    return pl.pallas_call(
        total_kernel,
        out_shape=jax.ShapeDtypeStruct(shape, F32),
        in_specs=[VECTOR] * (1 + len(arrived)),
        out_specs=VECTOR,
        compiler_params=ROOM,
        cost_estimate=cost(own.size * len(arrived), 2 * own.size * len(arrived)),
        name="total",
    )(own, *arrived)


def hold_kernel(ready_ref, from_ref, to_ref, semaphore):
    copy = pltpu.make_async_copy(from_ref, to_ref, semaphore)
    copy.start()
    copy.wait()


def hold(array, ready):
    return pl.pallas_call(
        hold_kernel,
        out_shape=pltpu.VMEM(array.shape, array.dtype),
        in_specs=[pl.BlockSpec(memory_space=pl.ANY), pl.BlockSpec(memory_space=pltpu.HBM)],
        scratch_shapes=[pltpu.SemaphoreType.DMA],
        out_specs=VECTOR,
        compiler_params=ROOM,
        cost_estimate=cost(0, 2 * array.size),
        name="hold",
    )(ready, array)


def project_kernel(which_ref, *refs):
    *row_refs, w_ref, a_ref, y_ref, r_ref = refs
    half = row_refs[0].shape[1]
    totals = [None, None, None]
    for i in range(half // CHUNK):
        rows = jnp.concatenate([ref[:, i * CHUNK : (i + 1) * CHUNK] for ref in row_refs])
        place = pl.ds(pl.multiple_of(which_ref[0] * half + i * CHUNK, CHUNK), CHUNK)
        maps = a_ref[:, :, place].reshape(-1, CHUNK)
        terms = [dot(rows, w_ref[part, place, :]) for part in range(2)] + [dot(rows, maps, NT)]
        totals = [new if old is None else old + new for old, new in zip(totals, terms)]
    y_ref[0] = totals[0]
    y_ref[1] = totals[1]
    r_ref[...] = totals[2]


def project(blocks, weights, down_maps, which):
    count, half = len(blocks) * blocks[0].shape[0], blocks[0].shape[1]
    width, ranks = weights.shape[2], 2 * down_maps.shape[1]
    return pl.pallas_call(
        project_kernel,
        out_shape=[
            jax.ShapeDtypeStruct((2, count, width), F32),
            jax.ShapeDtypeStruct((count, ranks), F32),
        ],
        in_specs=[SCALAR] + [VECTOR] * (len(blocks) + 2),
        out_specs=[VECTOR] * 2,
        compiler_params=ROOM,
        cost_estimate=cost(4 * 192 * half * width, 4 * half * width + 2 * count * half),
        name="project",
    )(which, *blocks, weights, down_maps)


def attention_kernel(
    count_ref, start_ref, y0, y1, y2, r0, r1, r2, own_map, other_map, own_back, other_back,
    up_diagonal, gains_ref, pair_ref, g_own, m_own, g_other, m_other, middle_ref, up_ref, grad_ref,
):
    width = y0.shape[2]
    head = gains_ref.shape[1]
    kv_heads = width // head
    batches = pair_ref.shape[0] // kv_heads
    tokens = own_map.shape[0] // batches
    ranks = r0.shape[1]
    text = 128
    scale = head ** (-0.5)

    def ordered(own, other):
        total = None
        for mapping, values in ((own_map, own), (other_map, other)):
            high = values.astype(LOW)
            rest = values - high.astype(F32)
            middle = rest.astype(LOW)
            lowest = (rest - middle.astype(F32)).astype(LOW)
            for term in (lowest, middle, high):
                moved = dot(mapping[...], term)
                total = moved if total is None else total + moved
        return total

    reduced = ordered(jnp.concatenate([r0[...], r1[...]]), r2[...]).astype(LOW)
    adapted = ADAPTER_SCALE * dot(reduced, up_diagonal[...])
    raw = [
        ordered(jnp.concatenate([y0[part], y1[part]]), y2[part])
        + adapted[:, part * width : (part + 1) * width]
        for part in range(2)
    ]
    gain = gains_ref[1:2, :].astype(F32)
    lane = lax.broadcasted_iota(jnp.int32, (1, pair_ref.shape[1]), 1) % text
    token = lax.broadcasted_iota(jnp.int32, (tokens, 1), 0)
    for kv in range(kv_heads):
        columns = slice(kv * head, (kv + 1) * head)
        key_raw = raw[0][:, columns]
        key_scale = lax.rsqrt(jnp.mean(key_raw * key_raw, axis=-1, keepdims=True) + EPS)
        unit = key_raw * key_scale
        keys = (unit * gain).astype(LOW)
        values = raw[1][:, columns].astype(LOW)
        for batch in range(batches):
            rows = slice(batch * tokens, (batch + 1) * tokens)
            none = jnp.zeros((tokens, head), LOW)
            both = jnp.concatenate(
                [
                    jnp.concatenate([keys[rows], none], 1),
                    jnp.concatenate([none, values[rows]], 1),
                ]
            )
            pair = pair_ref[batch * kv_heads + kv]
            scores = dot(both, pair, NT)
            allowed = token < count_ref[batch] * (tokens // TILES)
            live = (lane >= start_ref[batch]).astype(F32)
            weighted = jnp.where(allowed, jnp.exp(scores[:tokens] * scale), 0.0)
            attention = weighted * (live / jnp.sum(weighted, axis=0, keepdims=True))
            probs = scores[tokens:]
            mean = jnp.sum(attention * probs, axis=0, keepdims=True)
            grads = attention * (probs - mean) * scale
            out = dot(jnp.concatenate([grads.astype(LOW), attention.astype(LOW)]), pair)
            gained = out[:tokens, :head] * gain
            inner = jnp.mean(gained * unit[rows], axis=-1, keepdims=True)
            grad_ref[rows, columns] = (key_scale[rows] * (gained - unit[rows] * inner)).astype(LOW)
            grad_ref[rows, width + kv * head : width + (kv + 1) * head] = out[
                tokens:, head:
            ].astype(LOW)
    grad = grad_ref[...]
    middle = dot(grad, up_diagonal[...], NT).astype(LOW)
    middle_ref[...] = (ADAPTER_SCALE * middle.astype(F32)).astype(LOW)
    up = ADAPTER_SCALE * dot(reduced, grad, TN)
    for part in range(2):
        half = slice(part * ranks // 2, (part + 1) * ranks // 2)
        up_ref[half, :] = up[half, part * width : (part + 1) * width]
    for back, g_ref, m_ref in ((own_back, g_own, m_own), (other_back, g_other, m_other)):
        g_ref[...] = dot(back[...], grad).astype(LOW)
        m_ref[...] = (ADAPTER_SCALE * dot(back[...], middle)).astype(LOW)


def attend(counts, starts, projected, maps, up_diagonal, gains, pair):
    (y0, r0), (y1, r1), (y2, r2) = projected
    rows, ranks, width = y2.shape[1], r0.shape[1], y0.shape[2]
    scalar = pl.BlockSpec(memory_space=pltpu.SMEM)
    vector = pl.BlockSpec(memory_space=pltpu.VMEM)
    return pl.pallas_call(
        attention_kernel,
        out_shape=[
            jax.ShapeDtypeStruct((rows, 2 * width), LOW),
            jax.ShapeDtypeStruct((rows, ranks), LOW),
            jax.ShapeDtypeStruct((rows, 2 * width), LOW),
            jax.ShapeDtypeStruct((rows, ranks), LOW),
            jax.ShapeDtypeStruct((rows, ranks), LOW),
            jax.ShapeDtypeStruct((ranks, width), F32),
        ],
        in_specs=[scalar, scalar] + [vector] * 13,
        out_specs=[vector] * 6,
        scratch_shapes=[pltpu.VMEM((rows, 2 * width), LOW)],
        compiler_params=ROOM,
        cost_estimate=cost(1e9, 2 * pair.size),
        name="attend",
    )(counts, starts, y0, y1, y2, r0, r1, r2, *maps, up_diagonal, gains, pair)


def feature_kernel(which_ref, g_ref, m_ref, w_ref, a_ref, *out_refs):
    width = w_ref.shape[2]
    cut, half = out_refs[0].shape
    for i in range(half // CHUNK):
        place = pl.ds(pl.multiple_of(which_ref[0] * half + i * CHUNK, CHUNK), CHUNK)
        total = dot(m_ref[...], a_ref[:, :, place].reshape(-1, CHUNK))
        for part in range(2):
            total += dot(g_ref[:, part * width : (part + 1) * width], w_ref[part, place, :], NT)
        for j, ref in enumerate(out_refs):
            ref[:, i * CHUNK : (i + 1) * CHUNK] = total[j * cut : (j + 1) * cut].astype(LOW)


def feature_grad(grad, middle, weights, down_maps, which):
    rows, wide = grad.shape
    half = weights.shape[1] // 2
    return pl.pallas_call(
        feature_kernel,
        out_shape=[jax.ShapeDtypeStruct((rows // 4, half), LOW)] * 4,
        in_specs=[SCALAR] + [VECTOR] * 4,
        out_specs=[VECTOR] * 4,
        compiler_params=ROOM,
        cost_estimate=cost(2 * rows * half * wide, 2 * half * (wide + rows)),
        name="feature_grad",
    )(which, grad, middle, weights, down_maps)


def down_kernel(back_ref, mine_ref, facing_ref, *refs):
    *row_refs, out_ref = refs
    rows = jnp.concatenate([ref[...] for ref in row_refs])
    ranks = mine_ref.shape[1]
    both = jnp.concatenate([mine_ref[...], facing_ref[...]], 1)
    parts = dot(dot(back_ref[...], both).astype(LOW), rows, TN)
    out_ref[...] = parts[:ranks] + parts[ranks:]


def down_grad(back, mine, facing, blocks):
    ranks, half = mine.shape[1], blocks[0].shape[1]
    return pl.pallas_call(
        down_kernel,
        out_shape=jax.ShapeDtypeStruct((ranks, half), F32),
        in_specs=[VECTOR] * (3 + len(blocks)),
        out_specs=VECTOR,
        compiler_params=ROOM,
        cost_estimate=cost(5e7, 2 * 200 * half),
        name="down_grad",
    )(back, mine, facing, *blocks)


def row_tokens(x_hi, z, core, x_lo):
    def base_rows(chain, x_high):
        rows = []
        for k in (*SHIFTS, 0):
            token = ((x_high * NZ + (z - k) % NZ) * 2 + chain) * 2
            for batch in range(3):
                rows += [batch * 64 + token, batch * 64 + token + 1]
        return jnp.stack(rows)

    own_half, other_half = [], []
    for chain in (core, 1 - core):
        own_half += [base_rows(chain, x_hi)]
        near = jnp.where(chain == 0, x_hi, 1 - x_hi)
        other_half += [base_rows(chain, near), base_rows(chain, 1 - near)]
    for chain in (core, 1 - core):
        own_half += [base_rows(chain, 1 - x_hi)]
    return jnp.concatenate(own_half), jnp.concatenate(other_half)


def per_device(
    queries,
    context_gradient,
    vision_feature_states,
    key_value_weight,
    adapter_down_maps,
    adapter_up_maps,
    norm_gain_pair,
    image_tile_count,
    text_start_position,
):
    weights, down_maps, gains = key_value_weight[0], adapter_down_maps[0], norm_gain_pair[0]
    section, side = lax.axis_index("section"), lax.axis_index("tensor")
    width, half = weights.shape[2], vision_feature_states.shape[2]
    ranks = 2 * down_maps.shape[1]
    here = side.reshape(1).astype(jnp.int32)
    opposite = 1 - here

    own = flatten(vision_feature_states)
    base = jnp.concatenate([move(own, ALONG[k]) for k in SHIFTS] + [own])
    first = move(base, NEAR)
    second = move(base, FAR)
    base_there = move(base, SIBLING)
    late_side = after(side, base_there)
    late_section = after(section, base)
    up_maps = lax.dynamic_slice_in_dim(adapter_up_maps[0], late_side * width, width, 2)
    up_diagonal = jnp.concatenate(
        [jnp.pad(up_maps[0], ((0, 0), (0, width))), jnp.pad(up_maps[1], ((0, 0), (width, 0)))]
    )
    own_token, other_token = row_tokens(
        late_section // 16, (late_section // 2) % NZ, late_section % 2, late_side
    )
    line = jnp.arange(own_token.shape[0])
    maps = [
        (line[:, None] == own_token[None]).astype(LOW),
        (line[:, None] == other_token[None]).astype(LOW),
        (own_token[:, None] == line[None]).astype(LOW),
        (other_token[:, None] == line[None]).astype(LOW),
    ]
    pair = pair_queries(
        after(queries[0], base), context_gradient[0], gains, width // gains.shape[1]
    )
    step_a = project([base, base_there], weights, down_maps, here)
    first = after(first, pair, *step_a, up_diagonal, *maps)
    weights = hold(weights, first)
    third = move(first, FAR)
    first_there = move(first, SIBLING)
    second_there = move(second, SIBLING)
    others = [first, second, first_there, second_there]
    step_b = project(others, weights, down_maps, opposite)
    third = after(third, *step_b)
    third_there = move(third, SIBLING)
    step_c = project([third, third_there], weights, down_maps, here)
    owns = [base, base_there, third, third_there]

    g_own, m_own, g_other, m_other, middle, up_part = attend(
        image_tile_count,
        text_start_position,
        (step_a, step_c, step_b),
        maps,
        up_diagonal,
        gains,
        pair,
    )

    middle_facing = lax.ppermute(middle, "tensor", TENSOR_SWAP)
    base, base_out, third, third_out = feature_grad(g_own, m_own, weights, down_maps, here)

    def add(mine, theirs):
        return mine.astype(F32) + theirs.astype(F32)

    third = add(third, move(third_out, SIBLING)).astype(LOW)
    third_in = move(third, FAR)
    first, second, first_out, second_out = feature_grad(
        after(g_other, third), m_other, weights, down_maps, opposite
    )
    second = add(second, move(second_out, SIBLING)).astype(LOW)
    first = add(first, move(first_out, SIBLING))
    base = add(base, move(base_out, SIBLING))
    second_in = move(second, FAR)
    down_own = down_grad(maps[2], middle, after(middle_facing, second), owns)
    sums = jnp.concatenate([down_own, up_part], 1).astype(LOW)
    near_sums, far_sums, across_sums = (
        lax.ppermute(sums, "dp", pairs) for pairs in (DP_NEAR, DP_FAR, DP_ACROSS)
    )
    first = (first + third_in.astype(F32)).astype(LOW)
    first_in = move(first, NEAR)
    base = base + second_in.astype(F32) + first_in.astype(F32)
    low_base = base.astype(LOW)
    count = own.shape[0]
    arrived = [
        move(low_base[i * count : (i + 1) * count], ALONG[NZ - k]) for i, k in enumerate(SHIFTS)
    ]
    sums = (add(sums, after(near_sums, *arrived[:3])) + add(far_sums, across_sums)).astype(LOW)
    facing = lax.ppermute(sums, "tensor", TENSOR_SWAP)
    own_grad = total(base[len(SHIFTS) * count :], arrived, vision_feature_states.shape)

    left = jnp.where(side == 0, sums, facing).astype(F32)
    right = jnp.where(side == 0, facing, sums).astype(F32)
    down_total = jnp.concatenate([left[:, :half], right[:, :half]], 1)
    up_total = jnp.concatenate([left[:, half:], right[:, half:]], 1)
    return (
        own_grad,
        down_total.reshape(1, 2, ranks // 2, 2 * half),
        up_total.reshape(1, 2, ranks // 2, 2 * width),
    )


def solution(mesh):
    in_specs = (
        P("section", "dp", None, "tensor"),
        P("section", "dp", None, "tensor"),
        P("dp", "section", "tensor"),
        P("section", None, None, "tensor"),
        P("section", None, None, None),
        P("section", None, None, None),
        P("section", None, None),
        P("dp"),
        P("dp"),
    )
    out_specs = (
        P("dp", "section", "tensor"),
        P("section", None, None, None),
        P("section", None, None, None),
    )
    return jax.shard_map(
        per_device, mesh=mesh, in_specs=in_specs, out_specs=out_specs, check_vma=False
    )
```

```python
import jax
import jax.numpy as jnp
import numpy as np
from jax import lax
from jax.experimental import pallas as pl
from jax.experimental.pallas import tpu as pltpu
from jax.sharding import PartitionSpec as P

TILES = 4
ADAPTER_SCALE = 2.0
EPS = 1e-05
PLANE = ("section", "tensor")
NZ = 8


def plane_pairs(route):
    def index(x, z, core):
        return (((x // 2) * NZ + z) * 2 + core) * 2 + x % 2

    return [
        (index(x, z, core), index(*route(x, z, core)))
        for x in range(4)
        for z in range(NZ)
        for core in range(2)
    ]


SIBLING = plane_pairs(lambda x, z, core: (x, z, 1 - core))
SHIFTS = (4, 3, 5, 2, 6, 1, 7)
ALONG = {
    k: plane_pairs(lambda x, z, core, k=k: (x, (z + k) % NZ, core)) for k in SHIFTS
}
NEAR = plane_pairs(lambda x, z, core: (x ^ 1 if core == 0 else 3 - x, z, core))
FAR = plane_pairs(lambda x, z, core: (3 - x if core == 0 else x ^ 1, z, core))
TENSOR_SWAP = [(0, 1), (1, 0)]
DP_NEAR = [(i, i ^ 1) for i in range(4)]
DP_FAR = [(i, 3 - i) for i in range(4)]


def move(block, pairs):
    return lax.ppermute(block, PLANE, pairs)


def after(value, *others):
    return lax.optimization_barrier((value, *others))[0]


NT = (((1,), (1,)), ((), ()))
TN = (((0,), (0,)), ((), ()))
F32, LOW = jnp.float32, jnp.bfloat16
ROOM = pltpu.CompilerParams(vmem_limit_bytes=20 * 1024 * 1024)
SCALAR = pl.BlockSpec(memory_space=pltpu.SMEM)
VECTOR = pl.BlockSpec(memory_space=pltpu.VMEM)
CHUNK = 1024


def dot(first, second, dims=(((1,), (0,)), ((), ()))):
    return lax.dot_general(first, second, dims, preferred_element_type=F32)


def cost(flops, moved):
    return pl.CostEstimate(flops=int(flops), bytes_accessed=int(moved), transcendentals=0)


def pair_kernel(ready_ref, gain_ref, query_ref, context_ref, pair_ref):
    gain = gain_ref[0:1, :].astype(F32)
    head = gain.shape[1]
    text = query_ref.shape[1]
    kv_heads = pair_ref.shape[0]
    group = query_ref.shape[2] // (head * kv_heads)
    for kv in range(kv_heads):
        for member in range(group):
            columns = slice((kv * group + member) * head, (kv * group + member + 1) * head)
            rows = slice(member * text, (member + 1) * text)
            query = query_ref[0, :, columns].astype(F32)
            scale = lax.rsqrt(jnp.mean(query * query, axis=-1, keepdims=True) + EPS)
            pair_ref[kv, rows, 0:head] = (query * scale * gain).astype(LOW)
            pair_ref[kv, rows, head : 2 * head] = context_ref[0, :, columns]


def pair_queries(ready, queries, context, gains, kv_heads):
    batches, text, wide = queries.shape
    head = gains.shape[1]
    rows = wide // (kv_heads * head) * text
    block = pl.BlockSpec((1, text, wide), lambda b: (b, 0, 0))
    return pl.pallas_call(
        pair_kernel,
        out_shape=jax.ShapeDtypeStruct((batches * kv_heads, rows, 2 * head), LOW),
        grid=(batches,),
        in_specs=[
            pl.BlockSpec(memory_space=pl.ANY),
            pl.BlockSpec(gains.shape, lambda b: (0, 0)),
            block,
            block,
        ],
        out_specs=pl.BlockSpec((kv_heads, rows, 2 * head), lambda b: (b, 0, 0)),
        compiler_params=ROOM,
        cost_estimate=cost(2e8, 4 * queries.size * 2),
        name="pair_queries",
    )(ready, gains, queries, context)


def flatten_kernel(from_ref, to_ref):
    outer, inner, _ = from_ref.shape
    for i in range(outer):
        to_ref[i * inner : (i + 1) * inner, :] = from_ref[i]


def flatten(array):
    outer, inner, wide = array.shape
    return pl.pallas_call(
        flatten_kernel,
        out_shape=jax.ShapeDtypeStruct((outer * inner, wide), array.dtype),
        in_specs=[VECTOR],
        out_specs=VECTOR,
        compiler_params=ROOM,
        cost_estimate=cost(0, 4 * array.size),
        name="flatten",
    )(array)


def total_kernel(own_ref, *refs):
    *arrived, to_ref = refs
    rows = own_ref[...]
    for ref in arrived:
        rows += ref[...].astype(F32)
    outer, inner, _ = to_ref.shape
    for i in range(outer):
        to_ref[i] = rows[i * inner : (i + 1) * inner]


def total(own, arrived, shape):
    return pl.pallas_call(
        total_kernel,
        out_shape=jax.ShapeDtypeStruct(shape, F32),
        in_specs=[VECTOR] * (1 + len(arrived)),
        out_specs=VECTOR,
        compiler_params=ROOM,
        cost_estimate=cost(own.size * len(arrived), 2 * own.size * len(arrived)),
        name="total",
    )(own, *arrived)


def hold_kernel(ready_ref, from_ref, to_ref, semaphore):
    copy = pltpu.make_async_copy(from_ref, to_ref, semaphore)
    copy.start()
    copy.wait()


def hold(array, ready):
    return pl.pallas_call(
        hold_kernel,
        out_shape=pltpu.VMEM(array.shape, array.dtype),
        in_specs=[pl.BlockSpec(memory_space=pl.ANY), pl.BlockSpec(memory_space=pltpu.HBM)],
        scratch_shapes=[pltpu.SemaphoreType.DMA],
        out_specs=VECTOR,
        compiler_params=ROOM,
        cost_estimate=cost(0, 2 * array.size),
        name="hold",
    )(ready, array)


def project_kernel(which_ref, *refs):
    *row_refs, w_ref, a_ref, y_ref, r_ref = refs
    half = row_refs[0].shape[1]
    totals = [None, None, None]
    for i in range(half // CHUNK):
        rows = jnp.concatenate([ref[:, i * CHUNK : (i + 1) * CHUNK] for ref in row_refs])
        place = pl.ds(pl.multiple_of(which_ref[0] * half + i * CHUNK, CHUNK), CHUNK)
        maps = a_ref[:, :, place].reshape(-1, CHUNK)
        terms = [dot(rows, w_ref[part, place, :]) for part in range(2)] + [dot(rows, maps, NT)]
        totals = [new if old is None else old + new for old, new in zip(totals, terms)]
    y_ref[0] = totals[0]
    y_ref[1] = totals[1]
    r_ref[...] = totals[2]


def project(blocks, weights, down_maps, which):
    count, half = len(blocks) * blocks[0].shape[0], blocks[0].shape[1]
    width, ranks = weights.shape[2], 2 * down_maps.shape[1]
    return pl.pallas_call(
        project_kernel,
        out_shape=[
            jax.ShapeDtypeStruct((2, count, width), F32),
            jax.ShapeDtypeStruct((count, ranks), F32),
        ],
        in_specs=[SCALAR] + [VECTOR] * (len(blocks) + 2),
        out_specs=[VECTOR] * 2,
        compiler_params=ROOM,
        cost_estimate=cost(4 * 192 * half * width, 4 * half * width + 2 * count * half),
        name="project",
    )(which, *blocks, weights, down_maps)


def attention_kernel(
    count_ref, start_ref, y0, y1, y2, r0, r1, r2, own_map, other_map, own_back, other_back,
    up_diagonal, gains_ref, pair_ref, g_own, m_own, g_other, m_other, up_ref, grad_ref,
):
    width = y0.shape[2]
    head = gains_ref.shape[1]
    kv_heads = width // head
    batches = pair_ref.shape[0] // kv_heads
    tokens = own_map.shape[0] // batches
    ranks = r0.shape[1]
    text = 128
    scale = head ** (-0.5)

    def ordered(own, other):
        total = None
        for mapping, values in ((own_map, own), (other_map, other)):
            high = values.astype(LOW)
            rest = values - high.astype(F32)
            middle = rest.astype(LOW)
            lowest = (rest - middle.astype(F32)).astype(LOW)
            for term in (lowest, middle, high):
                moved = dot(mapping[...], term)
                total = moved if total is None else total + moved
        return total

    reduced = ordered(jnp.concatenate([r0[...], r1[...]]), r2[...]).astype(LOW)
    adapted = ADAPTER_SCALE * dot(reduced, up_diagonal[...])
    raw = [
        ordered(jnp.concatenate([y0[part], y1[part]]), y2[part])
        + adapted[:, part * width : (part + 1) * width]
        for part in range(2)
    ]
    gain = gains_ref[1:2, :].astype(F32)
    lane = lax.broadcasted_iota(jnp.int32, (1, pair_ref.shape[1]), 1) % text
    token = lax.broadcasted_iota(jnp.int32, (tokens, 1), 0)
    for kv in range(kv_heads):
        columns = slice(kv * head, (kv + 1) * head)
        key_raw = raw[0][:, columns]
        key_scale = lax.rsqrt(jnp.mean(key_raw * key_raw, axis=-1, keepdims=True) + EPS)
        unit = key_raw * key_scale
        keys = (unit * gain).astype(LOW)
        values = raw[1][:, columns].astype(LOW)
        for batch in range(batches):
            rows = slice(batch * tokens, (batch + 1) * tokens)
            none = jnp.zeros((tokens, head), LOW)
            both = jnp.concatenate(
                [
                    jnp.concatenate([keys[rows], none], 1),
                    jnp.concatenate([none, values[rows]], 1),
                ]
            )
            pair = pair_ref[batch * kv_heads + kv]
            scores = dot(both, pair, NT)
            allowed = token < count_ref[batch] * (tokens // TILES)
            live = (lane >= start_ref[batch]).astype(F32)
            weighted = jnp.where(allowed, jnp.exp(scores[:tokens] * scale), 0.0)
            attention = weighted * (live / jnp.sum(weighted, axis=0, keepdims=True))
            probs = scores[tokens:]
            mean = jnp.sum(attention * probs, axis=0, keepdims=True)
            grads = attention * (probs - mean) * scale
            out = dot(jnp.concatenate([grads.astype(LOW), attention.astype(LOW)]), pair)
            gained = out[:tokens, :head] * gain
            inner = jnp.mean(gained * unit[rows], axis=-1, keepdims=True)
            grad_ref[rows, columns] = (key_scale[rows] * (gained - unit[rows] * inner)).astype(LOW)
            grad_ref[rows, width + kv * head : width + (kv + 1) * head] = out[
                tokens:, head:
            ].astype(LOW)
    grad = grad_ref[...]
    middle = dot(grad, up_diagonal[...], NT).astype(LOW)
    up = ADAPTER_SCALE * dot(reduced, grad, TN)
    for part in range(2):
        half = slice(part * ranks // 2, (part + 1) * ranks // 2)
        up_ref[half, :] = up[half, part * width : (part + 1) * width]
    for back, g_ref, m_ref in ((own_back, g_own, m_own), (other_back, g_other, m_other)):
        g_ref[...] = dot(back[...], grad).astype(LOW)
        m_ref[...] = (ADAPTER_SCALE * dot(back[...], middle)).astype(LOW)


def attend(counts, starts, projected, maps, up_diagonal, gains, pair):
    (y0, r0), (y1, r1), (y2, r2) = projected
    rows, ranks, width = y2.shape[1], r0.shape[1], y0.shape[2]
    scalar = pl.BlockSpec(memory_space=pltpu.SMEM)
    vector = pl.BlockSpec(memory_space=pltpu.VMEM)
    return pl.pallas_call(
        attention_kernel,
        out_shape=[
            jax.ShapeDtypeStruct((rows, 2 * width), LOW),
            jax.ShapeDtypeStruct((rows, ranks), LOW),
            jax.ShapeDtypeStruct((rows, 2 * width), LOW),
            jax.ShapeDtypeStruct((rows, ranks), LOW),
            jax.ShapeDtypeStruct((ranks, width), F32),
        ],
        in_specs=[scalar, scalar] + [vector] * 13,
        out_specs=[vector] * 5,
        scratch_shapes=[pltpu.VMEM((rows, 2 * width), LOW)],
        compiler_params=ROOM,
        cost_estimate=cost(1e9, 2 * pair.size),
        name="attend",
    )(counts, starts, y0, y1, y2, r0, r1, r2, *maps, up_diagonal, gains, pair)


def feature_kernel(which_ref, g_ref, m_ref, w_ref, a_ref, *out_refs):
    width = w_ref.shape[2]
    cut, half = out_refs[0].shape
    for i in range(half // CHUNK):
        place = pl.ds(pl.multiple_of(which_ref[0] * half + i * CHUNK, CHUNK), CHUNK)
        total = dot(m_ref[...], a_ref[:, :, place].reshape(-1, CHUNK))
        for part in range(2):
            total += dot(g_ref[:, part * width : (part + 1) * width], w_ref[part, place, :], NT)
        for j, ref in enumerate(out_refs):
            ref[:, i * CHUNK : (i + 1) * CHUNK] = total[j * cut : (j + 1) * cut].astype(LOW)


def feature_grad(grad, middle, weights, down_maps, which):
    rows, wide = grad.shape
    half = weights.shape[1] // 2
    return pl.pallas_call(
        feature_kernel,
        out_shape=[jax.ShapeDtypeStruct((rows // 4, half), LOW)] * 4,
        in_specs=[SCALAR] + [VECTOR] * 4,
        out_specs=[VECTOR] * 4,
        compiler_params=ROOM,
        cost_estimate=cost(2 * rows * half * wide, 2 * half * (wide + rows)),
        name="feature_grad",
    )(which, grad, middle, weights, down_maps)


def down_kernel(m_ref, *refs):
    *row_refs, out_ref = refs
    rows = jnp.concatenate([ref[...] for ref in row_refs])
    out_ref[...] = dot(m_ref[...], rows, TN).astype(out_ref.dtype)


def down_grad(middle, blocks, dtype):
    half = blocks[0].shape[1]
    return pl.pallas_call(
        down_kernel,
        out_shape=jax.ShapeDtypeStruct((middle.shape[1], half), dtype),
        in_specs=[VECTOR] * (1 + len(blocks)),
        out_specs=VECTOR,
        compiler_params=ROOM,
        cost_estimate=cost(5e7, 2 * 200 * half),
        name="down_grad",
    )(middle, *blocks)


def row_tokens(x_hi, z, core):
    row = np.arange(192)
    shift = np.array((*SHIFTS, 0))[row % 48 // 6]
    place = row % 6 // 2 * 64 + row % 2

    def rows(theirs, flip):
        chain = jnp.where(theirs, 1 - core, core)
        x_high = jnp.where(flip(chain), 1 - x_hi, x_hi)
        return place + ((x_high * NZ + (z - shift + NZ) % NZ) * 2 + chain) * 2

    own = rows(row // 48 % 2 == 1, lambda chain: row // 96 == 1)
    other = rows(row // 96 == 1, lambda chain: (row // 48 % 2) != chain)
    return own, other


def per_device(
    queries,
    context_gradient,
    vision_feature_states,
    key_value_weight,
    adapter_down_maps,
    adapter_up_maps,
    norm_gain_pair,
    image_tile_count,
    text_start_position,
):
    weights, down_maps, gains = key_value_weight[0], adapter_down_maps[0], norm_gain_pair[0]
    section, side = lax.axis_index("section"), lax.axis_index("tensor")
    width, half = weights.shape[2], vision_feature_states.shape[2]
    ranks = 2 * down_maps.shape[1]
    here = side.reshape(1).astype(jnp.int32)
    opposite = 1 - here

    own = flatten(vision_feature_states)
    base = jnp.concatenate([move(own, ALONG[k]) for k in SHIFTS] + [own])
    first = move(base, NEAR)
    second = move(base, FAR)
    base_there = move(base, SIBLING)
    late_side = after(side, base)
    late_section = after(section, base)
    up_maps = lax.dynamic_slice_in_dim(adapter_up_maps[0], late_side * width, width, 2)
    up_diagonal = jnp.concatenate(
        [jnp.pad(up_maps[0], ((0, 0), (0, width))), jnp.pad(up_maps[1], ((0, 0), (width, 0)))]
    )
    own_token, other_token = row_tokens(
        late_section // 16, (late_section // 2) % NZ, late_section % 2
    )
    line = jnp.arange(own_token.shape[0])
    maps = [
        (line[:, None] == own_token[None]).astype(LOW),
        (line[:, None] == other_token[None]).astype(LOW),
        (own_token[:, None] == line[None]).astype(LOW),
        (other_token[:, None] == line[None]).astype(LOW),
    ]
    pair = pair_queries(
        base, queries[0], context_gradient[0], gains, width // gains.shape[1]
    )
    weights = hold(weights, after(pair, up_diagonal, *maps))
    first = after(first, weights)
    step_a = project([base, base_there], weights, down_maps, here)
    third = move(first, FAR)
    first_there = move(first, SIBLING)
    second_there = move(second, SIBLING)
    others = [first, second, first_there, second_there]
    step_b = project(others, weights, down_maps, opposite)
    third = after(third, *step_a, *step_b)
    third_there = move(third, SIBLING)
    step_c = project([third, third_there], weights, down_maps, here)
    owns = [base, base_there, third, third_there]

    g_own, m_own, g_other, m_other, up_part = attend(
        image_tile_count,
        text_start_position,
        (step_a, step_c, step_b),
        maps,
        up_diagonal,
        gains,
        pair,
    )

    down_other = down_grad(m_other, others, LOW)
    down_facing = lax.ppermute(down_other, "tensor", TENSOR_SWAP)
    base, base_out, third, third_out = feature_grad(
        after(g_own, down_other), m_own, weights, down_maps, here
    )
    down_own = down_grad(m_own, owns, F32)

    def add(mine, theirs):
        return mine.astype(F32) + theirs.astype(F32)

    third = add(third, move(third_out, SIBLING)).astype(LOW)
    third_in = move(third, FAR)
    first, second, first_out, second_out = feature_grad(
        after(g_other, third, down_own), m_other, weights, down_maps, opposite
    )
    second = add(second, move(second_out, SIBLING)).astype(LOW)
    first = add(first, move(first_out, SIBLING))
    base = add(base, move(base_out, SIBLING))
    sums = jnp.concatenate(
        [down_own + after(down_facing, first_out).astype(F32), up_part], 1
    ).astype(LOW)
    near_sums = lax.ppermute(sums, "dp", DP_NEAR)
    second_in = move(second, FAR)
    first = (first + third_in.astype(F32)).astype(LOW)
    first_in = move(first, NEAR)
    sums = add(sums, after(near_sums, second_in, first)).astype(LOW)
    far_sums = lax.ppermute(sums, "dp", DP_FAR)
    base = base + second_in.astype(F32) + first_in.astype(F32)
    low_base = base.astype(LOW)
    sums = add(sums, after(far_sums, low_base)).astype(LOW)
    low_base = after(low_base, sums)
    facing = lax.ppermute(sums, "tensor", TENSOR_SWAP)
    count = own.shape[0]
    arrived = [
        move(low_base[i * count : (i + 1) * count], ALONG[NZ - k]) for i, k in enumerate(SHIFTS)
    ]
    own_grad = total(base[len(SHIFTS) * count :], arrived, vision_feature_states.shape)

    left = jnp.where(side == 0, sums, facing).astype(F32)
    right = jnp.where(side == 0, facing, sums).astype(F32)
    down_total = jnp.concatenate([left[:, :half], right[:, :half]], 1)
    up_total = jnp.concatenate([left[:, half:], right[:, half:]], 1)
    return (
        own_grad,
        down_total.reshape(1, 2, ranks // 2, 2 * half),
        up_total.reshape(1, 2, ranks // 2, 2 * width),
    )


def solution(mesh):
    in_specs = (
        P("section", "dp", None, "tensor"),
        P("section", "dp", None, "tensor"),
        P("dp", "section", "tensor"),
        P("section", None, None, "tensor"),
        P("section", None, None, None),
        P("section", None, None, None),
        P("section", None, None),
        P("dp"),
        P("dp"),
    )
    out_specs = (
        P("dp", "section", "tensor"),
        P("section", None, None, None),
        P("section", None, None, None),
    )
    return jax.shard_map(
        per_device, mesh=mesh, in_specs=in_specs, out_specs=out_specs, check_vma=False
    )
```

```python
import jax
import jax.numpy as jnp
from jax import lax
from jax.experimental import pallas as pl
from jax.experimental.pallas import tpu as pltpu
from jax.sharding import PartitionSpec as P

TILES = 4
ADAPTER_SCALE = 2.0
EPS = 1e-05
PLANE = ("section", "tensor")
NZ = 8


def plane_pairs(route):
    def index(x, z, core):
        return (((x // 2) * NZ + z) * 2 + core) * 2 + x % 2

    return [
        (index(x, z, core), index(*route(x, z, core)))
        for x in range(4)
        for z in range(NZ)
        for core in range(2)
    ]


SIBLING = plane_pairs(lambda x, z, core: (x, z, 1 - core))
SHIFTS = (4, 3, 5, 2, 6, 1, 7)
ALONG = {
    k: plane_pairs(lambda x, z, core, k=k: (x, (z + k) % NZ, core)) for k in SHIFTS
}
NEAR = plane_pairs(lambda x, z, core: (x ^ 1 if core == 0 else 3 - x, z, core))
FAR = plane_pairs(lambda x, z, core: (3 - x if core == 0 else x ^ 1, z, core))
TENSOR_SWAP = [(0, 1), (1, 0)]
DP_NEAR = [(i, i ^ 1) for i in range(4)]
DP_FAR = [(i, 3 - i) for i in range(4)]


def move(block, pairs):
    return lax.ppermute(block, PLANE, pairs)


def after(value, *others):
    return lax.optimization_barrier((value, *others))[0]


NT = (((1,), (1,)), ((), ()))
TN = (((0,), (0,)), ((), ()))
F32, LOW = jnp.float32, jnp.bfloat16
ROOM = pltpu.CompilerParams(vmem_limit_bytes=20 * 1024 * 1024)
SCALAR = pl.BlockSpec(memory_space=pltpu.SMEM)
VECTOR = pl.BlockSpec(memory_space=pltpu.VMEM)
CHUNK = 1024


def dot(first, second, dims=(((1,), (0,)), ((), ()))):
    return lax.dot_general(first, second, dims, preferred_element_type=F32)


def cost(flops, moved):
    return pl.CostEstimate(flops=int(flops), bytes_accessed=int(moved), transcendentals=0)


def pair_kernel(gain_ref, query_ref, context_ref, pair_ref):
    gain = gain_ref[0:1, :].astype(F32)
    head = gain.shape[1]
    text = query_ref.shape[1]
    kv_heads = pair_ref.shape[0]
    group = query_ref.shape[2] // (head * kv_heads)
    for kv in range(kv_heads):
        for member in range(group):
            columns = slice((kv * group + member) * head, (kv * group + member + 1) * head)
            rows = slice(member * text, (member + 1) * text)
            query = query_ref[0, :, columns].astype(F32)
            scale = lax.rsqrt(jnp.mean(query * query, axis=-1, keepdims=True) + EPS)
            pair_ref[kv, rows, 0:head] = (query * scale * gain).astype(LOW)
            pair_ref[kv, rows, head : 2 * head] = context_ref[0, :, columns]


def pair_queries(queries, context, gains, kv_heads):
    batches, text, wide = queries.shape
    head = gains.shape[1]
    rows = wide // (kv_heads * head) * text
    block = pl.BlockSpec((1, text, wide), lambda b: (b, 0, 0))
    return pl.pallas_call(
        pair_kernel,
        out_shape=jax.ShapeDtypeStruct((batches * kv_heads, rows, 2 * head), LOW),
        grid=(batches,),
        in_specs=[pl.BlockSpec(gains.shape, lambda b: (0, 0)), block, block],
        out_specs=pl.BlockSpec((kv_heads, rows, 2 * head), lambda b: (b, 0, 0)),
        compiler_params=ROOM,
        cost_estimate=cost(2e8, 4 * queries.size * 2),
        name="pair_queries",
    )(gains, queries, context)


def hold_kernel(ready_ref, from_ref, to_ref, semaphore):
    copy = pltpu.make_async_copy(from_ref, to_ref, semaphore)
    copy.start()
    copy.wait()


def hold(array, ready):
    return pl.pallas_call(
        hold_kernel,
        out_shape=pltpu.VMEM(array.shape, array.dtype),
        in_specs=[pl.BlockSpec(memory_space=pl.ANY), pl.BlockSpec(memory_space=pltpu.HBM)],
        scratch_shapes=[pltpu.SemaphoreType.DMA],
        out_specs=VECTOR,
        compiler_params=ROOM,
        cost_estimate=cost(0, 2 * array.size),
        name="hold",
    )(ready, array)


def finish_kernel(side_ref, mine_ref, facing_ref, down_ref, up_ref):
    half, width = down_ref.shape[1] // 2, up_ref.shape[1] // 2
    for ref, place in ((mine_ref, side_ref[0]), (facing_ref, 1 - side_ref[0])):
        columns = pl.ds(pl.multiple_of(place * half, half), half)
        down_ref[:, columns] = ref[:, :half].astype(F32)
        columns = pl.ds(pl.multiple_of(place * width, width), width)
        up_ref[:, columns] = ref[:, half:].astype(F32)


def finish(side, mine, facing, half):
    ranks, wide = mine.shape
    return pl.pallas_call(
        finish_kernel,
        out_shape=[
            jax.ShapeDtypeStruct((ranks, 2 * half), F32),
            jax.ShapeDtypeStruct((ranks, 2 * (wide - half)), F32),
        ],
        in_specs=[SCALAR, VECTOR, VECTOR],
        out_specs=[VECTOR] * 2,
        compiler_params=ROOM,
        cost_estimate=cost(0, 8 * mine.size),
        name="finish",
    )(side, mine, facing)


def project_kernel(which_ref, *refs):
    *row_refs, w_ref, a_ref, y_ref, r_ref = refs
    half = row_refs[0].shape[1]
    totals = [None, None, None]
    for i in range(half // CHUNK):
        rows = jnp.concatenate([ref[:, i * CHUNK : (i + 1) * CHUNK] for ref in row_refs])
        place = pl.ds(pl.multiple_of(which_ref[0] * half + i * CHUNK, CHUNK), CHUNK)
        maps = a_ref[:, :, place].reshape(-1, CHUNK)
        terms = [dot(rows, w_ref[part, place, :]) for part in range(2)] + [dot(rows, maps, NT)]
        totals = [new if old is None else old + new for old, new in zip(totals, terms)]
    y_ref[0] = totals[0]
    y_ref[1] = totals[1]
    r_ref[...] = totals[2]


def project(blocks, weights, down_maps, which):
    count, half = len(blocks) * blocks[0].shape[0], blocks[0].shape[1]
    width, ranks = weights.shape[2], 2 * down_maps.shape[1]
    return pl.pallas_call(
        project_kernel,
        out_shape=[
            jax.ShapeDtypeStruct((2, count, width), F32),
            jax.ShapeDtypeStruct((count, ranks), F32),
        ],
        in_specs=[SCALAR] + [VECTOR] * (len(blocks) + 2),
        out_specs=[VECTOR] * 2,
        compiler_params=ROOM,
        cost_estimate=cost(4 * 192 * half * width, 4 * half * width + 2 * count * half),
        name="project",
    )(which, *blocks, weights, down_maps)


def attention_kernel(
    count_ref, start_ref, y0, y1, y2, r0, r1, r2, own_map, other_map, own_back, other_back,
    up_diagonal, gains_ref, pair_ref, g_own, m_own, g_other, m_other, up_ref, grad_ref,
):
    width = y0.shape[2]
    head = gains_ref.shape[1]
    kv_heads = width // head
    batches = pair_ref.shape[0] // kv_heads
    tokens = own_map.shape[0] // batches
    ranks = r0.shape[1]
    text = 128
    scale = head ** (-0.5)

    def ordered(own, other):
        total = None
        for mapping, values in ((own_map, own), (other_map, other)):
            high = values.astype(LOW)
            rest = values - high.astype(F32)
            middle = rest.astype(LOW)
            lowest = (rest - middle.astype(F32)).astype(LOW)
            for term in (lowest, middle, high):
                moved = dot(mapping[...], term)
                total = moved if total is None else total + moved
        return total

    reduced = ordered(jnp.concatenate([r0[...], r1[...]]), r2[...]).astype(LOW)
    adapted = ADAPTER_SCALE * dot(reduced, up_diagonal[...])
    raw = [
        ordered(jnp.concatenate([y0[part], y1[part]]), y2[part])
        + adapted[:, part * width : (part + 1) * width]
        for part in range(2)
    ]
    gain = gains_ref[1:2, :].astype(F32)
    lane = lax.broadcasted_iota(jnp.int32, (1, pair_ref.shape[1]), 1) % text
    token = lax.broadcasted_iota(jnp.int32, (tokens, 1), 0)
    for kv in range(kv_heads):
        columns = slice(kv * head, (kv + 1) * head)
        key_raw = raw[0][:, columns]
        key_scale = lax.rsqrt(jnp.mean(key_raw * key_raw, axis=-1, keepdims=True) + EPS)
        unit = key_raw * key_scale
        keys = (unit * gain).astype(LOW)
        values = raw[1][:, columns].astype(LOW)
        for batch in range(batches):
            rows = slice(batch * tokens, (batch + 1) * tokens)
            none = jnp.zeros((tokens, head), LOW)
            both = jnp.concatenate(
                [
                    jnp.concatenate([keys[rows], none], 1),
                    jnp.concatenate([none, values[rows]], 1),
                ]
            )
            pair = pair_ref[batch * kv_heads + kv]
            scores = dot(both, pair, NT)
            allowed = token < count_ref[batch] * (tokens // TILES)
            live = (lane >= start_ref[batch]).astype(F32)
            weighted = jnp.where(allowed, jnp.exp(scores[:tokens] * scale), 0.0)
            attention = weighted * (live / jnp.sum(weighted, axis=0, keepdims=True))
            probs = scores[tokens:]
            mean = jnp.sum(attention * probs, axis=0, keepdims=True)
            grads = attention * (probs - mean) * scale
            out = dot(jnp.concatenate([grads.astype(LOW), attention.astype(LOW)]), pair)
            gained = out[:tokens, :head] * gain
            inner = jnp.mean(gained * unit[rows], axis=-1, keepdims=True)
            grad_ref[rows, columns] = (key_scale[rows] * (gained - unit[rows] * inner)).astype(LOW)
            grad_ref[rows, width + kv * head : width + (kv + 1) * head] = out[
                tokens:, head:
            ].astype(LOW)
    grad = grad_ref[...]
    middle = dot(grad, up_diagonal[...], NT).astype(LOW)
    up = ADAPTER_SCALE * dot(reduced, grad, TN)
    for part in range(2):
        half = slice(part * ranks // 2, (part + 1) * ranks // 2)
        up_ref[half, :] = up[half, part * width : (part + 1) * width]
    for back, g_ref, m_ref in ((own_back, g_own, m_own), (other_back, g_other, m_other)):
        g_ref[...] = dot(back[...], grad).astype(LOW)
        m_ref[...] = (ADAPTER_SCALE * dot(back[...], middle)).astype(LOW)


def attend(counts, starts, projected, maps, up_diagonal, gains, pair):
    (y0, r0), (y1, r1), (y2, r2) = projected
    rows, ranks, width = y2.shape[1], r0.shape[1], y0.shape[2]
    scalar = pl.BlockSpec(memory_space=pltpu.SMEM)
    vector = pl.BlockSpec(memory_space=pltpu.VMEM)
    return pl.pallas_call(
        attention_kernel,
        out_shape=[
            jax.ShapeDtypeStruct((rows, 2 * width), LOW),
            jax.ShapeDtypeStruct((rows, ranks), LOW),
            jax.ShapeDtypeStruct((rows, 2 * width), LOW),
            jax.ShapeDtypeStruct((rows, ranks), LOW),
            jax.ShapeDtypeStruct((ranks, width), F32),
        ],
        in_specs=[scalar, scalar] + [vector] * 13,
        out_specs=[vector] * 5,
        scratch_shapes=[pltpu.VMEM((rows, 2 * width), LOW)],
        compiler_params=ROOM,
        cost_estimate=cost(1e9, 2 * pair.size),
        name="attend",
    )(counts, starts, y0, y1, y2, r0, r1, r2, *maps, up_diagonal, gains, pair)


def feature_kernel(which_ref, g_ref, m_ref, w_ref, a_ref, *out_refs):
    width = w_ref.shape[2]
    cut, half = out_refs[0].shape
    for i in range(half // CHUNK):
        place = pl.ds(pl.multiple_of(which_ref[0] * half + i * CHUNK, CHUNK), CHUNK)
        total = dot(m_ref[...], a_ref[:, :, place].reshape(-1, CHUNK))
        for part in range(2):
            total += dot(g_ref[:, part * width : (part + 1) * width], w_ref[part, place, :], NT)
        for j, ref in enumerate(out_refs):
            ref[:, i * CHUNK : (i + 1) * CHUNK] = total[j * cut : (j + 1) * cut].astype(LOW)


def feature_grad(grad, middle, weights, down_maps, which):
    rows, wide = grad.shape
    half = weights.shape[1] // 2
    return pl.pallas_call(
        feature_kernel,
        out_shape=[jax.ShapeDtypeStruct((rows // 4, half), LOW)] * 4,
        in_specs=[SCALAR] + [VECTOR] * 4,
        out_specs=[VECTOR] * 4,
        compiler_params=ROOM,
        cost_estimate=cost(2 * rows * half * wide, 2 * half * (wide + rows)),
        name="feature_grad",
    )(which, grad, middle, weights, down_maps)


def down_kernel(m_ref, *refs):
    *row_refs, out_ref = refs
    rows = jnp.concatenate([ref[...] for ref in row_refs])
    out_ref[...] = dot(m_ref[...], rows, TN).astype(out_ref.dtype)


def down_grad(middle, blocks, dtype):
    half = blocks[0].shape[1]
    return pl.pallas_call(
        down_kernel,
        out_shape=jax.ShapeDtypeStruct((middle.shape[1], half), dtype),
        in_specs=[VECTOR] * (1 + len(blocks)),
        out_specs=VECTOR,
        compiler_params=ROOM,
        cost_estimate=cost(5e7, 2 * 200 * half),
        name="down_grad",
    )(middle, *blocks)


def row_tokens(x_hi, z, core, x_lo):
    def base_rows(chain, x_high):
        rows = []
        for k in (*SHIFTS, 0):
            token = ((x_high * NZ + (z - k) % NZ) * 2 + chain) * 2
            for batch in range(3):
                rows += [batch * 64 + token, batch * 64 + token + 1]
        return jnp.stack(rows)

    own_half, other_half = [], []
    for chain in (core, 1 - core):
        own_half += [base_rows(chain, x_hi)]
        near = jnp.where(chain == 0, x_hi, 1 - x_hi)
        other_half += [base_rows(chain, near), base_rows(chain, 1 - near)]
    for chain in (core, 1 - core):
        own_half += [base_rows(chain, 1 - x_hi)]
    return jnp.concatenate(own_half), jnp.concatenate(other_half)


def per_device(
    queries,
    context_gradient,
    vision_feature_states,
    key_value_weight,
    adapter_down_maps,
    adapter_up_maps,
    norm_gain_pair,
    image_tile_count,
    text_start_position,
):
    weights, down_maps, gains = key_value_weight[0], adapter_down_maps[0], norm_gain_pair[0]
    section, side = lax.axis_index("section"), lax.axis_index("tensor")
    width, half = weights.shape[2], vision_feature_states.shape[2]
    ranks = 2 * down_maps.shape[1]
    here = side.reshape(1).astype(jnp.int32)
    opposite = 1 - here

    own = vision_feature_states.reshape(-1, half)
    base = jnp.concatenate([move(own, ALONG[k]) for k in SHIFTS] + [own])
    first = move(base, NEAR)
    second = move(base, FAR)
    base_there = move(base, SIBLING)
    late_side = after(side, base)
    late_section = after(section, base)
    up_maps = lax.dynamic_slice_in_dim(adapter_up_maps[0], late_side * width, width, 2)
    up_diagonal = jnp.concatenate(
        [jnp.pad(up_maps[0], ((0, 0), (0, width))), jnp.pad(up_maps[1], ((0, 0), (width, 0)))]
    )
    own_token, other_token = row_tokens(
        late_section // 16, (late_section // 2) % NZ, late_section % 2, late_side
    )
    line = jnp.arange(own_token.shape[0])
    maps = [
        (line[:, None] == own_token[None]).astype(LOW),
        (line[:, None] == other_token[None]).astype(LOW),
        (own_token[:, None] == line[None]).astype(LOW),
        (other_token[:, None] == line[None]).astype(LOW),
    ]
    pair = pair_queries(
        after(queries[0], base), context_gradient[0], gains, width // gains.shape[1]
    )
    step_a = project([base, base_there], weights, down_maps, here)
    first = after(first, pair, *step_a, up_diagonal, *maps)
    weights = hold(weights, first)
    third = move(first, FAR)
    first_there = move(first, SIBLING)
    second_there = move(second, SIBLING)
    others = [first, second, first_there, second_there]
    step_b = project(others, weights, down_maps, opposite)
    third = after(third, *step_b)
    third_there = move(third, SIBLING)
    step_c = project([third, third_there], weights, down_maps, here)
    owns = [base, base_there, third, third_there]

    g_own, m_own, g_other, m_other, up_part = attend(
        image_tile_count,
        text_start_position,
        (step_a, step_c, step_b),
        maps,
        up_diagonal,
        gains,
        pair,
    )

    down_other = down_grad(m_other, others, LOW)
    down_facing = lax.ppermute(down_other, "tensor", TENSOR_SWAP)
    base, base_out, third, third_out = feature_grad(
        after(g_own, down_other), m_own, weights, down_maps, here
    )
    down_own = down_grad(m_own, owns, F32)

    def add(mine, theirs):
        return mine.astype(F32) + theirs.astype(F32)

    third = add(third, move(third_out, SIBLING)).astype(LOW)
    third_in = move(third, FAR)
    first, second, first_out, second_out = feature_grad(
        after(g_other, third, down_own), m_other, weights, down_maps, opposite
    )
    second = add(second, move(second_out, SIBLING)).astype(LOW)
    first = add(first, move(first_out, SIBLING))
    base = add(base, move(base_out, SIBLING))
    sums = jnp.concatenate(
        [down_own + after(down_facing, first_out).astype(F32), up_part], 1
    ).astype(LOW)
    near_sums = lax.ppermute(sums, "dp", DP_NEAR)
    second_in = move(second, FAR)
    first = (first + third_in.astype(F32)).astype(LOW)
    first_in = move(first, NEAR)
    sums = add(sums, after(near_sums, first)).astype(LOW)
    far_sums = lax.ppermute(sums, "dp", DP_FAR)
    base = base + second_in.astype(F32) + first_in.astype(F32)
    low_base = base.astype(LOW)
    sums = add(sums, after(far_sums, low_base)).astype(LOW)
    low_base = after(low_base, sums)
    facing = lax.ppermute(sums, "tensor", TENSOR_SWAP)
    count = own.shape[0]
    own_grad = base[len(SHIFTS) * count :]
    for i, k in enumerate(SHIFTS):
        own_grad += move(low_base[i * count : (i + 1) * count], ALONG[NZ - k]).astype(F32)

    down_total, up_total = finish(here, sums, facing, half)
    return (
        own_grad.reshape(vision_feature_states.shape),
        down_total.reshape(1, 2, ranks // 2, 2 * half),
        up_total.reshape(1, 2, ranks // 2, 2 * width),
    )


def solution(mesh):
    in_specs = (
        P("section", "dp", None, "tensor"),
        P("section", "dp", None, "tensor"),
        P("dp", "section", "tensor"),
        P("section", None, None, "tensor"),
        P("section", None, None, None),
        P("section", None, None, None),
        P("section", None, None),
        P("dp"),
        P("dp"),
    )
    out_specs = (
        P("dp", "section", "tensor"),
        P("section", None, None, None),
        P("section", None, None, None),
    )
    return jax.shard_map(
        per_device, mesh=mesh, in_specs=in_specs, out_specs=out_specs, check_vma=False
    )
```

```python
import jax
import jax.numpy as jnp
from jax import lax
from jax.experimental import pallas as pl
from jax.experimental.pallas import tpu as pltpu
from jax.sharding import PartitionSpec as P

TILES = 4
ADAPTER_SCALE = 2.0
EPS = 1e-05
PLANE = ("section", "tensor")
NZ = 8


def plane_pairs(route):
    def index(x, z, core):
        return (((x // 2) * NZ + z) * 2 + core) * 2 + x % 2

    return [
        (index(x, z, core), index(*route(x, z, core)))
        for x in range(4)
        for z in range(NZ)
        for core in range(2)
    ]


SIBLING = plane_pairs(lambda x, z, core: (x, z, 1 - core))
SHIFTS = (4, 3, 5, 2, 6, 1, 7)
ALONG = {
    k: plane_pairs(lambda x, z, core, k=k: (x, (z + k) % NZ, core)) for k in SHIFTS
}
NEAR = plane_pairs(lambda x, z, core: (x ^ 1 if core == 0 else 3 - x, z, core))
FAR = plane_pairs(lambda x, z, core: (3 - x if core == 0 else x ^ 1, z, core))
TENSOR_SWAP = [(0, 1), (1, 0)]
DP_NEAR = [(i, i ^ 1) for i in range(4)]
DP_FAR = [(i, 3 - i) for i in range(4)]


def move(block, pairs):
    return lax.ppermute(block, PLANE, pairs)


def after(value, *others):
    return lax.optimization_barrier((value, *others))[0]


NT = (((1,), (1,)), ((), ()))
TN = (((0,), (0,)), ((), ()))
F32, LOW = jnp.float32, jnp.bfloat16
ROOM = pltpu.CompilerParams(vmem_limit_bytes=20 * 1024 * 1024)
SCALAR = pl.BlockSpec(memory_space=pltpu.SMEM)
VECTOR = pl.BlockSpec(memory_space=pltpu.VMEM)
CHUNK = 1024


def dot(first, second, dims=(((1,), (0,)), ((), ()))):
    return lax.dot_general(first, second, dims, preferred_element_type=F32)


def cost(flops, moved):
    return pl.CostEstimate(flops=int(flops), bytes_accessed=int(moved), transcendentals=0)


def pair_kernel(gain_ref, query_ref, context_ref, pair_ref):
    gain = gain_ref[0:1, :].astype(F32)
    head = gain.shape[1]
    text = query_ref.shape[1]
    kv_heads = pair_ref.shape[0]
    group = query_ref.shape[2] // (head * kv_heads)
    for kv in range(kv_heads):
        for member in range(group):
            columns = slice((kv * group + member) * head, (kv * group + member + 1) * head)
            rows = slice(member * text, (member + 1) * text)
            query = query_ref[0, :, columns].astype(F32)
            scale = lax.rsqrt(jnp.mean(query * query, axis=-1, keepdims=True) + EPS)
            pair_ref[kv, rows, 0:head] = (query * scale * gain).astype(LOW)
            pair_ref[kv, rows, head : 2 * head] = context_ref[0, :, columns]


def pair_queries(queries, context, gains, kv_heads):
    batches, text, wide = queries.shape
    head = gains.shape[1]
    rows = wide // (kv_heads * head) * text
    block = pl.BlockSpec((1, text, wide), lambda b: (b, 0, 0))
    return pl.pallas_call(
        pair_kernel,
        out_shape=jax.ShapeDtypeStruct((batches * kv_heads, rows, 2 * head), LOW),
        grid=(batches,),
        in_specs=[pl.BlockSpec(gains.shape, lambda b: (0, 0)), block, block],
        out_specs=pl.BlockSpec((kv_heads, rows, 2 * head), lambda b: (b, 0, 0)),
        compiler_params=ROOM,
        cost_estimate=cost(2e8, 4 * queries.size * 2),
        name="pair_queries",
    )(gains, queries, context)


def hold_kernel(ready_ref, from_ref, to_ref, semaphore):
    copy = pltpu.make_async_copy(from_ref, to_ref, semaphore)
    copy.start()
    copy.wait()


def hold(array, ready):
    return pl.pallas_call(
        hold_kernel,
        out_shape=pltpu.VMEM(array.shape, array.dtype),
        in_specs=[pl.BlockSpec(memory_space=pl.ANY), pl.BlockSpec(memory_space=pltpu.HBM)],
        scratch_shapes=[pltpu.SemaphoreType.DMA],
        out_specs=VECTOR,
        compiler_params=ROOM,
        cost_estimate=cost(0, 2 * array.size),
        name="hold",
    )(ready, array)


def finish_kernel(side_ref, mine_ref, facing_ref, down_ref, up_ref):
    half, width = down_ref.shape[1] // 2, up_ref.shape[1] // 2
    for ref, place in ((mine_ref, side_ref[0]), (facing_ref, 1 - side_ref[0])):
        columns = pl.ds(pl.multiple_of(place * half, half), half)
        down_ref[:, columns] = ref[:, :half].astype(F32)
        columns = pl.ds(pl.multiple_of(place * width, width), width)
        up_ref[:, columns] = ref[:, half:].astype(F32)


def finish(side, mine, facing, half):
    ranks, wide = mine.shape
    return pl.pallas_call(
        finish_kernel,
        out_shape=[
            jax.ShapeDtypeStruct((ranks, 2 * half), F32),
            jax.ShapeDtypeStruct((ranks, 2 * (wide - half)), F32),
        ],
        in_specs=[SCALAR, VECTOR, VECTOR],
        out_specs=[VECTOR] * 2,
        compiler_params=ROOM,
        cost_estimate=cost(0, 8 * mine.size),
        name="finish",
    )(side, mine, facing)


def project_kernel(which_ref, *refs):
    *row_refs, w_ref, a_ref, y_ref, r_ref = refs
    half = row_refs[0].shape[1]
    totals = [None, None, None]
    for i in range(half // CHUNK):
        rows = jnp.concatenate([ref[:, i * CHUNK : (i + 1) * CHUNK] for ref in row_refs])
        place = pl.ds(pl.multiple_of(which_ref[0] * half + i * CHUNK, CHUNK), CHUNK)
        maps = a_ref[:, :, place].reshape(-1, CHUNK)
        terms = [dot(rows, w_ref[part, place, :]) for part in range(2)] + [dot(rows, maps, NT)]
        totals = [new if old is None else old + new for old, new in zip(totals, terms)]
    y_ref[0] = totals[0]
    y_ref[1] = totals[1]
    r_ref[...] = totals[2]


def project(blocks, weights, down_maps, which):
    count, half = len(blocks) * blocks[0].shape[0], blocks[0].shape[1]
    width, ranks = weights.shape[2], 2 * down_maps.shape[1]
    return pl.pallas_call(
        project_kernel,
        out_shape=[
            jax.ShapeDtypeStruct((2, count, width), F32),
            jax.ShapeDtypeStruct((count, ranks), F32),
        ],
        in_specs=[SCALAR] + [VECTOR] * (len(blocks) + 2),
        out_specs=[VECTOR] * 2,
        compiler_params=ROOM,
        cost_estimate=cost(4 * 192 * half * width, 4 * half * width + 2 * count * half),
        name="project",
    )(which, *blocks, weights, down_maps)


def attention_kernel(
    count_ref, start_ref, y0, y1, y2, r0, r1, r2, own_map, other_map, own_back, other_back,
    up_diagonal, gains_ref, pair_ref, g_own, m_own, g_other, m_other, middle_ref, up_ref, grad_ref,
):
    width = y0.shape[2]
    head = gains_ref.shape[1]
    kv_heads = width // head
    batches = pair_ref.shape[0] // kv_heads
    tokens = own_map.shape[0] // batches
    ranks = r0.shape[1]
    text = 128
    scale = head ** (-0.5)

    def ordered(own, other):
        total = None
        for mapping, values in ((own_map, own), (other_map, other)):
            high = values.astype(LOW)
            rest = values - high.astype(F32)
            middle = rest.astype(LOW)
            lowest = (rest - middle.astype(F32)).astype(LOW)
            for term in (lowest, middle, high):
                moved = dot(mapping[...], term)
                total = moved if total is None else total + moved
        return total

    reduced = ordered(jnp.concatenate([r0[...], r1[...]]), r2[...]).astype(LOW)
    adapted = ADAPTER_SCALE * dot(reduced, up_diagonal[...])
    raw = [
        ordered(jnp.concatenate([y0[part], y1[part]]), y2[part])
        + adapted[:, part * width : (part + 1) * width]
        for part in range(2)
    ]
    gain = gains_ref[1:2, :].astype(F32)
    lane = lax.broadcasted_iota(jnp.int32, (1, pair_ref.shape[1]), 1) % text
    token = lax.broadcasted_iota(jnp.int32, (tokens, 1), 0)
    for kv in range(kv_heads):
        columns = slice(kv * head, (kv + 1) * head)
        key_raw = raw[0][:, columns]
        key_scale = lax.rsqrt(jnp.mean(key_raw * key_raw, axis=-1, keepdims=True) + EPS)
        unit = key_raw * key_scale
        keys = (unit * gain).astype(LOW)
        values = raw[1][:, columns].astype(LOW)
        for batch in range(batches):
            rows = slice(batch * tokens, (batch + 1) * tokens)
            none = jnp.zeros((tokens, head), LOW)
            both = jnp.concatenate(
                [
                    jnp.concatenate([keys[rows], none], 1),
                    jnp.concatenate([none, values[rows]], 1),
                ]
            )
            pair = pair_ref[batch * kv_heads + kv]
            scores = dot(both, pair, NT)
            allowed = token < count_ref[batch] * (tokens // TILES)
            live = (lane >= start_ref[batch]).astype(F32)
            weighted = jnp.where(allowed, jnp.exp(scores[:tokens] * scale), 0.0)
            attention = weighted * (live / jnp.sum(weighted, axis=0, keepdims=True))
            probs = scores[tokens:]
            mean = jnp.sum(attention * probs, axis=0, keepdims=True)
            grads = attention * (probs - mean) * scale
            out = dot(jnp.concatenate([grads.astype(LOW), attention.astype(LOW)]), pair)
            gained = out[:tokens, :head] * gain
            inner = jnp.mean(gained * unit[rows], axis=-1, keepdims=True)
            grad_ref[rows, columns] = (key_scale[rows] * (gained - unit[rows] * inner)).astype(LOW)
            grad_ref[rows, width + kv * head : width + (kv + 1) * head] = out[
                tokens:, head:
            ].astype(LOW)
    grad = grad_ref[...]
    middle = dot(grad, up_diagonal[...], NT).astype(LOW)
    middle_ref[...] = (ADAPTER_SCALE * middle.astype(F32)).astype(LOW)
    up = ADAPTER_SCALE * dot(reduced, grad, TN)
    for part in range(2):
        half = slice(part * ranks // 2, (part + 1) * ranks // 2)
        up_ref[half, :] = up[half, part * width : (part + 1) * width]
    for back, g_ref, m_ref in ((own_back, g_own, m_own), (other_back, g_other, m_other)):
        g_ref[...] = dot(back[...], grad).astype(LOW)
        m_ref[...] = (ADAPTER_SCALE * dot(back[...], middle)).astype(LOW)


def attend(counts, starts, projected, maps, up_diagonal, gains, pair):
    (y0, r0), (y1, r1), (y2, r2) = projected
    rows, ranks, width = y2.shape[1], r0.shape[1], y0.shape[2]
    scalar = pl.BlockSpec(memory_space=pltpu.SMEM)
    vector = pl.BlockSpec(memory_space=pltpu.VMEM)
    return pl.pallas_call(
        attention_kernel,
        out_shape=[
            jax.ShapeDtypeStruct((rows, 2 * width), LOW),
            jax.ShapeDtypeStruct((rows, ranks), LOW),
            jax.ShapeDtypeStruct((rows, 2 * width), LOW),
            jax.ShapeDtypeStruct((rows, ranks), LOW),
            jax.ShapeDtypeStruct((rows, ranks), LOW),
            jax.ShapeDtypeStruct((ranks, width), F32),
        ],
        in_specs=[scalar, scalar] + [vector] * 13,
        out_specs=[vector] * 6,
        scratch_shapes=[pltpu.VMEM((rows, 2 * width), LOW)],
        compiler_params=ROOM,
        cost_estimate=cost(1e9, 2 * pair.size),
        name="attend",
    )(counts, starts, y0, y1, y2, r0, r1, r2, *maps, up_diagonal, gains, pair)


def feature_kernel(which_ref, g_ref, m_ref, w_ref, a_ref, *out_refs):
    width = w_ref.shape[2]
    cut, half = out_refs[0].shape
    for i in range(half // CHUNK):
        place = pl.ds(pl.multiple_of(which_ref[0] * half + i * CHUNK, CHUNK), CHUNK)
        total = dot(m_ref[...], a_ref[:, :, place].reshape(-1, CHUNK))
        for part in range(2):
            total += dot(g_ref[:, part * width : (part + 1) * width], w_ref[part, place, :], NT)
        for j, ref in enumerate(out_refs):
            ref[:, i * CHUNK : (i + 1) * CHUNK] = total[j * cut : (j + 1) * cut].astype(LOW)


def feature_grad(grad, middle, weights, down_maps, which):
    rows, wide = grad.shape
    half = weights.shape[1] // 2
    return pl.pallas_call(
        feature_kernel,
        out_shape=[jax.ShapeDtypeStruct((rows // 4, half), LOW)] * 4,
        in_specs=[SCALAR] + [VECTOR] * 4,
        out_specs=[VECTOR] * 4,
        compiler_params=ROOM,
        cost_estimate=cost(2 * rows * half * wide, 2 * half * (wide + rows)),
        name="feature_grad",
    )(which, grad, middle, weights, down_maps)


def down_kernel(back_ref, mine_ref, facing_ref, *refs):
    *row_refs, out_ref = refs
    rows = jnp.concatenate([ref[...] for ref in row_refs])
    ranks = mine_ref.shape[1]
    both = jnp.concatenate([mine_ref[...], facing_ref[...]], 1)
    parts = dot(dot(back_ref[...], both).astype(LOW), rows, TN)
    out_ref[...] = parts[:ranks] + parts[ranks:]


def down_grad(back, mine, facing, blocks):
    ranks, half = mine.shape[1], blocks[0].shape[1]
    return pl.pallas_call(
        down_kernel,
        out_shape=jax.ShapeDtypeStruct((ranks, half), F32),
        in_specs=[VECTOR] * (3 + len(blocks)),
        out_specs=VECTOR,
        compiler_params=ROOM,
        cost_estimate=cost(5e7, 2 * 200 * half),
        name="down_grad",
    )(back, mine, facing, *blocks)


def row_tokens(x_hi, z, core, x_lo):
    def base_rows(chain, x_high):
        rows = []
        for k in (*SHIFTS, 0):
            token = ((x_high * NZ + (z - k) % NZ) * 2 + chain) * 2
            for batch in range(3):
                rows += [batch * 64 + token, batch * 64 + token + 1]
        return jnp.stack(rows)

    own_half, other_half = [], []
    for chain in (core, 1 - core):
        own_half += [base_rows(chain, x_hi)]
        near = jnp.where(chain == 0, x_hi, 1 - x_hi)
        other_half += [base_rows(chain, near), base_rows(chain, 1 - near)]
    for chain in (core, 1 - core):
        own_half += [base_rows(chain, 1 - x_hi)]
    return jnp.concatenate(own_half), jnp.concatenate(other_half)


def per_device(
    queries,
    context_gradient,
    vision_feature_states,
    key_value_weight,
    adapter_down_maps,
    adapter_up_maps,
    norm_gain_pair,
    image_tile_count,
    text_start_position,
):
    weights, down_maps, gains = key_value_weight[0], adapter_down_maps[0], norm_gain_pair[0]
    section, side = lax.axis_index("section"), lax.axis_index("tensor")
    width, half = weights.shape[2], vision_feature_states.shape[2]
    ranks = 2 * down_maps.shape[1]
    here = side.reshape(1).astype(jnp.int32)
    opposite = 1 - here

    own = vision_feature_states.reshape(-1, half)
    base = jnp.concatenate([move(own, ALONG[k]) for k in SHIFTS] + [own])
    first = move(base, NEAR)
    second = move(base, FAR)
    base_there = move(base, SIBLING)
    late_side = after(side, base)
    late_section = after(section, base)
    up_maps = lax.dynamic_slice_in_dim(adapter_up_maps[0], late_side * width, width, 2)
    up_diagonal = jnp.concatenate(
        [jnp.pad(up_maps[0], ((0, 0), (0, width))), jnp.pad(up_maps[1], ((0, 0), (width, 0)))]
    )
    own_token, other_token = row_tokens(
        late_section // 16, (late_section // 2) % NZ, late_section % 2, late_side
    )
    line = jnp.arange(own_token.shape[0])
    maps = [
        (line[:, None] == own_token[None]).astype(LOW),
        (line[:, None] == other_token[None]).astype(LOW),
        (own_token[:, None] == line[None]).astype(LOW),
        (other_token[:, None] == line[None]).astype(LOW),
    ]
    pair = pair_queries(
        after(queries[0], base), context_gradient[0], gains, width // gains.shape[1]
    )
    step_a = project([base, base_there], weights, down_maps, here)
    first = after(first, pair, *step_a, up_diagonal, *maps)
    weights = hold(weights, first)
    third = move(first, FAR)
    first_there = move(first, SIBLING)
    second_there = move(second, SIBLING)
    others = [first, second, first_there, second_there]
    step_b = project(others, weights, down_maps, opposite)
    third = after(third, *step_b)
    third_there = move(third, SIBLING)
    step_c = project([third, third_there], weights, down_maps, here)
    owns = [base, base_there, third, third_there]

    g_own, m_own, g_other, m_other, middle, up_part = attend(
        image_tile_count,
        text_start_position,
        (step_a, step_c, step_b),
        maps,
        up_diagonal,
        gains,
        pair,
    )

    middle_facing = lax.ppermute(middle, "tensor", TENSOR_SWAP)
    base, base_out, third, third_out = feature_grad(g_own, m_own, weights, down_maps, here)

    def add(mine, theirs):
        return mine.astype(F32) + theirs.astype(F32)

    third = add(third, move(third_out, SIBLING)).astype(LOW)
    third_in = move(third, FAR)
    first, second, first_out, second_out = feature_grad(
        after(g_other, third), m_other, weights, down_maps, opposite
    )
    second = add(second, move(second_out, SIBLING)).astype(LOW)
    first = add(first, move(first_out, SIBLING))
    base = add(base, move(base_out, SIBLING))
    down_own = down_grad(maps[2], middle, after(middle_facing, first_out), owns)
    sums = jnp.concatenate([down_own, up_part], 1).astype(LOW)
    near_sums = lax.ppermute(sums, "dp", DP_NEAR)
    second_in = move(second, FAR)
    first = (first + third_in.astype(F32)).astype(LOW)
    first_in = move(first, NEAR)
    sums = add(sums, after(near_sums, first)).astype(LOW)
    far_sums = lax.ppermute(sums, "dp", DP_FAR)
    base = base + second_in.astype(F32) + first_in.astype(F32)
    low_base = base.astype(LOW)
    sums = add(sums, after(far_sums, low_base)).astype(LOW)
    low_base = after(low_base, sums)
    facing = lax.ppermute(sums, "tensor", TENSOR_SWAP)
    count = own.shape[0]
    own_grad = base[len(SHIFTS) * count :]
    for i, k in enumerate(SHIFTS):
        own_grad += move(low_base[i * count : (i + 1) * count], ALONG[NZ - k]).astype(F32)

    down_total, up_total = finish(here, sums, facing, half)
    return (
        own_grad.reshape(vision_feature_states.shape),
        down_total.reshape(1, 2, ranks // 2, 2 * half),
        up_total.reshape(1, 2, ranks // 2, 2 * width),
    )


def solution(mesh):
    in_specs = (
        P("section", "dp", None, "tensor"),
        P("section", "dp", None, "tensor"),
        P("dp", "section", "tensor"),
        P("section", None, None, "tensor"),
        P("section", None, None, None),
        P("section", None, None, None),
        P("section", None, None),
        P("dp"),
        P("dp"),
    )
    out_specs = (
        P("dp", "section", "tensor"),
        P("section", None, None, None),
        P("section", None, None, None),
    )
    return jax.shard_map(
        per_device, mesh=mesh, in_specs=in_specs, out_specs=out_specs, check_vma=False
    )
```

```python
import jax
import jax.numpy as jnp
from jax import lax
from jax.experimental import pallas as pl
from jax.experimental.pallas import tpu as pltpu
from jax.sharding import PartitionSpec as P

TILES = 4
ADAPTER_SCALE = 2.0
EPS = 1e-05
PLANE = ("section", "tensor")
NZ = 8


def plane_pairs(route):
    def index(x, z, core):
        return (((x // 2) * NZ + z) * 2 + core) * 2 + x % 2

    return [
        (index(x, z, core), index(*route(x, z, core)))
        for x in range(4)
        for z in range(NZ)
        for core in range(2)
    ]


SIBLING = plane_pairs(lambda x, z, core: (x, z, 1 - core))
SHIFTS = (4, 3, 5, 2, 6, 1, 7)
ALONG = {
    k: plane_pairs(lambda x, z, core, k=k: (x, (z + k) % NZ, core)) for k in SHIFTS
}
NEAR = plane_pairs(lambda x, z, core: (x ^ 1 if core == 0 else 3 - x, z, core))
FAR = plane_pairs(lambda x, z, core: (3 - x if core == 0 else x ^ 1, z, core))
TENSOR_SWAP = [(0, 1), (1, 0)]
DP_NEAR = [(i, i ^ 1) for i in range(4)]
DP_FAR = [(i, 3 - i) for i in range(4)]


def move(block, pairs):
    return lax.ppermute(block, PLANE, pairs)


def after(value, *others):
    return lax.optimization_barrier((value, *others))[0]


NT = (((1,), (1,)), ((), ()))
TN = (((0,), (0,)), ((), ()))
F32, LOW = jnp.float32, jnp.bfloat16
ROOM = pltpu.CompilerParams(vmem_limit_bytes=20 * 1024 * 1024)
SCALAR = pl.BlockSpec(memory_space=pltpu.SMEM)
VECTOR = pl.BlockSpec(memory_space=pltpu.VMEM)
CHUNK = 1024


def dot(first, second, dims=(((1,), (0,)), ((), ()))):
    return lax.dot_general(first, second, dims, preferred_element_type=F32)


def cost(flops, moved):
    return pl.CostEstimate(flops=int(flops), bytes_accessed=int(moved), transcendentals=0)


def pair_kernel(gain_ref, query_ref, context_ref, pair_ref):
    gain = gain_ref[0:1, :].astype(F32)
    head = gain.shape[1]
    text = query_ref.shape[1]
    kv_heads = pair_ref.shape[0]
    group = query_ref.shape[2] // (head * kv_heads)
    for kv in range(kv_heads):
        for member in range(group):
            columns = slice((kv * group + member) * head, (kv * group + member + 1) * head)
            rows = slice(member * text, (member + 1) * text)
            query = query_ref[0, :, columns].astype(F32)
            scale = lax.rsqrt(jnp.mean(query * query, axis=-1, keepdims=True) + EPS)
            pair_ref[kv, rows, 0:head] = (query * scale * gain).astype(LOW)
            pair_ref[kv, rows, head : 2 * head] = context_ref[0, :, columns]


def pair_queries(queries, context, gains, kv_heads):
    batches, text, wide = queries.shape
    head = gains.shape[1]
    rows = wide // (kv_heads * head) * text
    block = pl.BlockSpec((1, text, wide), lambda b: (b, 0, 0))
    return pl.pallas_call(
        pair_kernel,
        out_shape=jax.ShapeDtypeStruct((batches * kv_heads, rows, 2 * head), LOW),
        grid=(batches,),
        in_specs=[pl.BlockSpec(gains.shape, lambda b: (0, 0)), block, block],
        out_specs=pl.BlockSpec((kv_heads, rows, 2 * head), lambda b: (b, 0, 0)),
        compiler_params=ROOM,
        cost_estimate=cost(2e8, 4 * queries.size * 2),
        name="pair_queries",
    )(gains, queries, context)


def hold_kernel(ready_ref, from_ref, to_ref, semaphore):
    copy = pltpu.make_async_copy(from_ref, to_ref, semaphore)
    copy.start()
    copy.wait()


def hold(array, ready):
    return pl.pallas_call(
        hold_kernel,
        out_shape=pltpu.VMEM(array.shape, array.dtype),
        in_specs=[pl.BlockSpec(memory_space=pl.ANY), pl.BlockSpec(memory_space=pltpu.HBM)],
        scratch_shapes=[pltpu.SemaphoreType.DMA],
        out_specs=VECTOR,
        compiler_params=ROOM,
        cost_estimate=cost(0, 2 * array.size),
        name="hold",
    )(ready, array)


def finish_kernel(side_ref, mine_ref, facing_ref, down_ref, up_ref):
    half, width = down_ref.shape[1] // 2, up_ref.shape[1] // 2
    for ref, place in ((mine_ref, side_ref[0]), (facing_ref, 1 - side_ref[0])):
        columns = pl.ds(pl.multiple_of(place * half, half), half)
        down_ref[:, columns] = ref[:, :half].astype(F32)
        columns = pl.ds(pl.multiple_of(place * width, width), width)
        up_ref[:, columns] = ref[:, half:].astype(F32)


def finish(side, mine, facing, half):
    ranks, wide = mine.shape
    return pl.pallas_call(
        finish_kernel,
        out_shape=[
            jax.ShapeDtypeStruct((ranks, 2 * half), F32),
            jax.ShapeDtypeStruct((ranks, 2 * (wide - half)), F32),
        ],
        in_specs=[SCALAR, VECTOR, VECTOR],
        out_specs=[VECTOR] * 2,
        compiler_params=ROOM,
        cost_estimate=cost(0, 8 * mine.size),
        name="finish",
    )(side, mine, facing)


def project_kernel(which_ref, *refs):
    *row_refs, w_ref, a_ref, y_ref, r_ref = refs
    half = row_refs[0].shape[1]
    totals = [None, None, None]
    for i in range(half // CHUNK):
        rows = jnp.concatenate([ref[:, i * CHUNK : (i + 1) * CHUNK] for ref in row_refs])
        place = pl.ds(pl.multiple_of(which_ref[0] * half + i * CHUNK, CHUNK), CHUNK)
        maps = a_ref[:, :, place].reshape(-1, CHUNK)
        terms = [dot(rows, w_ref[part, place, :]) for part in range(2)] + [dot(rows, maps, NT)]
        totals = [new if old is None else old + new for old, new in zip(totals, terms)]
    y_ref[0] = totals[0]
    y_ref[1] = totals[1]
    r_ref[...] = totals[2]


def project(blocks, weights, down_maps, which):
    count, half = len(blocks) * blocks[0].shape[0], blocks[0].shape[1]
    width, ranks = weights.shape[2], 2 * down_maps.shape[1]
    return pl.pallas_call(
        project_kernel,
        out_shape=[
            jax.ShapeDtypeStruct((2, count, width), F32),
            jax.ShapeDtypeStruct((count, ranks), F32),
        ],
        in_specs=[SCALAR] + [VECTOR] * (len(blocks) + 2),
        out_specs=[VECTOR] * 2,
        compiler_params=ROOM,
        cost_estimate=cost(4 * 192 * half * width, 4 * half * width + 2 * count * half),
        name="project",
    )(which, *blocks, weights, down_maps)


def attention_kernel(
    count_ref, start_ref, y0, y1, y2, r0, r1, r2, own_map, other_map, own_back, other_back,
    up_diagonal, gains_ref, pair_ref, g_own, m_own, g_other, m_other, middle_ref, up_ref, grad_ref,
):
    width = y0.shape[2]
    head = gains_ref.shape[1]
    kv_heads = width // head
    batches = pair_ref.shape[0] // kv_heads
    tokens = own_map.shape[0] // batches
    ranks = r0.shape[1]
    text = 128
    scale = head ** (-0.5)

    def ordered(own, other):
        total = None
        for mapping, values in ((own_map, own), (other_map, other)):
            high = values.astype(LOW)
            rest = values - high.astype(F32)
            middle = rest.astype(LOW)
            lowest = (rest - middle.astype(F32)).astype(LOW)
            for term in (lowest, middle, high):
                moved = dot(mapping[...], term)
                total = moved if total is None else total + moved
        return total

    reduced = ordered(jnp.concatenate([r0[...], r1[...]]), r2[...]).astype(LOW)
    adapted = ADAPTER_SCALE * dot(reduced, up_diagonal[...])
    raw = [
        ordered(jnp.concatenate([y0[part], y1[part]]), y2[part])
        + adapted[:, part * width : (part + 1) * width]
        for part in range(2)
    ]
    gain = gains_ref[1:2, :].astype(F32)
    lane = lax.broadcasted_iota(jnp.int32, (1, pair_ref.shape[1]), 1) % text
    token = lax.broadcasted_iota(jnp.int32, (tokens, 1), 0)
    for kv in range(kv_heads):
        columns = slice(kv * head, (kv + 1) * head)
        key_raw = raw[0][:, columns]
        key_scale = lax.rsqrt(jnp.mean(key_raw * key_raw, axis=-1, keepdims=True) + EPS)
        unit = key_raw * key_scale
        keys = (unit * gain).astype(LOW)
        values = raw[1][:, columns].astype(LOW)
        for batch in range(batches):
            rows = slice(batch * tokens, (batch + 1) * tokens)
            none = jnp.zeros((tokens, head), LOW)
            both = jnp.concatenate(
                [
                    jnp.concatenate([keys[rows], none], 1),
                    jnp.concatenate([none, values[rows]], 1),
                ]
            )
            pair = pair_ref[batch * kv_heads + kv]
            scores = dot(both, pair, NT)
            allowed = token < count_ref[batch] * (tokens // TILES)
            live = (lane >= start_ref[batch]).astype(F32)
            weighted = jnp.where(allowed, jnp.exp(scores[:tokens] * scale), 0.0)
            attention = weighted * (live / jnp.sum(weighted, axis=0, keepdims=True))
            probs = scores[tokens:]
            mean = jnp.sum(attention * probs, axis=0, keepdims=True)
            grads = attention * (probs - mean) * scale
            out = dot(jnp.concatenate([grads.astype(LOW), attention.astype(LOW)]), pair)
            gained = out[:tokens, :head] * gain
            inner = jnp.mean(gained * unit[rows], axis=-1, keepdims=True)
            grad_ref[rows, columns] = (key_scale[rows] * (gained - unit[rows] * inner)).astype(LOW)
            grad_ref[rows, width + kv * head : width + (kv + 1) * head] = out[
                tokens:, head:
            ].astype(LOW)
    grad = grad_ref[...]
    middle = dot(grad, up_diagonal[...], NT).astype(LOW)
    middle_ref[...] = (ADAPTER_SCALE * middle.astype(F32)).astype(LOW)
    up = ADAPTER_SCALE * dot(reduced, grad, TN)
    for part in range(2):
        half = slice(part * ranks // 2, (part + 1) * ranks // 2)
        up_ref[half, :] = up[half, part * width : (part + 1) * width]
    for back, g_ref, m_ref in ((own_back, g_own, m_own), (other_back, g_other, m_other)):
        g_ref[...] = dot(back[...], grad).astype(LOW)
        m_ref[...] = (ADAPTER_SCALE * dot(back[...], middle)).astype(LOW)


def attend(counts, starts, projected, maps, up_diagonal, gains, pair):
    (y0, r0), (y1, r1), (y2, r2) = projected
    rows, ranks, width = y2.shape[1], r0.shape[1], y0.shape[2]
    scalar = pl.BlockSpec(memory_space=pltpu.SMEM)
    vector = pl.BlockSpec(memory_space=pltpu.VMEM)
    return pl.pallas_call(
        attention_kernel,
        out_shape=[
            jax.ShapeDtypeStruct((rows, 2 * width), LOW),
            jax.ShapeDtypeStruct((rows, ranks), LOW),
            jax.ShapeDtypeStruct((rows, 2 * width), LOW),
            jax.ShapeDtypeStruct((rows, ranks), LOW),
            jax.ShapeDtypeStruct((rows, ranks), LOW),
            jax.ShapeDtypeStruct((ranks, width), F32),
        ],
        in_specs=[scalar, scalar] + [vector] * 13,
        out_specs=[vector] * 6,
        scratch_shapes=[pltpu.VMEM((rows, 2 * width), LOW)],
        compiler_params=ROOM,
        cost_estimate=cost(1e9, 2 * pair.size),
        name="attend",
    )(counts, starts, y0, y1, y2, r0, r1, r2, *maps, up_diagonal, gains, pair)


def feature_kernel(which_ref, g_ref, m_ref, w_ref, a_ref, *out_refs):
    width = w_ref.shape[2]
    cut, half = out_refs[0].shape
    for i in range(half // CHUNK):
        place = pl.ds(pl.multiple_of(which_ref[0] * half + i * CHUNK, CHUNK), CHUNK)
        total = dot(m_ref[...], a_ref[:, :, place].reshape(-1, CHUNK))
        for part in range(2):
            total += dot(g_ref[:, part * width : (part + 1) * width], w_ref[part, place, :], NT)
        for j, ref in enumerate(out_refs):
            ref[:, i * CHUNK : (i + 1) * CHUNK] = total[j * cut : (j + 1) * cut].astype(LOW)


def feature_grad(grad, middle, weights, down_maps, which):
    rows, wide = grad.shape
    half = weights.shape[1] // 2
    return pl.pallas_call(
        feature_kernel,
        out_shape=[jax.ShapeDtypeStruct((rows // 4, half), LOW)] * 4,
        in_specs=[SCALAR] + [VECTOR] * 4,
        out_specs=[VECTOR] * 4,
        compiler_params=ROOM,
        cost_estimate=cost(2 * rows * half * wide, 2 * half * (wide + rows)),
        name="feature_grad",
    )(which, grad, middle, weights, down_maps)


def down_kernel(back_ref, mine_ref, facing_ref, *refs):
    *row_refs, out_ref = refs
    rows = jnp.concatenate([ref[...] for ref in row_refs])
    ranks = mine_ref.shape[1]
    both = jnp.concatenate([mine_ref[...], facing_ref[...]], 1)
    parts = dot(dot(back_ref[...], both).astype(LOW), rows, TN)
    out_ref[...] = parts[:ranks] + parts[ranks:]


def down_grad(back, mine, facing, blocks):
    ranks, half = mine.shape[1], blocks[0].shape[1]
    return pl.pallas_call(
        down_kernel,
        out_shape=jax.ShapeDtypeStruct((ranks, half), F32),
        in_specs=[VECTOR] * (3 + len(blocks)),
        out_specs=VECTOR,
        compiler_params=ROOM,
        cost_estimate=cost(5e7, 2 * 200 * half),
        name="down_grad",
    )(back, mine, facing, *blocks)


def row_tokens(x_hi, z, core, x_lo):
    def base_rows(chain, x_high):
        rows = []
        for k in (*SHIFTS, 0):
            token = ((x_high * NZ + (z - k) % NZ) * 2 + chain) * 2
            for batch in range(3):
                rows += [batch * 64 + token, batch * 64 + token + 1]
        return jnp.stack(rows)

    own_half, other_half = [], []
    for chain in (core, 1 - core):
        own_half += [base_rows(chain, x_hi)]
        near = jnp.where(chain == 0, x_hi, 1 - x_hi)
        other_half += [base_rows(chain, near), base_rows(chain, 1 - near)]
    for chain in (core, 1 - core):
        own_half += [base_rows(chain, 1 - x_hi)]
    return jnp.concatenate(own_half), jnp.concatenate(other_half)


def per_device(
    queries,
    context_gradient,
    vision_feature_states,
    key_value_weight,
    adapter_down_maps,
    adapter_up_maps,
    norm_gain_pair,
    image_tile_count,
    text_start_position,
):
    weights, down_maps, gains = key_value_weight[0], adapter_down_maps[0], norm_gain_pair[0]
    section, side = lax.axis_index("section"), lax.axis_index("tensor")
    width, half = weights.shape[2], vision_feature_states.shape[2]
    ranks = 2 * down_maps.shape[1]
    here = side.reshape(1).astype(jnp.int32)
    opposite = 1 - here

    own = vision_feature_states.reshape(-1, half)
    base = jnp.concatenate([move(own, ALONG[k]) for k in SHIFTS] + [own])
    first = move(base, NEAR)
    second = move(base, FAR)
    base_there = move(base, SIBLING)
    late_side = after(side, base)
    late_section = after(section, base)
    up_maps = lax.dynamic_slice_in_dim(adapter_up_maps[0], late_side * width, width, 2)
    up_diagonal = jnp.concatenate(
        [jnp.pad(up_maps[0], ((0, 0), (0, width))), jnp.pad(up_maps[1], ((0, 0), (width, 0)))]
    )
    own_token, other_token = row_tokens(
        late_section // 16, (late_section // 2) % NZ, late_section % 2, late_side
    )
    line = jnp.arange(own_token.shape[0])
    maps = [
        (line[:, None] == own_token[None]).astype(LOW),
        (line[:, None] == other_token[None]).astype(LOW),
        (own_token[:, None] == line[None]).astype(LOW),
        (other_token[:, None] == line[None]).astype(LOW),
    ]
    pair = pair_queries(
        after(queries[0], base), context_gradient[0], gains, width // gains.shape[1]
    )
    step_a = project([base, base_there], weights, down_maps, here)
    first = after(first, pair, *step_a, up_diagonal, *maps)
    weights = hold(weights, first)
    third = move(first, FAR)
    first_there = move(first, SIBLING)
    second_there = move(second, SIBLING)
    others = [first, second, first_there, second_there]
    step_b = project(others, weights, down_maps, opposite)
    third = after(third, *step_b)
    third_there = move(third, SIBLING)
    step_c = project([third, third_there], weights, down_maps, here)
    owns = [base, base_there, third, third_there]

    g_own, m_own, g_other, m_other, middle, up_part = attend(
        image_tile_count,
        text_start_position,
        (step_a, step_c, step_b),
        maps,
        up_diagonal,
        gains,
        pair,
    )

    middle_facing = lax.ppermute(middle, "tensor", TENSOR_SWAP)
    base, base_out, third, third_out = feature_grad(g_own, m_own, weights, down_maps, here)

    def add(mine, theirs):
        return mine.astype(F32) + theirs.astype(F32)

    third = add(third, move(third_out, SIBLING)).astype(LOW)
    third_in = move(third, FAR)
    first, second, first_out, second_out = feature_grad(
        after(g_other, third), m_other, weights, down_maps, opposite
    )
    second = add(second, move(second_out, SIBLING)).astype(LOW)
    first = add(first, move(first_out, SIBLING))
    base = add(base, move(base_out, SIBLING))
    down_own = down_grad(maps[2], middle, after(middle_facing, first_out), owns)
    sums = jnp.concatenate([down_own, up_part], 1).astype(LOW)
    cut = ranks // 2
    ways = ((sums[:cut], DP_NEAR, DP_FAR), (sums[cut:], DP_FAR, DP_NEAR))
    early_sums = [lax.ppermute(part, "dp", pairs) for part, pairs, _ in ways]
    second_in = move(second, FAR)
    first = (first + third_in.astype(F32)).astype(LOW)
    first_in = move(first, NEAR)
    halves = [
        add(part, after(arriving, first)).astype(LOW)
        for (part, _, _), arriving in zip(ways, early_sums)
    ]
    late_sums = [lax.ppermute(part, "dp", pairs) for part, (_, _, pairs) in zip(halves, ways)]
    base = base + second_in.astype(F32) + first_in.astype(F32)
    low_base = base.astype(LOW)
    sums = jnp.concatenate(
        [
            add(part, after(arriving, low_base)).astype(LOW)
            for part, arriving in zip(halves, late_sums)
        ]
    )
    low_base = after(low_base, sums)
    facing = lax.ppermute(sums, "tensor", TENSOR_SWAP)
    count = own.shape[0]
    own_grad = base[len(SHIFTS) * count :]
    for i, k in enumerate(SHIFTS):
        own_grad += move(low_base[i * count : (i + 1) * count], ALONG[NZ - k]).astype(F32)

    down_total, up_total = finish(here, sums, facing, half)
    return (
        own_grad.reshape(vision_feature_states.shape),
        down_total.reshape(1, 2, ranks // 2, 2 * half),
        up_total.reshape(1, 2, ranks // 2, 2 * width),
    )


def solution(mesh):
    in_specs = (
        P("section", "dp", None, "tensor"),
        P("section", "dp", None, "tensor"),
        P("dp", "section", "tensor"),
        P("section", None, None, "tensor"),
        P("section", None, None, None),
        P("section", None, None, None),
        P("section", None, None),
        P("dp"),
        P("dp"),
    )
    out_specs = (
        P("dp", "section", "tensor"),
        P("section", None, None, None),
        P("section", None, None, None),
    )
    return jax.shard_map(
        per_device, mesh=mesh, in_specs=in_specs, out_specs=out_specs, check_vma=False
    )
```

```python
import jax
import jax.numpy as jnp
import numpy as np
from jax import lax
from jax.experimental import pallas as pl
from jax.experimental.pallas import tpu as pltpu
from jax.sharding import PartitionSpec as P

TILES = 4
ADAPTER_SCALE = 2.0
EPS = 1e-05
PLANE = ("section", "tensor")
NZ = 8


def plane_pairs(route):
    def index(x, z, core):
        return (((x // 2) * NZ + z) * 2 + core) * 2 + x % 2

    return [
        (index(x, z, core), index(*route(x, z, core)))
        for x in range(4)
        for z in range(NZ)
        for core in range(2)
    ]


SIBLING = plane_pairs(lambda x, z, core: (x, z, 1 - core))
SHIFTS = (4, 3, 5, 2, 6, 1, 7)
ALONG = {
    k: plane_pairs(lambda x, z, core, k=k: (x, (z + k) % NZ, core)) for k in SHIFTS
}
NEAR = plane_pairs(lambda x, z, core: (x ^ 1 if core == 0 else 3 - x, z, core))
FAR = plane_pairs(lambda x, z, core: (3 - x if core == 0 else x ^ 1, z, core))
TENSOR_SWAP = [(0, 1), (1, 0)]
DP_NEAR = [(i, i ^ 1) for i in range(4)]
DP_FAR = [(i, 3 - i) for i in range(4)]


def move(block, pairs):
    return lax.ppermute(block, PLANE, pairs)


def after(value, *others):
    return lax.optimization_barrier((value, *others))[0]


NT = (((1,), (1,)), ((), ()))
TN = (((0,), (0,)), ((), ()))
F32, LOW = jnp.float32, jnp.bfloat16
ROOM = pltpu.CompilerParams(vmem_limit_bytes=20 * 1024 * 1024)
SCALAR = pl.BlockSpec(memory_space=pltpu.SMEM)
VECTOR = pl.BlockSpec(memory_space=pltpu.VMEM)
CHUNK = 1024


def dot(first, second, dims=(((1,), (0,)), ((), ()))):
    return lax.dot_general(first, second, dims, preferred_element_type=F32)


def cost(flops, moved):
    return pl.CostEstimate(flops=int(flops), bytes_accessed=int(moved), transcendentals=0)


def pair_kernel(gain_ref, query_ref, context_ref, pair_ref):
    gain = gain_ref[0:1, :].astype(F32)
    head = gain.shape[1]
    text = query_ref.shape[1]
    kv_heads = pair_ref.shape[0]
    group = query_ref.shape[2] // (head * kv_heads)
    for kv in range(kv_heads):
        for member in range(group):
            columns = slice((kv * group + member) * head, (kv * group + member + 1) * head)
            rows = slice(member * text, (member + 1) * text)
            query = query_ref[0, :, columns].astype(F32)
            scale = lax.rsqrt(jnp.mean(query * query, axis=-1, keepdims=True) + EPS)
            pair_ref[kv, rows, 0:head] = (query * scale * gain).astype(LOW)
            pair_ref[kv, rows, head : 2 * head] = context_ref[0, :, columns]


def pair_queries(queries, context, gains, kv_heads):
    batches, text, wide = queries.shape
    head = gains.shape[1]
    rows = wide // (kv_heads * head) * text
    block = pl.BlockSpec((1, text, wide), lambda b: (b, 0, 0))
    return pl.pallas_call(
        pair_kernel,
        out_shape=jax.ShapeDtypeStruct((batches * kv_heads, rows, 2 * head), LOW),
        grid=(batches,),
        in_specs=[pl.BlockSpec(gains.shape, lambda b: (0, 0)), block, block],
        out_specs=pl.BlockSpec((kv_heads, rows, 2 * head), lambda b: (b, 0, 0)),
        compiler_params=ROOM,
        cost_estimate=cost(2e8, 4 * queries.size * 2),
        name="pair_queries",
    )(gains, queries, context)


def hold_kernel(ready_ref, from_ref, to_ref, semaphore):
    copy = pltpu.make_async_copy(from_ref, to_ref, semaphore)
    copy.start()
    copy.wait()


def hold(array, ready):
    return pl.pallas_call(
        hold_kernel,
        out_shape=pltpu.VMEM(array.shape, array.dtype),
        in_specs=[pl.BlockSpec(memory_space=pl.ANY), pl.BlockSpec(memory_space=pltpu.HBM)],
        scratch_shapes=[pltpu.SemaphoreType.DMA],
        out_specs=VECTOR,
        compiler_params=ROOM,
        cost_estimate=cost(0, 2 * array.size),
        name="hold",
    )(ready, array)


def finish_kernel(side_ref, mine_ref, facing_ref, down_ref, up_ref):
    half, width = down_ref.shape[1] // 2, up_ref.shape[1] // 2
    for ref, place in ((mine_ref, side_ref[0]), (facing_ref, 1 - side_ref[0])):
        columns = pl.ds(pl.multiple_of(place * half, half), half)
        down_ref[:, columns] = ref[:, :half].astype(F32)
        columns = pl.ds(pl.multiple_of(place * width, width), width)
        up_ref[:, columns] = ref[:, half:].astype(F32)


def finish(side, mine, facing, half):
    ranks, wide = mine.shape
    return pl.pallas_call(
        finish_kernel,
        out_shape=[
            jax.ShapeDtypeStruct((ranks, 2 * half), F32),
            jax.ShapeDtypeStruct((ranks, 2 * (wide - half)), F32),
        ],
        in_specs=[SCALAR, VECTOR, VECTOR],
        out_specs=[VECTOR] * 2,
        compiler_params=ROOM,
        cost_estimate=cost(0, 8 * mine.size),
        name="finish",
    )(side, mine, facing)


def project_kernel(which_ref, *refs):
    *row_refs, w_ref, a_ref, y_ref, r_ref = refs
    half = row_refs[0].shape[1]
    totals = [None, None, None]
    for i in range(half // CHUNK):
        rows = jnp.concatenate([ref[:, i * CHUNK : (i + 1) * CHUNK] for ref in row_refs])
        place = pl.ds(pl.multiple_of(which_ref[0] * half + i * CHUNK, CHUNK), CHUNK)
        maps = a_ref[:, :, place].reshape(-1, CHUNK)
        terms = [dot(rows, w_ref[part, place, :]) for part in range(2)] + [dot(rows, maps, NT)]
        totals = [new if old is None else old + new for old, new in zip(totals, terms)]
    y_ref[0] = totals[0]
    y_ref[1] = totals[1]
    r_ref[...] = totals[2]


def project(blocks, weights, down_maps, which):
    count, half = len(blocks) * blocks[0].shape[0], blocks[0].shape[1]
    width, ranks = weights.shape[2], 2 * down_maps.shape[1]
    return pl.pallas_call(
        project_kernel,
        out_shape=[
            jax.ShapeDtypeStruct((2, count, width), F32),
            jax.ShapeDtypeStruct((count, ranks), F32),
        ],
        in_specs=[SCALAR] + [VECTOR] * (len(blocks) + 2),
        out_specs=[VECTOR] * 2,
        compiler_params=ROOM,
        cost_estimate=cost(4 * 192 * half * width, 4 * half * width + 2 * count * half),
        name="project",
    )(which, *blocks, weights, down_maps)


def attention_kernel(
    count_ref, start_ref, y0, y1, y2, r0, r1, r2, own_map, other_map, own_back, other_back,
    up_diagonal, gains_ref, pair_ref, g_own, m_own, g_other, m_other, middle_ref, up_ref, grad_ref,
):
    width = y0.shape[2]
    head = gains_ref.shape[1]
    kv_heads = width // head
    batches = pair_ref.shape[0] // kv_heads
    tokens = own_map.shape[0] // batches
    ranks = r0.shape[1]
    text = 128
    scale = head ** (-0.5)

    def ordered(own, other):
        total = None
        for mapping, values in ((own_map, own), (other_map, other)):
            high = values.astype(LOW)
            rest = values - high.astype(F32)
            middle = rest.astype(LOW)
            lowest = (rest - middle.astype(F32)).astype(LOW)
            for term in (lowest, middle, high):
                moved = dot(mapping[...], term)
                total = moved if total is None else total + moved
        return total

    reduced = ordered(jnp.concatenate([r0[...], r1[...]]), r2[...]).astype(LOW)
    adapted = ADAPTER_SCALE * dot(reduced, up_diagonal[...])
    raw = [
        ordered(jnp.concatenate([y0[part], y1[part]]), y2[part])
        + adapted[:, part * width : (part + 1) * width]
        for part in range(2)
    ]
    gain = gains_ref[1:2, :].astype(F32)
    lane = lax.broadcasted_iota(jnp.int32, (1, pair_ref.shape[1]), 1) % text
    token = lax.broadcasted_iota(jnp.int32, (tokens, 1), 0)
    for kv in range(kv_heads):
        columns = slice(kv * head, (kv + 1) * head)
        key_raw = raw[0][:, columns]
        key_scale = lax.rsqrt(jnp.mean(key_raw * key_raw, axis=-1, keepdims=True) + EPS)
        unit = key_raw * key_scale
        keys = (unit * gain).astype(LOW)
        values = raw[1][:, columns].astype(LOW)
        for batch in range(batches):
            rows = slice(batch * tokens, (batch + 1) * tokens)
            none = jnp.zeros((tokens, head), LOW)
            both = jnp.concatenate(
                [
                    jnp.concatenate([keys[rows], none], 1),
                    jnp.concatenate([none, values[rows]], 1),
                ]
            )
            pair = pair_ref[batch * kv_heads + kv]
            scores = dot(both, pair, NT)
            allowed = token < count_ref[batch] * (tokens // TILES)
            live = (lane >= start_ref[batch]).astype(F32)
            weighted = jnp.where(allowed, jnp.exp(scores[:tokens] * scale), 0.0)
            attention = weighted * (live / jnp.sum(weighted, axis=0, keepdims=True))
            probs = scores[tokens:]
            mean = jnp.sum(attention * probs, axis=0, keepdims=True)
            grads = attention * (probs - mean) * scale
            out = dot(jnp.concatenate([grads.astype(LOW), attention.astype(LOW)]), pair)
            gained = out[:tokens, :head] * gain
            inner = jnp.mean(gained * unit[rows], axis=-1, keepdims=True)
            grad_ref[rows, columns] = (key_scale[rows] * (gained - unit[rows] * inner)).astype(LOW)
            grad_ref[rows, width + kv * head : width + (kv + 1) * head] = out[
                tokens:, head:
            ].astype(LOW)
    grad = grad_ref[...]
    middle = dot(grad, up_diagonal[...], NT).astype(LOW)
    middle_ref[...] = (ADAPTER_SCALE * middle.astype(F32)).astype(LOW)
    up = ADAPTER_SCALE * dot(reduced, grad, TN)
    for part in range(2):
        half = slice(part * ranks // 2, (part + 1) * ranks // 2)
        up_ref[half, :] = up[half, part * width : (part + 1) * width]
    for back, g_ref, m_ref in ((own_back, g_own, m_own), (other_back, g_other, m_other)):
        g_ref[...] = dot(back[...], grad).astype(LOW)
        m_ref[...] = (ADAPTER_SCALE * dot(back[...], middle)).astype(LOW)


def attend(counts, starts, projected, maps, up_diagonal, gains, pair):
    (y0, r0), (y1, r1), (y2, r2) = projected
    rows, ranks, width = y2.shape[1], r0.shape[1], y0.shape[2]
    scalar = pl.BlockSpec(memory_space=pltpu.SMEM)
    vector = pl.BlockSpec(memory_space=pltpu.VMEM)
    return pl.pallas_call(
        attention_kernel,
        out_shape=[
            jax.ShapeDtypeStruct((rows, 2 * width), LOW),
            jax.ShapeDtypeStruct((rows, ranks), LOW),
            jax.ShapeDtypeStruct((rows, 2 * width), LOW),
            jax.ShapeDtypeStruct((rows, ranks), LOW),
            jax.ShapeDtypeStruct((rows, ranks), LOW),
            jax.ShapeDtypeStruct((ranks, width), F32),
        ],
        in_specs=[scalar, scalar] + [vector] * 13,
        out_specs=[vector] * 6,
        scratch_shapes=[pltpu.VMEM((rows, 2 * width), LOW)],
        compiler_params=ROOM,
        cost_estimate=cost(1e9, 2 * pair.size),
        name="attend",
    )(counts, starts, y0, y1, y2, r0, r1, r2, *maps, up_diagonal, gains, pair)


def feature_kernel(which_ref, g_ref, m_ref, w_ref, a_ref, *out_refs):
    width = w_ref.shape[2]
    cut, half = out_refs[0].shape
    for i in range(half // CHUNK):
        place = pl.ds(pl.multiple_of(which_ref[0] * half + i * CHUNK, CHUNK), CHUNK)
        total = dot(m_ref[...], a_ref[:, :, place].reshape(-1, CHUNK))
        for part in range(2):
            total += dot(g_ref[:, part * width : (part + 1) * width], w_ref[part, place, :], NT)
        for j, ref in enumerate(out_refs):
            ref[:, i * CHUNK : (i + 1) * CHUNK] = total[j * cut : (j + 1) * cut].astype(LOW)


def feature_grad(grad, middle, weights, down_maps, which):
    rows, wide = grad.shape
    half = weights.shape[1] // 2
    return pl.pallas_call(
        feature_kernel,
        out_shape=[jax.ShapeDtypeStruct((rows // 4, half), LOW)] * 4,
        in_specs=[SCALAR] + [VECTOR] * 4,
        out_specs=[VECTOR] * 4,
        compiler_params=ROOM,
        cost_estimate=cost(2 * rows * half * wide, 2 * half * (wide + rows)),
        name="feature_grad",
    )(which, grad, middle, weights, down_maps)


def down_kernel(back_ref, mine_ref, facing_ref, *refs):
    *row_refs, out_ref = refs
    rows = jnp.concatenate([ref[...] for ref in row_refs])
    ranks = mine_ref.shape[1]
    both = jnp.concatenate([mine_ref[...], facing_ref[...]], 1)
    parts = dot(dot(back_ref[...], both).astype(LOW), rows, TN)
    out_ref[...] = parts[:ranks] + parts[ranks:]


def down_grad(back, mine, facing, blocks):
    ranks, half = mine.shape[1], blocks[0].shape[1]
    return pl.pallas_call(
        down_kernel,
        out_shape=jax.ShapeDtypeStruct((ranks, half), F32),
        in_specs=[VECTOR] * (3 + len(blocks)),
        out_specs=VECTOR,
        compiler_params=ROOM,
        cost_estimate=cost(5e7, 2 * 200 * half),
        name="down_grad",
    )(back, mine, facing, *blocks)


def row_tokens(x_hi, z, core):
    row = np.arange(192)
    shift = np.array((*SHIFTS, 0))[row % 48 // 6]
    place = row % 6 // 2 * 64 + row % 2

    def rows(theirs, flip):
        chain = jnp.where(theirs, 1 - core, core)
        x_high = jnp.where(flip(chain), 1 - x_hi, x_hi)
        return place + ((x_high * NZ + (z - shift + NZ) % NZ) * 2 + chain) * 2

    own = rows(row // 48 % 2 == 1, lambda chain: row // 96 == 1)
    other = rows(row // 96 == 1, lambda chain: (row // 48 % 2) != chain)
    return own, other


def per_device(
    queries,
    context_gradient,
    vision_feature_states,
    key_value_weight,
    adapter_down_maps,
    adapter_up_maps,
    norm_gain_pair,
    image_tile_count,
    text_start_position,
):
    weights, down_maps, gains = key_value_weight[0], adapter_down_maps[0], norm_gain_pair[0]
    section, side = lax.axis_index("section"), lax.axis_index("tensor")
    width, half = weights.shape[2], vision_feature_states.shape[2]
    ranks = 2 * down_maps.shape[1]
    here = side.reshape(1).astype(jnp.int32)
    opposite = 1 - here

    own = vision_feature_states.reshape(-1, half)
    base = jnp.concatenate([move(own, ALONG[k]) for k in SHIFTS] + [own])
    first = move(base, NEAR)
    second = move(base, FAR)
    base_there = move(base, SIBLING)
    late_side = after(side, base)
    late_section = after(section, base)
    up_maps = lax.dynamic_slice_in_dim(adapter_up_maps[0], late_side * width, width, 2)
    up_diagonal = jnp.concatenate(
        [jnp.pad(up_maps[0], ((0, 0), (0, width))), jnp.pad(up_maps[1], ((0, 0), (width, 0)))]
    )
    own_token, other_token = row_tokens(
        late_section // 16, (late_section // 2) % NZ, late_section % 2
    )
    line = jnp.arange(own_token.shape[0])
    maps = [
        (line[:, None] == own_token[None]).astype(LOW),
        (line[:, None] == other_token[None]).astype(LOW),
        (own_token[:, None] == line[None]).astype(LOW),
        (other_token[:, None] == line[None]).astype(LOW),
    ]
    pair = pair_queries(
        after(queries[0], base), context_gradient[0], gains, width // gains.shape[1]
    )
    step_a = project([base, base_there], weights, down_maps, here)
    first = after(first, pair, *step_a, up_diagonal, *maps)
    weights = hold(weights, first)
    third = move(first, FAR)
    first_there = move(first, SIBLING)
    second_there = move(second, SIBLING)
    others = [first, second, first_there, second_there]
    step_b = project(others, weights, down_maps, opposite)
    third = after(third, *step_b)
    third_there = move(third, SIBLING)
    step_c = project([third, third_there], weights, down_maps, here)
    owns = [base, base_there, third, third_there]

    g_own, m_own, g_other, m_other, middle, up_part = attend(
        image_tile_count,
        text_start_position,
        (step_a, step_c, step_b),
        maps,
        up_diagonal,
        gains,
        pair,
    )

    middle_facing = lax.ppermute(middle, "tensor", TENSOR_SWAP)
    base, base_out, third, third_out = feature_grad(g_own, m_own, weights, down_maps, here)

    def add(mine, theirs):
        return mine.astype(F32) + theirs.astype(F32)

    third = add(third, move(third_out, SIBLING)).astype(LOW)
    third_in = move(third, FAR)
    first, second, first_out, second_out = feature_grad(
        after(g_other, third), m_other, weights, down_maps, opposite
    )
    second = add(second, move(second_out, SIBLING)).astype(LOW)
    first = add(first, move(first_out, SIBLING))
    base = add(base, move(base_out, SIBLING))
    down_own = down_grad(maps[2], middle, after(middle_facing, first_out), owns)
    sums = jnp.concatenate([down_own, up_part], 1).astype(LOW)
    cut = ranks // 2
    ways = ((sums[:cut], DP_NEAR, DP_FAR), (sums[cut:], DP_FAR, DP_NEAR))
    early_sums = [lax.ppermute(part, "dp", pairs) for part, pairs, _ in ways]
    second_in = move(second, FAR)
    first = (first + third_in.astype(F32)).astype(LOW)
    first_in = move(first, NEAR)
    halves = [
        add(part, after(arriving, first)).astype(LOW)
        for (part, _, _), arriving in zip(ways, early_sums)
    ]
    late_sums = [lax.ppermute(part, "dp", pairs) for part, (_, _, pairs) in zip(halves, ways)]
    base = base + second_in.astype(F32) + first_in.astype(F32)
    low_base = base.astype(LOW)
    sums = jnp.concatenate(
        [
            add(part, after(arriving, low_base)).astype(LOW)
            for part, arriving in zip(halves, late_sums)
        ]
    )
    low_base = after(low_base, sums)
    facing = lax.ppermute(sums, "tensor", TENSOR_SWAP)
    count = own.shape[0]
    own_grad = base[len(SHIFTS) * count :]
    for i, k in enumerate(SHIFTS):
        own_grad += move(low_base[i * count : (i + 1) * count], ALONG[NZ - k]).astype(F32)

    down_total, up_total = finish(here, sums, facing, half)
    return (
        own_grad.reshape(vision_feature_states.shape),
        down_total.reshape(1, 2, ranks // 2, 2 * half),
        up_total.reshape(1, 2, ranks // 2, 2 * width),
    )


def solution(mesh):
    in_specs = (
        P("section", "dp", None, "tensor"),
        P("section", "dp", None, "tensor"),
        P("dp", "section", "tensor"),
        P("section", None, None, "tensor"),
        P("section", None, None, None),
        P("section", None, None, None),
        P("section", None, None),
        P("dp"),
        P("dp"),
    )
    out_specs = (
        P("dp", "section", "tensor"),
        P("section", None, None, None),
        P("section", None, None, None),
    )
    return jax.shard_map(
        per_device, mesh=mesh, in_specs=in_specs, out_specs=out_specs, check_vma=False
    )
```
